32 devices in a mesh: dp: 16 (over z, x, core), mp: 2 (over y).
Axes of the slice: x: 2, y: 2, z: 4, core: 2. Of those that a mesh axis runs over, the one named last changes fastest.
Arguments:
- text_in: bfloat16 [24576, 768], P('dp'), may hold values from -6 to 6
- layout_in: bfloat16 [24576, 192], P('dp'), may hold values from -6 to 6
- token_mask: int32 [24576], P('dp'), may hold values 0 or 1
- box_mask: int32 [24576], P('dp'), may hold values from 0 to 1, as said below
- lengths: int32 [48], P('dp'), may hold values from 256 to 512, as said below
- text_mask_vec: bfloat16 [768], replicated, may hold values from -4 to 4
- layout_mask_vec: bfloat16 [192], replicated, may hold values from -4 to 4
- text_qkv: bfloat16 [3, 768, 768], P(None, None, 'mp'), may hold values from -0.21875 to 0.21875
- text_qv_bias: bfloat16 [2, 768], P(None, 'mp'), may hold values from -3 to 3
- text_out_w: bfloat16 [768, 768], P('mp'), may hold values from -0.625 to 0.625
- text_shifts: bfloat16 [4, 768], replicated, may hold values from -3 to 3
- text_gains: bfloat16 [2, 768], replicated, may hold values from 0.099609375 to 1.8984375
- text_up: bfloat16 [768, 3072], P(None, 'mp'), may hold values from -0.21875 to 0.21875
- text_up_bias: bfloat16 [3072], P('mp'), may hold values from -3 to 3
- text_down: bfloat16 [3072, 768], P('mp'), may hold values from -0.109375 to 0.109375
- layout_qkv: bfloat16 [3, 192, 192], P(None, None, 'mp'), may hold values from -0.4375 to 0.4375
- layout_qv_bias: bfloat16 [2, 192], P(None, 'mp'), may hold values from -3 to 3
- layout_out_w: bfloat16 [192, 192], P('mp'), may hold values from -1.25 to 1.25
- layout_shifts: bfloat16 [4, 192], replicated, may hold values from -3 to 3
- layout_gains: bfloat16 [2, 192], replicated, may hold values from 0.099609375 to 1.8984375
- layout_up: bfloat16 [192, 768], P(None, 'mp'), may hold values from -0.4375 to 0.4375
- layout_up_bias: bfloat16 [768], P('mp'), may hold values from -3 to 3
- layout_down: bfloat16 [768, 192], P('mp'), may hold values from -0.21875 to 0.21875
- text_cot: bfloat16 [24576, 768], P('dp'), may hold values from -6 to 6
- layout_cot: bfloat16 [24576, 192], P('dp'), may hold values from -6 to 6
Outputs:
- text_out: float32 [24576, 768], P('dp')
- layout_out: float32 [24576, 192], P('dp')
- text_in_grad: float32 [24576, 768], P('dp')
- layout_in_grad: float32 [24576, 192], P('dp')
- text_mask_vec_grad: float32 [768], replicated
- layout_mask_vec_grad: float32 [192], replicated
- text_qkv_grad: float32 [3, 768, 768], P(None, 'dp', 'mp')
- text_qv_bias_grad: float32 [2, 768], P(None, 'mp')
- text_out_w_grad: float32 [768, 768], P('mp', 'dp')
- text_shifts_grad: float32 [4, 768], replicated
- text_gains_grad: float32 [2, 768], replicated
- text_up_grad: float32 [768, 3072], P('dp', 'mp')
- text_up_bias_grad: float32 [3072], P('mp')
- text_down_grad: float32 [3072, 768], P('mp', 'dp')
- layout_qkv_grad: float32 [3, 192, 192], P(None, None, 'mp')
- layout_qv_bias_grad: float32 [2, 192], P(None, 'mp')
- layout_out_w_grad: float32 [192, 192], P('mp')
- layout_shifts_grad: float32 [4, 192], replicated
- layout_gains_grad: float32 [2, 192], replicated
- layout_up_grad: float32 [192, 768], P(None, 'mp')
- layout_up_bias_grad: float32 [768], P('mp')
- layout_down_grad: float32 [768, 192], P('mp')
The draws below stay inside these ranges and needn't reach their ends.
Inputs may be any that keep to these rules, and one draw needn't show every extreme that they name: `box_mask`: boxes are masked in aligned runs of 8 tokens (whole regions). `lengths`: each page's unpadded tokens stand at its start; in every draw some page is full.
All inputs are finite; a program needn't handle non-finite values. No bound on the sum of `token_mask` on one device may be relied on, other than what follows from the above.
Results may differ from the reference program's by a relative error of at most 0.012.
The reference program's roundings to bfloat16 on the way count: a program that leaves them out, or rounds other values in their place, can miss the bound.
Values sent between devices are 32-bit elements; how exact they have to be, the bound alone decides.
No kernel may reach another device: no remote copies, remote signals or barrier semaphores. Data moves between devices by JAX's collectives and lax.ppermute only.
A program may use at most 256 MiB of HBM per device.

```python
import math
import jax
import jax.numpy as jnp
from jax import lax

D = 768
HD = 64
FF = 3072
L = 192
LHD = 16
FL = 768
SEQ = 512
PAGES = 48
TOKENS = 24576


def draw_box_mask(key, part):
    key = jax.random.fold_in(key, 11)
    regions = jax.random.randint(key, (TOKENS // 8,), 0, 4)
    return jnp.repeat((regions == 0).astype(jnp.int32), 8)


def draw_lengths(key, part):
    key = jax.random.fold_in(key, 23)
    first_key, second_key = jax.random.split(key)
    drawn = jax.random.randint(first_key, (PAGES,), SEQ // 2, SEQ + 1)
    longest = jax.random.randint(second_key, (), 0, PAGES)
    return jnp.where(jnp.arange(PAGES) == longest, SEQ, drawn).astype(jnp.int32)


def with_ends(entries, stream_key, smallest, high):
    extent = entries.shape
    place = [jax.random.randint(jax.random.fold_in(stream_key, axis), (), 0, extent[axis]) for axis in range(len(extent))]
    entries = entries.at[tuple(place)].set(smallest)
    longest = extent.index(max(extent))
    place[longest] = (place[longest] + 1) % extent[longest]
    return entries.at[tuple(place)].set(high)


def level_of(key, dims, pieces, smallest, high):
    level = 1.0
    for position, shards_of in pieces:
        steps = jax.random.uniform(jax.random.fold_in(jax.random.fold_in(key, 6), position), (shards_of,), jnp.float32, smallest / len(pieces), high / len(pieces))
        level = level * jnp.repeat(jnp.exp(steps), dims[position] // shards_of).reshape((-1,) + (1,) * (len(dims) - 1 - position))
    return level


def normal_values(key, extent, deviation, reach, pieces=(), kind=jnp.bfloat16):
    values = jax.random.normal(key, extent, jnp.float32) * deviation
    if len(pieces) > 0:
        values = level_of(key, extent, pieces, -0.22, 0.18) * values
    return jnp.clip(values, min=-reach, max=reach).astype(kind)


def setup_inputs(seed: int = 0) -> dict:
    key_of = jax.random.split(jax.random.key(seed), 26)
    return {
        "text_in": normal_values(key_of[0], (TOKENS, D), 1.0, 6.0, ((0, 16),)),
        "layout_in": normal_values(key_of[1], (TOKENS, L), 1.0, 6.0, ((0, 16),)),
        "token_mask": with_ends((jax.random.randint(key_of[2], (TOKENS,), 0, 20) < 3).astype(jnp.int32), jax.random.fold_in(key_of[2], 1), 0, 1),
        "box_mask": draw_box_mask(jax.random.fold_in(key_of[25], 71), 0),
        "lengths": draw_lengths(jax.random.fold_in(key_of[25], 71), 0),
        "text_mask_vec": normal_values(key_of[5], (D,), 1.0, 4.0),
        "layout_mask_vec": normal_values(key_of[6], (L,), 1.0, 4.0),
        "text_qkv": normal_values(key_of[7], (3, D, D), D ** -0.5, 0.21875, ((2, 2),)),
        "text_qv_bias": normal_values(key_of[8], (2, D), 0.5, 3.0, ((1, 2),)),
        "text_out_w": normal_values(key_of[9], (D, D), (D // 8) ** -0.5, 0.625, ((0, 2),)),
        "text_shifts": normal_values(key_of[10], (4, D), 0.5, 3.0),
        "text_gains": jnp.clip(1.0 + 0.18 * jax.random.normal(key_of[11], (2, D), jnp.float32), 0.099609375, 1.8984375).astype(jnp.bfloat16),
        "text_up": normal_values(key_of[12], (D, FF), D ** -0.5, 0.21875, ((1, 2),)),
        "text_up_bias": normal_values(key_of[13], (FF,), 0.5, 3.0, ((0, 2),)),
        "text_down": normal_values(key_of[14], (FF, D), FF ** -0.5, 0.109375, ((0, 2),)),
        "layout_qkv": normal_values(key_of[15], (3, L, L), L ** -0.5, 0.4375, ((2, 2),)),
        "layout_qv_bias": normal_values(key_of[16], (2, L), 0.5, 3.0, ((1, 2),)),
        "layout_out_w": normal_values(key_of[17], (L, L), (L // 8) ** -0.5, 1.25, ((0, 2),)),
        "layout_shifts": normal_values(key_of[18], (4, L), 0.5, 3.0),
        "layout_gains": jnp.clip(1.0 + 0.18 * jax.random.normal(key_of[19], (2, L), jnp.float32), 0.099609375, 1.8984375).astype(jnp.bfloat16),
        "layout_up": normal_values(key_of[20], (L, FL), L ** -0.5, 0.4375, ((1, 2),)),
        "layout_up_bias": normal_values(key_of[21], (FL,), 0.5, 3.0, ((0, 2),)),
        "layout_down": normal_values(key_of[22], (FL, L), FL ** -0.5, 0.21875, ((0, 2),)),
        "text_cot": normal_values(key_of[23], (TOKENS, D), 1.0, 6.0, ((0, 16),)),
        "layout_cot": normal_values(key_of[24], (TOKENS, L), 1.0, 6.0, ((0, 16),)),
    }


@jax.custom_vjp
def low(v):
    return lax.optimization_barrier(v.astype(jnp.bfloat16)).astype(jnp.float32)

@jax.custom_vjp
def low_back(v):
    return v

def low_keep(v):
    return (low(v), None)

def low_pass(kept, grad):
    return (grad,)

def back_keep(v):
    return (v, None)

def back_low(kept, grad):
    return (low(grad),)
low.defvjp(low_keep, low_pass)
low_back.defvjp(back_keep, back_low)
EPSILON = 1e-05
NEGATIVE = -1000000000.0
HIGHEST = lax.Precision.HIGHEST

def normalize(values, gain_row, offset):
    row_mean = lax.optimization_barrier(jnp.mean(values, -1, keepdims=True))
    centered = values - row_mean
    variance = lax.optimization_barrier(jnp.mean(centered * centered, -1, keepdims=True))
    return centered * lax.rsqrt(variance + EPSILON) * gain_row + offset

def masked(inputs, mask_flags, vector):
    return jnp.where(mask_flags[:, None] == 1, vector[None, :], inputs)

def project(inputs, weight, bias_pair):
    stacked = jnp.stack([bias_pair[0], jnp.zeros_like(bias_pair[0]), bias_pair[1]])
    product = jnp.einsum('nd,cde->cne', inputs, weight, precision=HIGHEST)
    return low(low_back(product + stacked[:, None, :]))

def layout_inputs(weight, bias_pair, vector, inputs, mask_flags):
    return project(masked(inputs, mask_flags, vector), weight, bias_pair)

def split_heads(values, head_width):
    return values.reshape(values.shape[0], values.shape[1] // head_width, head_width)

def scores(queries, keys_in, head_width):
    product = jnp.einsum('qhd,khd->hqk', split_heads(queries, head_width), split_heads(keys_in, head_width), precision=HIGHEST)
    return low_back(product) / math.sqrt(head_width)

def attend(page_items):
    text_q, text_k, text_v, layout_q, layout_k, layout_v, frozen_q, frozen_k, valid_keys = page_items
    text_scores = scores(text_q, text_k, HD)
    layout_scores = scores(layout_q, layout_k, LHD)
    frozen_scores = scores(frozen_q, frozen_k, LHD)
    key_bias = jnp.where(valid_keys, 0.0, NEGATIVE)[None, None, :]
    text_weights = low(jax.nn.softmax(text_scores + frozen_scores + key_bias, axis=-1))
    layout_weights = low(jax.nn.softmax(layout_scores + text_scores + key_bias, axis=-1))
    text_heads = jnp.einsum('hqk,khd->qhd', text_weights, split_heads(text_v, HD), precision=HIGHEST)
    layout_heads = jnp.einsum('hqk,khd->qhd', layout_weights, split_heads(layout_v, LHD), precision=HIGHEST)
    return (text_heads.reshape(text_q.shape[0], -1), layout_heads.reshape(layout_q.shape[0], -1))

def block_rest(inputs, attended, out_weight, offsets, gains, up_weight, up_bias, down_weight):
    merged = low(low_back(attended))
    first_sum = inputs + low_back(jnp.dot(merged, out_weight, precision=HIGHEST)) + offsets[2]
    hidden = normalize(first_sum, gains[0], offsets[0])
    pre_gelu = low_back(jnp.dot(low(hidden), up_weight, precision=HIGHEST) + up_bias)
    activated = low(jax.nn.gelu(pre_gelu, approximate=False))
    second_sum = hidden + low_back(jnp.dot(activated, down_weight, precision=HIGHEST)) + offsets[3]
    return normalize(second_sum, gains[1], offsets[1])

def forward(params, activations, token_flags, box_flags, valid_keys, frozen):
    text_vector, layout_vector, text_weight, text_bias, text_outw, text_offsets, text_gains, text_upw, text_upb, text_downw, layout_weight, layout_bias, layout_outw, layout_offsets, layout_gains, layout_upw, layout_upb, layout_downw = params
    text_input, layout_input = activations
    text_x = masked(text_input, token_flags, text_vector)
    layout_x = masked(layout_input, box_flags, layout_vector)
    text_proj = project(text_x, text_weight, text_bias)
    layout_proj = layout_inputs(layout_weight, layout_bias, layout_vector, layout_input, box_flags)
    page_count = valid_keys.shape[0]

    def paged(values):
        return values.reshape(page_count, -1, values.shape[-1])
    page_items = (paged(text_proj[0]), paged(text_proj[1]), paged(text_proj[2]), paged(layout_proj[0]), paged(layout_proj[1]), paged(layout_proj[2]), paged(frozen[0]), paged(frozen[1]), valid_keys)
    text_heads, layout_heads = lax.map(jax.checkpoint(attend), page_items)
    text_rows = text_heads.reshape(text_x.shape[0], -1)
    layout_rows = layout_heads.reshape(layout_x.shape[0], -1)
    text_result = block_rest(text_x, text_rows, text_outw, text_offsets, text_gains, text_upw, text_upb, text_downw)
    layout_result = block_rest(layout_x, layout_rows, layout_outw, layout_offsets, layout_gains, layout_upw, layout_upb, layout_downw)
    return (text_result, layout_result)

def reference(text_in, layout_in, token_mask, box_mask, lengths, text_mask_vec, layout_mask_vec, text_qkv, text_qv_bias, text_out_w, text_shifts, text_gains, text_up, text_up_bias, text_down, layout_qkv, layout_qv_bias, layout_out_w, layout_shifts, layout_gains, layout_up, layout_up_bias, layout_down, text_cot, layout_cot):
    params = tuple((entry.astype(jnp.float32) for entry in (text_mask_vec, layout_mask_vec, text_qkv, text_qv_bias, text_out_w, text_shifts, text_gains, text_up, text_up_bias, text_down, layout_qkv, layout_qv_bias, layout_out_w, layout_shifts, layout_gains, layout_up, layout_up_bias, layout_down)))
    token_count = text_in.shape[0]
    page_count = lengths.shape[0]
    seq_len = token_count // page_count
    group_size = math.gcd(page_count, max(1, 4096 // seq_len))
    group_count = page_count // group_size
    valid_all = lax.broadcasted_iota(jnp.int32, (page_count, seq_len), 1) < lengths[:, None]

    def regroup(values):
        return values.reshape((group_count, -1) + values.shape[1:])
    group_inputs = (regroup(text_in.astype(jnp.float32)), regroup(layout_in.astype(jnp.float32)), regroup(token_mask), regroup(box_mask), regroup(valid_all), regroup(text_cot.astype(jnp.float32)), regroup(layout_cot.astype(jnp.float32)))

    def group_step(running, group_item):
        text_input, layout_input, token_flags, box_flags, valid_keys, text_grad, layout_grad = group_item
        frozen = layout_inputs(params[10], params[11], params[1], layout_input, box_flags)

        def closed(weights_in, activations):
            return forward(weights_in, activations, token_flags, box_flags, valid_keys, frozen)
        results, pullback = jax.vjp(closed, params, (text_input, layout_input))
        weight_grads, input_grads = pullback((text_grad, layout_grad))
        running = jax.tree.map(lambda summed, added: summed + added, running, weight_grads)
        return (running, (results[0], results[1], input_grads[0], input_grads[1]))
    zero_grads = tuple((jnp.zeros_like(entry) for entry in params))
    running, stacked = lax.scan(group_step, zero_grads, group_inputs)
    text_out = stacked[0].reshape(token_count, -1)
    layout_out = stacked[1].reshape(token_count, -1)
    text_in_grad = stacked[2].reshape(token_count, -1)
    layout_in_grad = stacked[3].reshape(token_count, -1)
    return (text_out, layout_out, text_in_grad, layout_in_grad, running[0], running[1], running[2], running[3], running[4], running[5], running[6], running[7], running[8], running[9], running[10], running[11], running[12], running[13], running[14], running[15], running[16], running[17])
```

```python
import functools
import jax, jax.numpy as jnp
from jax import lax
from jax.experimental import pallas as pl
from jax.experimental.pallas import tpu as pltpu
F32=jnp.float32; BF=jnp.bfloat16
NT=(((1,),(1,)),((),()))
TN=(((0,),(0,)),((),()))
def dot(a,b): return jnp.dot(a,b,preferred_element_type=F32)
def dotg(a,b,dn): return lax.dot_general(a,b,dn,preferred_element_type=F32)
VLIM=60*1024*1024

def lane_iota(shape): return lax.broadcasted_iota(jnp.int32,shape,len(shape)-1)

def attn_fwd_kernel(len_ref, xt_ref, xl_ref, wt_ref, wl_ref, bt_ref, bl_ref,
                    qt_ref, kt_ref, vt_ref, ql_ref, kl_ref, vl_ref, ot_ref, ol_ref, lse_ref, olT, lseT):
    page=pl.program_id(0)
    seq=xt_ref.shape[0]
    xt=xt_ref[...]; xl=xl_ref[...]
    for c,(t,l) in enumerate(((qt_ref,ql_ref),(kt_ref,kl_ref),(vt_ref,vl_ref))):
        t[...]=(dot(xt,wt_ref[c])+bt_ref[c:c+1,:]).astype(BF)
        l[...]=(dot(xl,wl_ref[c])+bl_ref[c:c+1,:]).astype(BF)
    lane=lane_iota((seq,128))
    row=lax.broadcasted_iota(jnp.int32,(seq,128),0)
    length=len_ref[page]
    bias=jnp.where(row<length,0.0,-1e9).astype(BF)
    one=jnp.ones((seq,128),BF)
    ql=jnp.where(lane==96,one,ql_ref[...]*BF(0.25))
    kl=jnp.where(lane==96,bias,kl_ref[...])
    vlT=vl_ref[...].T
    zero=jnp.zeros((seq,128),BF)
    olT[...]=jnp.zeros_like(olT); lseT[...]=jnp.zeros_like(lseT)
    for j in range(3):
        cols=slice(128*j,128*j+128)
        qbig=jnp.concatenate([qt_ref[:,cols]*BF(0.125),ql],1)
        vT=vt_ref[:,cols].T
        halves=[]
        for s in range(2):
            h=2*j+s
            kbig=jnp.concatenate([jnp.where(lane//64==s,kt_ref[:,cols],zero),
                                  jnp.where((lane//16==h)|(lane==96),kl,zero)],1)
            S=dotg(kbig,qbig,NT)
            m=jnp.max(S,0,keepdims=True)
            e=jnp.exp(S-m)
            ssum=jnp.sum(e,0,keepdims=True)
            v80=jnp.concatenate([vT[64*s:64*s+64],vlT[16*h:16*h+16]],0)
            o=dot(v80,e.astype(BF))*(1.0/ssum)
            halves.append(o[:64])
            olT[16*h:16*h+16,:]=o[64:]
            lseT[h:h+1,:]=m+jnp.log(ssum)
        ot_ref[:,cols]=jnp.concatenate(halves,0).T.astype(BF)
    ol_ref[...]=olT[...].T.astype(BF)
    lse_ref[...]=pltpu.roll(lseT[...].T,97,1)

def attn_fwd(lengths, xt, xl, wt, wl, bt, bl):
    rows=xt.shape[0]; pages=lengths.shape[0]; seq=rows//pages
    rb=lambda n: pl.BlockSpec((seq,n),lambda p,*_:(p,0))
    full=lambda a: pl.BlockSpec(a.shape,lambda p,*_:(0,)*a.ndim)
    o=lambda n,d=BF: jax.ShapeDtypeStruct((rows,n),d)
    return pl.pallas_call(attn_fwd_kernel,
        grid_spec=pltpu.PrefetchScalarGridSpec(num_scalar_prefetch=1,grid=(pages,),
            in_specs=[rb(768),rb(192),full(wt),full(wl),full(bt),full(bl)],
            out_specs=[rb(384)]*3+[rb(128)]*3+[rb(384),rb(128),rb(128)],
            scratch_shapes=[pltpu.VMEM((128,seq),F32),pltpu.VMEM((128,seq),F32)]),
        out_shape=[o(384)]*3+[o(128)]*3+[o(384),o(128),o(128,F32)],
        compiler_params=pltpu.CompilerParams(vmem_limit_bytes=VLIM),name="attn_fwd")(lengths,xt,xl,wt,wl,bt,bl)

def ind_matrix(j):
    r=lax.broadcasted_iota(jnp.int32,(256,128),0)%128
    l=lax.broadcasted_iota(jnp.int32,(256,128),1)
    h=(r//64+2*j) if j is not None else r//16
    return jnp.where((l==97+h)&(h<6),1.0,0.0).astype(BF)

def split2(v):
    hi=v.astype(BF)
    return hi,(v-hi.astype(F32)).astype(BF)

def attn_bwd_kernel(mode, len_ref, qt_ref, kt_ref, vt_ref, ql_ref, kl_ref, vl_ref, ot_ref, ol_ref, lse_ref, dot_ref, dol_ref,
                    dpt_ref, dpl_ref, dqlT):
    page=pl.program_id(0)
    seq=qt_ref.shape[0]
    lane=lane_iota((seq,128))
    row=lax.broadcasted_iota(jnp.int32,(seq,128),0)
    bias=jnp.where(row<len_ref[page],0.0,-1e9).astype(BF)
    zero=jnp.zeros((seq,128),BF); one=jnp.ones((seq,128),BF)
    nl=-lse_ref[...]
    hi=nl.astype(BF); r1=nl-hi.astype(F32); mid=r1.astype(BF); lo=r1-mid.astype(F32)
    ext=hi+pltpu.roll(mid.astype(F32),7,1).astype(BF)+pltpu.roll(lo,14,1).astype(BF)
    qle=jnp.where(lane<96,ql_ref[...]*BF(0.25),jnp.where(lane==96,one,ext))
    kl=kl_ref[...]; vl=vl_ref[...]; ql=ql_ref[...]
    if mode==2:
        klT=kl.T
        dqlT[...]=jnp.zeros_like(dqlT)
    def sums(a,b,m):
        p=a.astype(F32)*b.astype(F32)
        h_,l_=split2(p)
        return dot(jnp.concatenate([h_,l_],1),m)
    dol=dol_ref[...]
    d_l=sums(dol,ol_ref[...],ind_matrix(None))
    d_t=d_l
    for j in range(3):
        cols=slice(128*j,128*j+128)
        d_t=d_t+sums(dot_ref[:,cols],ot_ref[:,cols],ind_matrix(j))
    def ext_delta(d):
        h_=d.astype(BF); l_=d-h_.astype(F32)
        return h_+pltpu.roll(l_,7,1).astype(BF)
    dol1=jnp.where(lane<96,dol*BF(0.125),ext_delta(d_t*-0.125))
    dol2=jnp.where(lane<96,dol*BF(0.25),ext_delta(d_l*-0.25))
    for j in range(3):
        cols=slice(128*j,128*j+128)
        qt=qt_ref[:,cols]; kt=kt_ref[:,cols]; vt=vt_ref[:,cols]; dO=dot_ref[:,cols]
        qbig=jnp.concatenate([qt*BF(0.125),qle],1)
        dbig=jnp.concatenate([dO*BF(0.125),dol1],1)
        dObig=jnp.concatenate([dO,dol],1)
        prev=None
        if mode==2: ktT=kt.T
        for s in range(2):
            h=2*j+s
            tm=lane//64==s; lm=lane//16==h
            kbig=jnp.concatenate([jnp.where(tm,kt,zero),jnp.where(lm,kl,jnp.where(lane==96,bias,
                 jnp.where((lane==97+h)|(lane==104+h)|(lane==111+h),one,zero)))],1)
            vle=jnp.where(lm,vl,jnp.where((lane==97+h)|(lane==104+h),one,zero))
            vbig=jnp.concatenate([jnp.where(tm,vt,zero),vle],1)
            S=dotg(kbig,qbig,NT)
            M1=dotg(vbig,dbig,NT)
            M2=dotg(vle,dol2,NT)
            Pm=jnp.exp(S)
            Pb=Pm.astype(BF)
            R1=(Pm*M1).astype(BF)
            R2=(Pm*M2).astype(BF)
            dk_t=dot(R1,qt); dk_l=dot(R2,ql); dv=dot(Pb,dObig)
            if mode==0:
                dq_t=dotg(R1,kt,TN); dq_l=dotg(R2,kl,TN)
            elif mode==2:
                dq_t=dot(ktT[64*s:64*s+64],R1)
                dq_l=dot(klT[16*h:16*h+16],R2)
            elif mode==1:
                dq_t=dotg(kt,R1,TN).T; dq_l=dotg(kl,R2,TN).T
            cur=(dq_t,dk_t,dv[:,:128])
            curl=(dq_l,dk_l,dv[:,128:])
            if mode==2:
                dqlT[16*h:16*h+16,:]=dq_l
                if s==1:
                    dpt_ref[0,:,cols]=jnp.concatenate([prev[0],dq_t],0).T.astype(BF)
            for c in range(1 if mode==2 else 0,3):
                if s==1:
                    dpt_ref[c,:,cols]=jnp.where(lane<64,prev[c],cur[c]).astype(BF)
                pv=jnp.zeros((seq,128),BF) if h==0 else dpl_ref[c]
                dpl_ref[c]=jnp.where(lm,curl[c].astype(BF),pv)
            prev=cur
    if mode==2: dpl_ref[0]=dqlT[...].T.astype(BF)

def attn_bwd(mode,lengths,qt,kt,vt,ql,kl,vl,ot,ol,lse,dO,dol):
    rows=qt.shape[0]; pages=lengths.shape[0]; seq=rows//pages
    rb=lambda n: pl.BlockSpec((seq,n),lambda p,*_:(p,0))
    return pl.pallas_call(functools.partial(attn_bwd_kernel,mode),
        grid_spec=pltpu.PrefetchScalarGridSpec(num_scalar_prefetch=1,grid=(pages,),
            in_specs=[rb(384)]*3+[rb(128)]*3+[rb(384),rb(128),rb(128),rb(384),rb(128)],
            out_specs=[pl.BlockSpec((3,seq,384),lambda p,*_:(0,p,0)),pl.BlockSpec((3,seq,128),lambda p,*_:(0,p,0))],
            scratch_shapes=[pltpu.VMEM((128,seq),F32)]),
        out_shape=[jax.ShapeDtypeStruct((3,rows,384),BF),jax.ShapeDtypeStruct((3,rows,128),BF)],
        compiler_params=pltpu.CompilerParams(vmem_limit_bytes=VLIM),name=f"attn_bwd{mode}")(lengths,qt,kt,vt,ql,kl,vl,ot,ol,lse,dO,dol)


EPS=1e-5
def gelu_parts(x):
    cdf=0.5+0.5*lax.erf(x*0.7071067811865476)
    phi=jnp.exp2(x*x*-0.7213475204444817-1.3257480647361593)
    return cdf, cdf+x*phi

def norm(v):
    mu=jnp.mean(v,-1,keepdims=True)
    c=v-mu
    inv=lax.rsqrt(jnp.mean(c*c,-1,keepdims=True)+EPS)
    return c*inv,inv

def norm_back(g,u,inv,gain):
    s=g*gain
    return inv*(s-jnp.mean(s,-1,keepdims=True)-u*jnp.mean(s*u,-1,keepdims=True))

def stream(own_col, own_off, x, o, o_own, cot, outw, up, down, shift, gain, upb, act, gp, out_ref, dr1_ref, dos, gup, gdn, gout, stat, bstat, first, chunk):
    d=x.shape[1]; F=up.shape[1]; half=F//2
    h1u,i1=norm(x.astype(F32)+dot(o,outw[...])+shift[2:3])
    h1=h1u*gain[0:1]+shift[0:1]
    h1b=h1.astype(BF)
    for f in range(0,F,chunk):
        cs=slice(f,f+chunk)
        pre=dot(h1b,up[:,cs])+upb[:,cs]
        cdf,der=gelu_parts(pre)
        act[:,cs]=(pre*cdf).astype(BF)
        gp[:,cs]=der.astype(BF)
    r2=h1+dot(act[...],down[...])+shift[3:4]
    u2,i2=norm(r2)
    out_ref[...]=u2*gain[1:2]+shift[1:2]
    g=cot.astype(F32)
    dr2=norm_back(g,u2,i2,gain[1:2])
    dr2b=dr2.astype(BF)
    for f in range(0,F,chunk):
        cs=slice(f,f+chunk)
        da=dotg(dr2b,down[cs,:],NT)
        gp[:,cs]=(da*gp[:,cs].astype(F32)).astype(BF)
    dh1=dotg(gp[...],up[...],NT)+dr2
    dr1=norm_back(dh1,h1u,i1,gain[0:1])
    dr1_ref[...]=dr1
    dr1b=dr1.astype(BF)
    dO=dotg(dr1b,outw[...],NT).astype(BF)
    w=dO.shape[1]//2
    dos[0]=dO[:,:w]; dos[1]=dO[:,w:]
    osl=pl.ds(pl.multiple_of(own_off,128),half)
    dpo=gp[:,osl]
    ones=jnp.ones((8,x.shape[0]),BF)
    rs=lambda v: jnp.sum(v,0,keepdims=True)
    st=jnp.concatenate([rs(dh1),rs(g),rs(dr1),rs(dr2),rs(dh1*h1u),rs(g*u2),jnp.zeros((2,d),F32)],0)
    def put(first):
        for ref,a,b in ((gup,h1b,dpo),(gdn,dr2b,act[:,osl]),(gout,dr1b,o_own)):
            v=dotg(a,b,TN)
            if first: ref[...]=v
            else: ref[...]+=v
        b=dot(ones,dpo)
        if first:
            stat[...]=st; bstat[...]=b
        else:
            stat[...]+=st; bstat[...]+=b
    pl.when(first)(lambda: put(True))
    pl.when(jnp.logical_not(first))(lambda: put(False))

def ffn_kernel(mp_ref, xt, xl, oa, ob, ola, olb, ct, cl, outw, up, down, sh, ga, upb, outwl, upl, downl, shl, gal, upbl,
               to, lo, dr1, dr1l, dos, dosl, gup, gdn, gout, st, bst, gupl, gdnl, goutl, stl, bstl, act, gp, actl, gpl):
    mp=mp_ref[0]
    first=pl.program_id(0)==0
    def both(a,b):
        a=a[...]; b=b[...]
        z=mp==0
        return jnp.concatenate([jnp.where(z,a,b),jnp.where(z,b,a)],1)
    stream(None,mp*1536,xt[...],both(oa,ob),oa[...],ct[...],outw,up,down,sh,ga,upb,act,gp,to,dr1,dos,gup,gdn,gout,st,bst,first,512)
    stream(None,mp*384,xl[...],both(ola,olb),ola[...],cl[...],outwl,upl,downl,shl,gal,upbl,actl,gpl,lo,dr1l,dosl,gupl,gdnl,goutl,stl,bstl,first,768)

def ffn(mp,xt,xl,oa,ob,ola,olb,ct,cl,wts,tile=384):
    rows=xt.shape[0]
    rb=lambda a: pl.BlockSpec((tile,a.shape[1]),lambda p,*_:(p,0))
    full=lambda a: pl.BlockSpec(a.shape,lambda p,*_:(0,)*len(a.shape),pipeline_mode=pl.Buffered(1))
    S=jax.ShapeDtypeStruct
    ins=[xt,xl,oa,ob,ola,olb,ct,cl]
    rowout=[S((rows,768),F32),S((rows,192),F32),S((rows,768),F32),S((rows,192),F32)]
    dos=[S((2,rows,384),BF),S((2,rows,128),BF)]
    acc=[S((768,1536),F32),S((768,1536),F32),S((768,384),F32),S((8,768),F32),S((8,1536),F32),
         S((192,384),F32),S((192,384),F32),S((192,128),F32),S((8,192),F32),S((8,384),F32)]
    return pl.pallas_call(ffn_kernel,
        grid_spec=pltpu.PrefetchScalarGridSpec(num_scalar_prefetch=1,grid=(rows//tile,),
            in_specs=[rb(a) for a in ins]+[full(w) for w in wts],
            out_specs=[rb(a) for a in rowout]+[pl.BlockSpec((2,tile,a.shape[2]),lambda p,*_:(0,p,0)) for a in dos]+[full(a) for a in acc],
            scratch_shapes=[pltpu.VMEM((tile,3072),BF),pltpu.VMEM((tile,3072),BF),pltpu.VMEM((tile,768),BF),pltpu.VMEM((tile,768),BF)]),
        out_shape=rowout+dos+acc,
        compiler_params=pltpu.CompilerParams(vmem_limit_bytes=VLIM),name="middle")(mp,*ins,*wts)


from jax.sharding import PartitionSpec as P


def pack_kernel(idx_ref, *refs):
    out=refs[-1]
    out[...]=jnp.zeros_like(out)
    r=0
    for src in refs[:-1]:
        lead=src.shape[0] if len(src.shape)==3 else None
        for c in range(lead or 1):
            w=src[c] if lead else src[...]
            n,m=w.shape
            for j in range(0,m,128):
                e=min(128,m-j)
                out[r:r+n,:e]=w[:,j:j+e].astype(F32)
                r+=n


def pack(idx, split, whole, parts):
    specs=[]; n=0
    for a in split:
        rows=a.shape[-2]//parts
        blocks=-(-a.shape[-1]//128)
        if a.ndim==3:
            specs.append(pl.BlockSpec((a.shape[0],rows,a.shape[2]),lambda i,s:(0,s[0],0)))
            n+=a.shape[0]*rows*blocks
        else:
            specs.append(pl.BlockSpec((rows,a.shape[1]),lambda i,s:(s[0],0)))
            n+=rows*blocks
    for a in whole:
        specs.append(pl.BlockSpec(a.shape,lambda i,s:(0,0)))
        n+=a.shape[0]*(-(-a.shape[1]//128))
    n=-(-n//8)*8
    return pl.pallas_call(pack_kernel,
        grid_spec=pltpu.PrefetchScalarGridSpec(num_scalar_prefetch=1,grid=(1,),in_specs=specs,
            out_specs=pl.BlockSpec((n,128),lambda i,s:(0,0))),
        out_shape=jax.ShapeDtypeStruct((n,128),F32),
        compiler_params=pltpu.CompilerParams(vmem_limit_bytes=VLIM),name="pack")(idx,*split,*whole)


def unpack_first_kernel(s_ref, pa, pb, pc, pd, o_own, u_own, d_own, wt, wl, bt, bl, outl, upl, downl, upb, upbl, s48, s24, s96, su):
    mp=s_ref[0]; other=1-mp
    wl[...]=jnp.zeros_like(wl); outl[...]=jnp.zeros_like(outl); s24[...]=jnp.zeros_like(s24)
    bt[...]=jnp.zeros_like(bt); bl[...]=jnp.zeros_like(bl)
    for p,ref in enumerate((pa,pb,pc,pd)):
        i=s_ref[1+p]
        at=lambda n: pl.ds(pl.multiple_of(i*n,n),n)
        r=0
        for c in range(3):
            for j in range(3):
                wt[c,at(192),128*j:128*j+128]=ref[r:r+192].astype(BF); r+=192
        for c in range(3):
            wl[c,at(48),:]=ref[r:r+48].astype(BF); r+=48
        s24[at(24),:128]=ref[r:r+24]; r+=24
        s24[at(24),128:]=ref[r:r+24,:64]; r+=24
        for j in range(3):
            su[at(48),128*j:128*j+128]=ref[r:r+48].astype(BF); r+=48
        s96[at(96),:128]=ref[r:r+96].astype(BF); r+=96
        s96[at(96),128:]=ref[r:r+96,:64].astype(BF); r+=96
        if p==0:
            for c in range(2):
                for j in range(3):
                    bt[2*c:2*c+1,128*j:128*j+128]=ref[r+2*j+c:r+2*j+c+1]
            r+=6
            for c in range(2):
                bl[2*c:2*c+1,:]=ref[r+c:r+c+1]
            r+=2
            base=pl.multiple_of(other*1536,128)
            for j in range(12):
                upb[:,pl.ds(base+128*j,128)]=ref[r+j:r+j+1]
            r+=12
            base=pl.multiple_of(other*384,128)
            for j in range(3):
                upbl[:,pl.ds(base+128*j,128)]=ref[r+j:r+j+1]
    half=lambda k,n: pl.ds(pl.multiple_of(k*n,n),n)
    outl[half(mp,128),:]=jnp.concatenate([o_own[...],jnp.zeros((32,192),BF)],0)
    outl[half(other,128),:]=s24[...].astype(BF)
    upl[:,half(mp,384)]=u_own[...]; upl[:,half(other,384)]=su[...]
    downl[half(mp,384),:]=d_own[...]; downl[half(other,384),:]=s96[...]


def unpack_first(scal, pieces, o_own, u_own, d_own, ub_own, ubl_own):
    S=jax.ShapeDtypeStruct
    full=lambda a: pl.BlockSpec(a.shape,lambda i,*_:(0,)*len(a.shape))
    outs=[S((3,768,384),BF),S((3,192,128),BF),S((3,384),F32),S((3,128),F32),S((256,192),BF),S((192,768),BF),S((768,192),BF),S((1,3072),F32),S((1,768),F32)]
    ins=[*pieces,o_own,u_own,d_own]
    res=pl.pallas_call(unpack_first_kernel,
        grid_spec=pltpu.PrefetchScalarGridSpec(num_scalar_prefetch=1,grid=(1,),in_specs=[full(a) for a in ins],
            out_specs=[full(a) for a in outs],
            scratch_shapes=[pltpu.VMEM((8,128),F32),pltpu.VMEM((128,192),F32),pltpu.VMEM((384,192),BF),pltpu.VMEM((192,384),BF)]),
        out_shape=outs,compiler_params=pltpu.CompilerParams(vmem_limit_bytes=VLIM),name="unpack_first")(scal,*ins)
    return res


def unpack_rows_kernel(parts, axis, s_ref, *refs):
    pieces=refs[:parts]; own=refs[parts]; out=refs[parts+1]
    mp=s_ref[0]; other=1-mp
    n,m=own.shape
    rows=n//parts
    if axis==1:
        out[:,pl.ds(pl.multiple_of(mp*m,128),m)]=own[...]
    else:
        out[pl.ds(pl.multiple_of(mp*n,n),n),:]=own[...]
    for p,ref in enumerate(pieces):
        i=s_ref[1+p]
        for j in range(m//128):
            v=ref[j*rows:j*rows+rows].astype(BF)
            if axis==1:
                out[pl.ds(pl.multiple_of(i*rows,rows),rows),pl.ds(pl.multiple_of(other*m+128*j,128),128)]=v
            else:
                out[pl.ds(pl.multiple_of(other*n+i*rows,rows),rows),128*j:128*j+128]=v


def unpack_rows(scal, pieces, own, axis, offset=0):
    parts=len(pieces)
    n,m=own.shape
    rows=n//parts*(m//128)
    shape=(n,2*m) if axis==1 else (2*n,m)
    return pl.pallas_call(functools.partial(unpack_rows_kernel,parts,axis),
        grid_spec=pltpu.PrefetchScalarGridSpec(num_scalar_prefetch=1,grid=(1,),
            in_specs=[pl.BlockSpec((rows,128),lambda i,*_:(offset,0)) for _ in pieces]+[pl.BlockSpec(own.shape,lambda i,*_:(0,0))],
            out_specs=pl.BlockSpec(shape,lambda i,*_:(0,0))),
        out_shape=jax.ShapeDtypeStruct(shape,BF),
        compiler_params=pltpu.CompilerParams(vmem_limit_bytes=VLIM),name="unpack")(scal,*pieces,own)


def flip(n, bit):
    return [(i,i^bit) for i in range(n)]


def cross(n):
    return [(i,i^(2 if i%2==0 else 4)) for i in range(n)]


def gather_pieces(piece, n):
    a=lax.ppermute(piece,"mp",[(0,1),(1,0)])
    b=lax.ppermute(a,"dp",cross(n))
    c=lax.ppermute(a,"dp",flip(n,1))
    d=lax.ppermute(b,"dp",flip(n,1))
    return a,b,c,d


def bias_rows(pair):
    b=pair.astype(F32)
    return jnp.stack([b[0],jnp.zeros_like(b[0]),b[1]])


def shards(text_in, layout_in, token_mask, box_mask, lengths, text_mask_vec, layout_mask_vec,
           text_qkv, text_qv_bias, text_out_w, text_shifts, text_gains, text_up, text_up_bias, text_down,
           layout_qkv, layout_qv_bias, layout_out_w, layout_shifts, layout_gains, layout_up, layout_up_bias, layout_down,
           text_cot, layout_cot):
    n=lax.axis_size("dp")
    mp=lax.axis_index("mp").astype(jnp.int32); dp=lax.axis_index("dp").astype(jnp.int32)
    core=dp&1; color=((dp>>1)^(dp>>2))&1
    ids=[2*color+core,2*(1-color)+core,2*color+1-core,2*(1-color)+1-core]
    scal=jnp.stack([mp]+ids)
    idx=ids[0][None]
    first=gather_pieces(pack(idx,[text_qkv,layout_qkv,layout_out_w,layout_up,layout_down],
        [text_qv_bias,layout_qv_bias,text_up_bias[None],layout_up_bias[None]],4),n)
    outp=gather_pieces(pack(idx,[text_out_w],[],4),n)
    upp=gather_pieces(pack(idx,[text_up],[],4),n)
    downp=gather_pieces(pack(idx,[text_down],[],4),n)

    tflag=token_mask[:,None]==1; lflag=box_mask[:,None]==1
    xt=jnp.where(tflag,text_mask_vec[None],text_in)
    xl=jnp.where(lflag,layout_mask_vec[None],layout_in)
    pad=lambda v: jnp.pad(v,((0,0),)*(v.ndim-1)+((0,32),))
    own=attn_fwd(lengths,xt,xl,text_qkv,pad(layout_qkv),bias_rows(text_qv_bias),pad(bias_rows(layout_qv_bias)))
    wt_o,wl_o,bt_o,bl_o,outl,upl,downl,upb,upbl=unpack_first(scal,first,layout_out_w,layout_up,layout_down,None,None)
    place=lambda full,half: lax.dynamic_update_slice(full,half.astype(F32)[None],(0,mp*half.shape[0]))
    upb=place(upb,text_up_bias); upbl=place(upbl,layout_up_bias)
    oth=attn_fwd(lengths,xt,xl,wt_o,wl_o,bt_o,bl_o)
    outw=unpack_rows(scal,outp,text_out_w,0)
    up=unpack_rows(scal,upp,text_up,1)
    down=unpack_rows(scal,downp,text_down,0)
    ws=[outw,up,down,text_shifts.astype(F32),text_gains.astype(F32),upb,outl,upl,downl,layout_shifts.astype(F32),layout_gains.astype(F32),upbl]
    (to,lo,dr1,dr1l,dO,dOl,gup,gdn,gout,st,bst,gupl,gdnl,goutl,stl,bstl)=ffn(mp[None],xt,xl,own[6],oth[6],own[7],oth[7],text_cot,layout_cot,ws)
    rs=lambda v: lax.psum_scatter(v,"dp",scatter_dimension=v.ndim-2,tiled=True)
    gup=rs(gup); gdn=rs(gdn); gout=rs(gout)
    pick=lambda v,k: lax.dynamic_index_in_dim(v,k,0,keepdims=False)
    d_own=attn_bwd(2,lengths,*own,pick(dO,mp),pick(dOl,mp))
    qg=jnp.einsum("nd,cne->cde",xt,d_own[0],preferred_element_type=F32)
    qgl=jnp.einsum("nd,cne->cde",xl,d_own[1],preferred_element_type=F32)[:,:,:96]
    cs=jnp.sum(d_own[0],1,dtype=F32); csl=jnp.sum(d_own[1],1,dtype=F32)[:,:96]
    qg=rs(qg)
    d_oth=attn_bwd(2,lengths,*oth,pick(dO,1-mp),pick(dOl,1-mp))
    back=lambda d,w: jnp.einsum("cne,cde->nd",d,w,preferred_element_type=F32)
    ta=back(d_own[0],text_qkv); tb=back(d_oth[0],wt_o)
    la=back(d_own[1],pad(layout_qkv)); lb=back(d_oth[1],wl_o)
    dx=(ta+tb)+dr1; dxl=(la+lb)+dr1l
    tg=jnp.where(tflag,0.0,dx); lg=jnp.where(lflag,0.0,dxl)
    tv=jnp.sum(jnp.where(tflag,dx,0.0),0); lv=jnp.sum(jnp.where(lflag,dxl,0.0),0)
    mixed=lax.psum((qgl,goutl[:,:96].T,gupl,gdnl.T,cs[0::2],csl[0::2],bst[0],bstl[0],tv,lv,st[:6],stl[:6]),"dp")
    qgl,goutl,gupl,gdnl,cs,csl,bst,bstl,tv,lv,st,stl=mixed
    return (to,lo,tg,lg,tv,lv,qg,cs,gout.T,st[:4],st[4:],gup,bst,gdn.T,
            qgl,csl,goutl,stl[:4],stl[4:],gupl,bstl,gdnl)


def solution(mesh):
    rows=P("dp",None); cols=P(None,"mp"); lead=P("mp",None); cube=P(None,None,"mp")
    weights=(cube,cols,lead,P(),P(),cols,P("mp"),lead)
    return jax.shard_map(shards,mesh=mesh,
        in_specs=(rows,rows,P("dp"),P("dp"),P("dp"),P(),P())+weights+weights+(rows,rows),
        out_specs=(rows,rows,rows,rows,P(),P(),P(None,"dp","mp"),cols,P("mp","dp"),P(),P(),P("dp","mp"),P("mp"),P("mp","dp"),
                   cube,cols,lead,P(),P(),cols,P("mp"),lead),
        check_vma=False)
```

```python
import functools
import jax, jax.numpy as jnp
from jax import lax
from jax.experimental import pallas as pl
from jax.experimental.pallas import tpu as pltpu
F32=jnp.float32; BF=jnp.bfloat16
NT=(((1,),(1,)),((),()))
TN=(((0,),(0,)),((),()))
def dot(a,b): return jnp.dot(a,b,preferred_element_type=F32)
def dotg(a,b,dn): return lax.dot_general(a,b,dn,preferred_element_type=F32)
VLIM=60*1024*1024

def cost(us): return pl.CostEstimate(flops=int(us*1e7),bytes_accessed=1024,transcendentals=0)

def lane_iota(shape): return lax.broadcasted_iota(jnp.int32,shape,len(shape)-1)

def attn_fwd_kernel(first, len_ref, half_ref, xt_ref, xl_ref, wt_ref, wl_ref, bt_ref, bl_ref, *rest):
    qt_ref, kt_ref, vt_ref, ql_ref, kl_ref, vl_ref, ot_ref, ol_ref, lse_ref, olT, lseT=rest[-11:]
    page=first+pl.program_id(0)
    seq=xt_ref.shape[0]
    xt=xt_ref[...]; xl=xl_ref[...]
    for c,(t,l) in enumerate(((qt_ref,ql_ref),(kt_ref,kl_ref),(vt_ref,vl_ref))):
        t[...]=(dot(xt,wt_ref[c])+bt_ref[c:c+1,:]).astype(BF)
        l[...]=(dot(xl,wl_ref[c])+bl_ref[c:c+1,:]).astype(BF)
    lane=lane_iota((seq,128))
    row=lax.broadcasted_iota(jnp.int32,(seq,128),0)
    length=len_ref[page]
    bias=jnp.where(row<length,0.0,-1e9).astype(BF)
    one=jnp.ones((seq,128),BF)
    ql=jnp.where(lane==96,one,ql_ref[...]*BF(0.25))
    kl=jnp.where(lane==96,bias,kl_ref[...])
    vlT=vl_ref[...].T
    zero=jnp.zeros((seq,128),BF)
    olT[...]=jnp.zeros_like(olT); lseT[...]=jnp.zeros_like(lseT)
    for j in range(3):
        cols=slice(128*j,128*j+128)
        qbig=jnp.concatenate([qt_ref[:,cols]*BF(0.125),ql],1)
        vT=vt_ref[:,cols].T
        halves=[]
        for s in range(2):
            h=2*j+s
            kbig=jnp.concatenate([jnp.where(lane//64==s,kt_ref[:,cols],zero),
                                  jnp.where((lane//16==h)|(lane==96),kl,zero)],1)
            S=dotg(kbig,qbig,NT)
            m=jnp.max(S,0,keepdims=True)
            e=jnp.exp(S-m)
            ssum=jnp.sum(e,0,keepdims=True)
            v80=jnp.concatenate([vT[64*s:64*s+64],vlT[16*h:16*h+16]],0)
            o=dot(v80,e.astype(BF))*(1.0/ssum)
            halves.append(o[:64])
            olT[16*h:16*h+16,:]=o[64:]
            lseT[h:h+1,:]=m+jnp.log(ssum)
        ot_ref[:,cols]=jnp.concatenate(halves,0).T.astype(BF)
    ol_ref[...]=olT[...].T.astype(BF)
    lse_ref[...]=pltpu.roll(lseT[...].T,97,1)

def attn_fwd(first, count, lengths, half, xt, xl, wt, wl, bt, bl, prev):
    rows=xt.shape[0]; pages=lengths.shape[0]; seq=rows//pages
    rb=lambda n: pl.BlockSpec((seq,n),lambda p,*_:(first+p,0))
    full=lambda a: pl.BlockSpec((None,)*(a.ndim-3)+a.shape[-3:],lambda p,l,h:(h[0],0,0,0)[4-a.ndim:]) if a.ndim>2 else pl.BlockSpec(a.shape,lambda p,*_:(0,0))
    whole=pl.BlockSpec(memory_space=pl.ANY)
    o=lambda n,d=BF: jax.ShapeDtypeStruct((rows,n),d)
    return pl.pallas_call(functools.partial(attn_fwd_kernel,first),
        grid_spec=pltpu.PrefetchScalarGridSpec(num_scalar_prefetch=2,grid=(count,),
            in_specs=[rb(768),rb(192),full(wt),full(wl),full(bt),full(bl)]+[whole]*len(prev),
            out_specs=[rb(384)]*3+[rb(128)]*3+[rb(384),rb(128),rb(128)],
            scratch_shapes=[pltpu.VMEM((128,seq),F32),pltpu.VMEM((128,seq),F32)]),
        out_shape=[o(384)]*3+[o(128)]*3+[o(384),o(128),o(128,F32)],
        input_output_aliases={8+i:i for i in range(len(prev))},
        compiler_params=pltpu.CompilerParams(vmem_limit_bytes=VLIM),cost_estimate=cost(6.2*count),name="attn_fwd")(lengths,half,xt,xl,wt,wl,bt,bl,*prev)

def ind_matrix(j):
    r=lax.broadcasted_iota(jnp.int32,(256,128),0)%128
    l=lax.broadcasted_iota(jnp.int32,(256,128),1)
    h=(r//64+2*j) if j is not None else r//16
    return jnp.where((l==97+h)&(h<6),1.0,0.0).astype(BF)

def split2(v):
    hi=v.astype(BF)
    return hi,(v-hi.astype(F32)).astype(BF)

def bwd_page(length, qt_ref, kt_ref, vt_ref, ql_ref, kl_ref, vl_ref, ot_ref, ol_ref, lse_ref, dot_ref, dol_ref,
                    dpt_ref, dpl_ref, dqlT):
    seq=qt_ref.shape[0]
    lane=lane_iota((seq,128))
    row=lax.broadcasted_iota(jnp.int32,(seq,128),0)
    bias=jnp.where(row<length,0.0,-1e9).astype(BF)
    zero=jnp.zeros((seq,128),BF); one=jnp.ones((seq,128),BF)
    nl=-lse_ref[...]
    hi=nl.astype(BF); r1=nl-hi.astype(F32); mid=r1.astype(BF); lo=r1-mid.astype(F32)
    ext=hi+pltpu.roll(mid.astype(F32),7,1).astype(BF)+pltpu.roll(lo,14,1).astype(BF)
    qle=jnp.where(lane<96,ql_ref[...]*BF(0.25),jnp.where(lane==96,one,ext))
    kl=kl_ref[...]; vl=vl_ref[...]; ql=ql_ref[...]
    klT=kl.T
    dqlT[...]=jnp.zeros_like(dqlT)
    def sums(a,b,m):
        p=a.astype(F32)*b.astype(F32)
        h_,l_=split2(p)
        return dot(jnp.concatenate([h_,l_],1),m)
    dol=dol_ref[...]
    d_l=sums(dol,ol_ref[...],ind_matrix(None))
    d_t=d_l
    for j in range(3):
        cols=slice(128*j,128*j+128)
        d_t=d_t+sums(dot_ref[:,cols],ot_ref[:,cols],ind_matrix(j))
    def ext_delta(d):
        h_=d.astype(BF); l_=d-h_.astype(F32)
        return h_+pltpu.roll(l_,7,1).astype(BF)
    dol1=jnp.where(lane<96,dol*BF(0.125),ext_delta(d_t*-0.125))
    dol2=jnp.where(lane<96,dol*BF(0.25),ext_delta(d_l*-0.25))
    for j in range(3):
        cols=slice(128*j,128*j+128)
        qt=qt_ref[:,cols]; kt=kt_ref[:,cols]; vt=vt_ref[:,cols]; dO=dot_ref[:,cols]
        qbig=jnp.concatenate([qt*BF(0.125),qle],1)
        dbig=jnp.concatenate([dO*BF(0.125),dol1],1)
        dObig=jnp.concatenate([dO,dol],1)
        prev=None
        ktT=kt.T
        for s in range(2):
            h=2*j+s
            tm=lane//64==s; lm=lane//16==h
            kbig=jnp.concatenate([jnp.where(tm,kt,zero),jnp.where(lm,kl,jnp.where(lane==96,bias,
                 jnp.where((lane==97+h)|(lane==104+h)|(lane==111+h),one,zero)))],1)
            vle=jnp.where(lm,vl,jnp.where((lane==97+h)|(lane==104+h),one,zero))
            vbig=jnp.concatenate([jnp.where(tm,vt,zero),vle],1)
            S=dotg(kbig,qbig,NT)
            M1=dotg(vbig,dbig,NT)
            M2=dotg(vle,dol2,NT)
            Pm=jnp.exp(S)
            Pb=Pm.astype(BF)
            R1=(Pm*M1).astype(BF)
            R2=(Pm*M2).astype(BF)
            dk_t=dot(R1,qt); dk_l=dot(R2,ql); dv=dot(Pb,dObig)
            dq_t=dot(ktT[64*s:64*s+64],R1)
            dq_l=dot(klT[16*h:16*h+16],R2)
            cur=(dq_t,dk_t,dv[:,:128])
            curl=(dq_l,dk_l,dv[:,128:])
            dqlT[16*h:16*h+16,:]=dq_l
            if s==1:
                dpt_ref[0,:,cols]=jnp.concatenate([prev[0],dq_t],0).T.astype(BF)
            for c in range(1,3):
                if s==1:
                    dpt_ref[c,:,cols]=jnp.where(lane<64,prev[c],cur[c]).astype(BF)
                pv=jnp.zeros((seq,128),BF) if h==0 else dpl_ref[c]
                dpl_ref[c]=jnp.where(lm,curl[c].astype(BF),pv)
            prev=cur
    dpl_ref[0]=dqlT[...].T.astype(BF)

def bwd_kernel(first, len_ref, half_ref, qt, kt, vt, ql, kl, vl, ot, ol, lse, dO, dOl, *rest):
    dpt,dpl,dqlT=rest[-3:]
    bwd_page(len_ref[first+pl.program_id(0)],qt,kt,vt,ql,kl,vl,ot,ol,lse,dO.at[0],dOl.at[0],dpt,dpl,dqlT)


def attn_bwd(first,count,lengths,half,saved,dO,dOl,prev):
    rows=saved[0].shape[0]; seq=rows//lengths.shape[0]
    rb=lambda n: pl.BlockSpec((seq,n),lambda i,*_:(first+i,0))
    hb=lambda n: pl.BlockSpec((1,seq,n),lambda i,l,h:(h[0],first+i,0))
    pb=lambda n: pl.BlockSpec((3,seq,n),lambda i,l,h:(h[0],first+i,0))
    whole=pl.BlockSpec(memory_space=pl.ANY)
    return pl.pallas_call(functools.partial(bwd_kernel,first),
        grid_spec=pltpu.PrefetchScalarGridSpec(num_scalar_prefetch=2,grid=(count,),
            in_specs=[rb(384)]*3+[rb(128)]*3+[rb(384),rb(128),rb(128),hb(384),hb(128)]+[whole]*len(prev),
            out_specs=[pb(384),pb(128)],scratch_shapes=[pltpu.VMEM((128,seq),F32)]),
        out_shape=[jax.ShapeDtypeStruct((6,rows,384),BF),jax.ShapeDtypeStruct((6,rows,128),BF)],
        input_output_aliases={13+i:i for i in range(len(prev))},
        compiler_params=pltpu.CompilerParams(vmem_limit_bytes=VLIM),cost_estimate=cost(9*count),name="attn_bwd")(lengths,half,*saved,dO,dOl,*prev)


def dx_kernel(dpt, dpl, wt, wl, dr1, dr1l, tm, lm, dx, dxl, wts, wls):
    @pl.when(pl.program_id(0)==0)
    def _():
        for h in range(2):
            for c in range(3):
                i=3*h+c
                wts[:,384*i:384*i+384]=wt[h,c]
                wls[:,128*i:128*i+128]=wl[h,c]
    def back(d,w,base,flag):
        v=dotg(jnp.concatenate([d[i] for i in range(6)],1),w[...],NT)+base[...]
        return jnp.where(flag[...]==1,0.0,v)
    dx[...]=back(dpt,wts,dr1,tm)
    dxl[...]=back(dpl,wls,dr1l,lm).T


def input_grad(tile,dp,wts,dr1,dr1l,tm,lm):
    rows=dr1.shape[0]
    rb=lambda n: pl.BlockSpec((tile,n),lambda i:(i,0))
    pb=lambda n: pl.BlockSpec((6,tile,n),lambda i:(0,i,0))
    full=lambda a: pl.BlockSpec(a.shape,lambda i:(0,0,0,0))
    return pl.pallas_call(dx_kernel,grid=(rows//tile,),
        in_specs=[pb(384),pb(128)]+[full(w) for w in wts]+[rb(768),rb(192),rb(1),rb(1)],
        out_specs=[rb(768),pl.BlockSpec((192,tile),lambda i:(0,i))],
        scratch_shapes=[pltpu.VMEM((768,2304),BF),pltpu.VMEM((192,768),BF)],
        out_shape=[jax.ShapeDtypeStruct((rows,768),F32),jax.ShapeDtypeStruct((192,rows),F32)],
        compiler_params=pltpu.CompilerParams(vmem_limit_bytes=VLIM),cost_estimate=cost(5),name="input_grad")(*dp,*wts,dr1,dr1l,tm,lm)


def place_blocks(acc, keep, send, sem, position, n):
    if n!=16:
        cp=pltpu.make_async_copy(acc,keep,sem); cp.start(); cp.wait()
        return
    c=position&1; x=(position>>1)&1; z0=(position>>2)&1; z1=(position>>3)&1
    rows=acc.shape[0]//16
    copies=[]
    for out,core in ((keep,c),(send,1-c)):
        for q in range(8):
            r2,r3,r4=q>>2,(q>>1)&1,q&1
            fx=jnp.where(core==0,r2,r3); fz=jnp.where(core==0,r3,r2)
            block=(z1^r4)*8+(z0^fz)*4+(x^fx)*2+core
            copies.append(pltpu.make_async_copy(acc.at[pl.ds(pl.multiple_of(block*rows,8),rows)],out.at[pl.ds(q*rows,rows)],sem))
    for cp in copies: cp.start()
    for cp in copies: cp.wait()


def block_shapes(rows,cols,n):
    S=jax.ShapeDtypeStruct
    if n!=16: return [S((rows,cols),F32),S((8,128),F32)]
    return [S((rows//2,cols),F32)]*2


def qkv_grad_kernel(n, pos_ref, xt, xl, dpt, dpl, sel, wt, wl, keep, send, acc, sums, suml, sem):
    x=xt[...]; s=sel[...]; xv=xl[...]
    def add(first):
        def put(ref,v):
            if first: ref[...]=v
            else: ref[...]+=v
        for c in range(3):
            put(acc.at[:,384*c:384*c+384],dotg(x,dpt[c],TN))
            put(acc.at[192*c:192*c+192,1152:],dotg(xv,dpl[c],TN))
            put(sums.at[c],dot(s,dpt[c])); put(suml.at[c],dot(s,dpl[c]))
    first=pl.program_id(0)==0
    pl.when(first)(lambda: add(True))
    pl.when(jnp.logical_not(first))(lambda: add(False))
    @pl.when(pl.program_id(0)==pl.num_programs(0)-1)
    def _():
        rest=[]
        t=jnp.zeros((8,768),F32); l=jnp.zeros((8,192),F32)
        for c in range(3):
            a=sums[c]; b=suml[c]
            rest.extend([a[:,128*j:128*j+128] for j in range(3)]+[b])
            for v,w,text in ((a,wt,True),(b,wl,False)):
                hi,lo=split2(v)
                lo2=(v-hi.astype(F32)-lo.astype(F32)).astype(BF)
                y=dotg(hi,w[0,c],NT)+dotg(lo,w[0,c],NT)+dotg(lo2,w[0,c],NT)
                if text: t=t+y
                else: l=l+y
        rest.extend([t[:,128*j:128*j+128] for j in range(6)]+[l[:,:128],jnp.concatenate([l[:,128:],jnp.zeros((8,64),F32)],1),jnp.zeros((32,128),F32)])
        acc[576:768,1152:]=jnp.concatenate(rest,0)
        place_blocks(acc,keep,send,sem,pos_ref[1],n)


def qkv_grad(n,pos,pages,xt,xl,dpt,dpl,sel,wt,wl):
    seq=xt.shape[0]//pages
    rb=lambda m: pl.BlockSpec((seq,m),lambda i,s:(i,0))
    pb=lambda m: pl.BlockSpec((3,seq,m),lambda i,s:(s[0],i,0))
    wb=lambda a: pl.BlockSpec((1,)+a.shape[1:],lambda i,s:(s[0],0,0,0))
    whole=pl.BlockSpec(memory_space=pl.ANY)
    return pl.pallas_call(functools.partial(qkv_grad_kernel,n),
        grid_spec=pltpu.PrefetchScalarGridSpec(num_scalar_prefetch=1,grid=(pages,),
            in_specs=[rb(768),rb(192),pb(384),pb(128),pl.BlockSpec((8,seq),lambda i,s:(0,i)),wb(wt),wb(wl)],
            out_specs=[whole,whole],
            scratch_shapes=[pltpu.VMEM((768,1280),F32),pltpu.VMEM((3,8,384),F32),pltpu.VMEM((3,8,128),F32),pltpu.SemaphoreType.DMA]),
        out_shape=block_shapes(768,1280,n),
        compiler_params=pltpu.CompilerParams(vmem_limit_bytes=VLIM),cost_estimate=cost(8),name="qkv_grad")(pos,xt,xl,dpt,dpl,sel,wt,wl)


EPS=1e-5
def gelu_parts(x):
    cdf=0.5+0.5*lax.erf(x*0.7071067811865476)
    phi=jnp.exp2(x*x*-0.7213475204444817-1.3257480647361593)
    return cdf, cdf+x*phi

def norm(v):
    mu=jnp.mean(v,-1,keepdims=True)
    c=v-mu
    inv=lax.rsqrt(jnp.mean(c*c,-1,keepdims=True)+EPS)
    return c*inv,inv

def norm_back(g,u,inv,gain):
    s=g*gain
    return inv*(s-jnp.mean(s,-1,keepdims=True)-u*jnp.mean(s*u,-1,keepdims=True))

def stream(own_col, own_off, x, o, o_own, cot, outw, up, down, shift, gain, upb, act, gp, out_ref, dr1_ref, dos, gup, gdn, gout, stat, bstat, first, chunk, flag, hook):
    d=x.shape[1]; F=up.shape[1]; half=F//2
    h1u,i1=norm(x.astype(F32)+dot(o,outw[...])+shift[2:3])
    h1=h1u*gain[0:1]+shift[0:1]
    h1b=h1.astype(BF)
    for f in range(0,F,chunk):
        cs=slice(f,f+chunk)
        pre=dot(h1b,up[:,cs])+upb[:,cs]
        cdf,der=gelu_parts(pre)
        act[:,cs]=(pre*cdf).astype(BF)
        gp[:,cs]=der.astype(BF)
    if hook is not None: hook()
    r2=h1+dot(act[...],down[...])+shift[3:4]
    u2,i2=norm(r2)
    y=u2*gain[1:2]+shift[1:2]
    out_ref[...]=y if out_ref.shape==y.shape else y.T
    g=cot.astype(F32)
    dr2=norm_back(g,u2,i2,gain[1:2])
    dr2b=dr2.astype(BF)
    for f in range(0,F,chunk):
        cs=slice(f,f+chunk)
        da=dotg(dr2b,down[cs,:],NT)
        gp[:,cs]=(da*gp[:,cs].astype(F32)).astype(BF)
    dh1=dotg(gp[...],up[...],NT)+dr2
    dr1=norm_back(dh1,h1u,i1,gain[0:1])
    dr1_ref[...]=dr1
    dr1b=dr1.astype(BF)
    dO=dotg(dr1b,outw[...],NT).astype(BF)
    w=dO.shape[1]//2
    dos[0]=dO[:,:w]; dos[1]=dO[:,w:]
    osl=pl.ds(pl.multiple_of(own_off,128),half)
    dpo=gp[:,osl]
    ones=jnp.ones((8,x.shape[0]),BF)
    rs=lambda v: jnp.sum(v,0,keepdims=True)
    st=jnp.concatenate([rs(dh1),rs(g),rs(dr1),rs(dr2),rs(dh1*h1u),rs(g*u2),rs(jnp.where(flag==1,dr1,0.0)),jnp.zeros((1,d),F32)],0)
    def put(first):
        for ref,a,b in ((gup,h1b,dpo),(gdn,dr2b,act[:,osl]),(gout,dr1b,o_own)):
            v=dotg(a,b,TN)
            if first: ref[...]=v
            else: ref[...]+=v
        b=dot(ones,dpo)
        if first:
            stat[...]=st; bstat[...]=b
        else:
            stat[...]+=st; bstat[...]+=b
    pl.when(first)(lambda: put(True))
    pl.when(jnp.logical_not(first))(lambda: put(False))

def ffn_kernel(n, s_ref, *refs):
    (xt, xl, oa, ob, ola, olb, ct, cl, tm, lm, sh, ga, shl, gal)=refs[:14]
    (up_own, outw_own, down_own, outl_own, upl_own, downl_own, upb_own, upbl_own)=refs[14:22]
    second=refs[22:30]; third=[refs[30+2*i:32+2*i] for i in range(4)]
    (to, lo, dr1, dr1l, dos, dosl, keep, send)=refs[38:46]
    (act, gp, actl, gpl, acc, up, outw, down, outwl, upl, downl, upb, upbl, st, bst, gupl, gdnl, goutl, stl, bstl, sem, sem_own, sem2, sem3)=refs[46:]
    mp=s_ref[0]; other=1-mp
    first=pl.program_id(0)==0
    half=lambda k,m: pl.ds(pl.multiple_of(k*m,m),m)
    column=lambda k: acc.at[:,128*k:128*k+128]
    own=[pltpu.make_async_copy(src,dst,sem_own.at[i]) for i,(src,dst) in enumerate((
        (outw_own,outw.at[half(mp,384),:]),(up_own,up.at[:,half(mp,1536)]),(down_own,down.at[half(mp,1536),:])))]
    two=[]; three=[]
    for i,src in enumerate(second):
        two.append([pltpu.make_async_copy(src.at[lo_:hi_],column(2*i+k).at[0:hi_-lo_],sem2.at[i,k]) for k,(lo_,hi_) in enumerate(((0,768),(768,1440)))])
    for i,src in enumerate(third):
        base=16+4*i if i<3 else 0
        three.append([pltpu.make_async_copy(src[s].at[r:r+m],column(base+k).at[d:d+m],sem3.at[i,q])
            for q,(s,r,k,d,m) in enumerate(((0,0,0,0,768),(0,768,1,0,384),(1,0,1,384,384),(1,384,2,0,768),(1,1152,3,0,400)))])
    @pl.when(first)
    def _():
        for cp in own: cp.start()
        for cps in two:
            for cp in cps: cp.start()
        for cps in three[:3]:
            for cp in cps: cp.start()
        for i,cps in enumerate(two):
            for cp in cps: cp.wait()
            p=s_ref[6+i]
            a,b=column(2*i),column(2*i+1)
            for j in range(12):
                src=a[96*j:96*j+96] if j<8 else b[96*(j-8):96*(j-8)+96]
                up[half(p,96),pl.ds(pl.multiple_of(other*1536+128*j,128),128)]=src.astype(BF)
            for j in range(6):
                outw[pl.ds(pl.multiple_of(other*384+p*48,16),48),128*j:128*j+128]=b[384+48*j:432+48*j].astype(BF)
        for cp in three[3]: cp.start()
        own[0].wait(); own[1].wait()
    def unpack_small():
        tail=[]
        for i in range(4):
            p=s_ref[2+i]
            v=column((16+4*i if i<3 else 0)+3)
            goutl[pl.ds(pl.multiple_of(p*24,8),24),:]=v[0:24]
            gdnl[pl.ds(pl.multiple_of(p*24,8),24),0:128]=v[24:48]
            for j in range(3):
                upl[pl.ds(pl.multiple_of(p*48,16),48),pl.ds(pl.multiple_of(other*384+128*j,128),128)]=v[48+48*j:96+48*j].astype(BF)
            rows=pl.ds(pl.multiple_of(other*384+p*96,16),96)
            downl[rows,0:128]=v[192:288].astype(BF)
            downl[rows,128:192]=v[288:384][:,:64].astype(BF)
        outwl[half(other,128),:]=jnp.concatenate([jnp.concatenate([goutl[0:96],gdnl[0:96,0:64]],1).astype(BF),jnp.zeros((32,192),BF)],0)
    def load_bias():
        v=column(19)
        for j in range(12):
            upb[:,pl.ds(pl.multiple_of(other*1536+128*j,128),128)]=v[384+j:385+j]
        for j in range(3):
            upbl[:,pl.ds(pl.multiple_of(other*384+128*j,128),128)]=v[396+j:397+j]
    @pl.when(first)
    def _():
        three[0][4].wait()
        load_bias()
        upb[:,half(mp,1536)]=upb_own[...]; upbl[:,half(mp,384)]=upbl_own[...]
    def hook():
        @pl.when(first)
        def _():
            own[2].wait()
            outwl[half(mp,128),:]=jnp.concatenate([outl_own[...],jnp.zeros((32,192),BF)],0)
            upl[:,half(mp,384)]=upl_own[...]
            downl[half(mp,384),:]=downl_own[...]
            for i,cps in enumerate(three):
                for k,cp in enumerate(cps):
                    if (i,k)!=(0,4): cp.wait()
                p=s_ref[2+i]
                base=16+4*i if i<3 else 0
                for j in range(6):
                    down[pl.ds(pl.multiple_of(other*1536+p*384,16),384),128*j:128*j+128]=column(base+j//2)[384*(j%2):384*(j%2)+384].astype(BF)
            unpack_small()
    def both(a,b):
        a=a[...]; b=b[...]
        z=mp==0
        return jnp.concatenate([jnp.where(z,a,b),jnp.where(z,b,a)],1)
    gup=acc.at[:,0:1536]; gdn=acc.at[:,1536:3072]; gout=acc.at[:,3072:3456]
    stream(None,mp*1536,xt[...],both(oa,ob),oa[...],ct[...],outw,up,down,sh,ga,upb,act,gp,to,dr1,dos,gup,gdn,gout,st,bst,first,512,tm[...],hook)
    stream(None,mp*384,xl[...],both(ola,olb),ola[...],cl[...].T,outwl,upl,downl,shl,gal,upbl,actl,gpl,lo,dr1l,dosl,gupl,gdnl,goutl,stl,bstl,first,768,lm[...],None)
    @pl.when(pl.program_id(0)==pl.num_programs(0)-1)
    def _():
        blocks=[gupl[:,128*j:128*j+128] for j in range(3)]+[gdnl[:,128*j:128*j+128] for j in range(3)]+[goutl[...]]
        rest=[st[:,128*j:128*j+128] for j in range(6)]+[bst[:,128*j:128*j+128] for j in range(12)]+[stl[:,0:128]]
        rest+=[jnp.concatenate([stl[:,128:192],jnp.zeros((8,64),F32)],1)]+[bstl[:,128*j:128*j+128] for j in range(3)]+[jnp.zeros((8,128),F32)]
        blocks.append(jnp.concatenate(rest,0))
        for i,v in enumerate(blocks):
            acc[192*(i%4):192*(i%4)+192,3456+128*(i//4):3584+128*(i//4)]=v
        place_blocks(acc,keep,send,sem,s_ref[1],n)


def ffn(n,scal,rowed,params,own,second,third,tile=384):
    rows=rowed[0].shape[0]
    rb=lambda a: pl.BlockSpec((tile,a.shape[1]),lambda p,*_:(p,0))
    full=lambda a: pl.BlockSpec(a.shape,lambda p,*_:(0,)*len(a.shape),pipeline_mode=pl.Buffered(1))
    whole=pl.BlockSpec(memory_space=pl.ANY)
    S=jax.ShapeDtypeStruct
    rowout=[S((rows,768),F32),S((192,rows),F32),S((rows,768),F32),S((rows,192),F32)]
    outspecs=[rb(rowout[0]),pl.BlockSpec((192,tile),lambda p,*_:(0,p)),rb(rowout[2]),rb(rowout[3])]
    dos=[S((2,rows,384),BF),S((2,rows,128),BF)]
    big=block_shapes(768,3712,n)
    V=pltpu.VMEM
    small=[V(a,F32) for a in ((8,768),(8,1536),(192,384),(192,384),(192,128),(8,192),(8,384))]
    weights=[V((768,3072),BF),V((768,768),BF),V((3072,768),BF),V((256,192),BF),V((192,768),BF),V((768,192),BF),V((1,3072),F32),V((1,768),F32)]
    return pl.pallas_call(functools.partial(ffn_kernel,n),
        grid_spec=pltpu.PrefetchScalarGridSpec(num_scalar_prefetch=1,grid=(rows//tile,),
            in_specs=[rb(a) if a.shape[0]==rows else pl.BlockSpec((a.shape[0],tile),lambda p,*_:(0,p)) for a in rowed]+[full(w) for w in params]+[whole]*3+[full(w) for w in own[3:]]+[whole]*16,
            out_specs=outspecs+[pl.BlockSpec((2,tile,a.shape[2]),lambda p,*_:(0,p,0)) for a in dos]+[whole,whole],
            scratch_shapes=[V((tile,3072),BF),V((tile,3072),BF),V((tile,768),BF),V((tile,768),BF),V((768,3712),F32)]+weights+small
                +[pltpu.SemaphoreType.DMA,pltpu.SemaphoreType.DMA((3,)),pltpu.SemaphoreType.DMA((8,2)),pltpu.SemaphoreType.DMA((4,5))]),
        out_shape=rowout+dos+big,
        compiler_params=pltpu.CompilerParams(vmem_limit_bytes=VLIM),cost_estimate=cost(80),name="middle")(scal,*rowed,*params,*own,*second,*[v for pair in third for v in pair])


from jax.sharding import PartitionSpec as P


def pack_kernel(idx_ref, *refs):
    out=refs[-1]
    out[...]=jnp.zeros_like(out)
    r=0
    for src in refs[:-1]:
        lead=src.shape[0] if len(src.shape)==3 else None
        for c in range(lead or 1):
            w=src[c] if lead else src[...]
            n,m=w.shape
            for j in range(0,m,128):
                e=min(128,m-j)
                out[r:r+n,:e]=w[:,j:j+e].astype(F32)
                r+=n


def pack(idx, split, whole, parts, part=(0,1)):
    specs=[]; n=0
    for k,a in enumerate(split):
        rows=a.shape[-2]//parts
        width=a.shape[-1]//(part[1] if k==0 else 1)
        blocks=-(-width//128)
        if a.ndim==3:
            specs.append(pl.BlockSpec((a.shape[0],rows,a.shape[2]),lambda i,s:(0,s[0],0)))
            n+=a.shape[0]*rows*blocks
        else:
            specs.append(pl.BlockSpec((rows,width),functools.partial(lambda c,i,s:(s[0],c),part[0] if k==0 else 0)))
            n+=rows*blocks
    for a in whole:
        specs.append(pl.BlockSpec(a.shape,lambda i,s:(0,0)))
        n+=a.shape[0]*(-(-a.shape[1]//128))
    n=-(-n//8)*8
    return pl.pallas_call(pack_kernel,
        grid_spec=pltpu.PrefetchScalarGridSpec(num_scalar_prefetch=1,grid=(1,),in_specs=specs,
            out_specs=pl.BlockSpec((n,128),lambda i,s:(0,0))),
        out_shape=jax.ShapeDtypeStruct((n,128),F32),
        compiler_params=pltpu.CompilerParams(vmem_limit_bytes=VLIM),cost_estimate=cost(2),name="pack")(idx,*split,*whole)


def unpack_first_kernel(s_ref, pa, pb, pc, pd, wt_own, wl_own, wt, wl, bt, bl):
    mine=s_ref[0]; other=1-mine
    wl[...]=jnp.zeros_like(wl)
    wt[mine]=wt_own[...]
    wl[mine]=wl_own[...]
    bt[...]=jnp.zeros_like(bt); bl[...]=jnp.zeros_like(bl)
    for p,ref in enumerate((pa,pb,pc,pd)):
        i=s_ref[2+p]
        at=lambda n: pl.ds(pl.multiple_of(i*n,n),n)
        r=0
        for c in range(3):
            for j in range(3):
                wt[other,c,at(192),128*j:128*j+128]=ref[r:r+192].astype(BF); r+=192
        for c in range(3):
            wl[other,c,at(48),:]=ref[r:r+48].astype(BF); r+=48
        if p==0:
            for c in range(2):
                for j in range(3):
                    bt[2*c:2*c+1,128*j:128*j+128]=ref[r+2*j+c:r+2*j+c+1]
            r+=6
            for c in range(2):
                bl[2*c:2*c+1,:]=ref[r+c:r+c+1]


def unpack_first(scal, pieces, wt, wl):
    S=jax.ShapeDtypeStruct
    full=lambda a: pl.BlockSpec(a.shape,lambda i,*_:(0,)*len(a.shape))
    outs=[S((2,3,768,384),BF),S((2,3,192,128),BF),S((3,384),F32),S((3,128),F32)]
    ins=[*pieces,wt,wl]
    return pl.pallas_call(unpack_first_kernel,
        grid_spec=pltpu.PrefetchScalarGridSpec(num_scalar_prefetch=1,grid=(1,),in_specs=[full(a) for a in ins],
            out_specs=[full(a) for a in outs]),
        out_shape=outs,compiler_params=pltpu.CompilerParams(vmem_limit_bytes=VLIM),cost_estimate=cost(4),name="unpack")(scal,*ins)


def flip(n, bit):
    return [(i,i^bit) for i in range(n)]


def cross(n, even, odd):
    return [(i,i^(even if i%2==0 else odd)) for i in range(n)]


def gather4(piece, n):
    a=lax.ppermute(piece,"mp",[(0,1),(1,0)])
    b=lax.ppermute(a,"dp",cross(n,2,4))
    c=lax.ppermute(a,"dp",flip(n,1))
    d=lax.ppermute(b,"dp",flip(n,1))
    return a,b,c,d


def gather8(piece, n):
    a=lax.ppermute(piece,"mp",[(0,1),(1,0)])
    b=lax.ppermute(a,"dp",cross(n,2,4))
    e=lax.ppermute(a,"dp",cross(n,4,2))
    f=lax.ppermute(b,"dp",cross(n,4,2))
    return (a,b,e,f)+tuple(lax.ppermute(v,"dp",flip(n,1)) for v in (a,b,e,f))


def ids8(dp):
    base=dp&7; odd=dp&1
    near=jnp.where(odd==0,2,4); far=6-near
    return [base,base^near,base^far,base^6,base^1,base^1^far,base^1^near,base^7]


def join(*values):
    return lax.optimization_barrier(values)


def stages(n):
    return (flip(n,1),cross(n,2,4),cross(n,4,2),flip(n,8))


def halve(keep, recv):
    half=keep.shape[0]//2
    return keep[:half]+recv[:half],keep[half:]+recv[half:]


def bias_rows(pair):
    b=pair.astype(F32)
    return jnp.stack([b[0],jnp.zeros_like(b[0]),b[1]])


def shards(text_in, layout_in, token_mask, box_mask, lengths, text_mask_vec, layout_mask_vec,
           text_qkv, text_qv_bias, text_out_w, text_shifts, text_gains, text_up, text_up_bias, text_down,
           layout_qkv, layout_qv_bias, layout_out_w, layout_shifts, layout_gains, layout_up, layout_up_bias, layout_down,
           text_cot, layout_cot):
    n=lax.axis_size("dp")
    mp=lax.axis_index("mp").astype(jnp.int32); dp=lax.axis_index("dp").astype(jnp.int32)
    core=dp&1; color=((dp>>1)^(dp>>2))&1
    ids=[2*color+core,2*(1-color)+core,2*color+1-core,2*(1-color)+1-core]
    scal=jnp.stack([mp,dp]+ids+ids8(dp))
    idx=ids[0][None]; idx8=(dp&7)[None]
    even_odd=cross(n,2,4); odd_even=cross(n,4,2); core_flip=flip(n,1)
    over=lambda v: lax.ppermute(v,"mp",[(0,1),(1,0)])
    send=lambda v,pairs: lax.ppermute(v,"dp",pairs)
    upb=text_up_bias.astype(F32)[None]; upbl=layout_up_bias.astype(F32)[None]
    p1=pack(idx,[text_qkv,layout_qkv],[text_qv_bias,layout_qv_bias],4)
    p2=pack(idx8,[text_up,text_out_w],[],8)
    p3=pack(idx,[text_down],[],4,(0,2))
    p4=pack(idx,[text_down,layout_out_w,layout_up,layout_down],[upb,upbl],4,(1,2))
    tm=token_mask[:,None]; lm=box_mask[:,None]
    xt=jnp.where(tm==1,text_mask_vec[None],text_in)
    xl=jnp.where(lm==1,layout_mask_vec[None],layout_in)
    sel=jnp.concatenate([jnp.ones_like(token_mask)[None],(token_mask==1).astype(jnp.int32)[None],(box_mask==1).astype(jnp.int32)[None],
        jnp.zeros((5,token_mask.shape[0]),jnp.int32)],0).astype(BF)
    pad=lambda v: jnp.pad(v,((0,0),)*(v.ndim-1)+((0,32),))
    wl=pad(layout_qkv)
    a1=over(p1); a2=over(p2)
    bt=bias_rows(text_qv_bias); bl=pad(bias_rows(layout_qv_bias))
    pages=lengths.shape[0]
    xa,p3,tm,lm,sel=join(xt,p3,tm,lm,sel)
    forward=lambda first,count,x,w,prev: attn_fwd(first,count,lengths,1-mp[None],x,xl,*w,prev)
    w_own=(text_qkv,wl,bt,bl)
    own=forward(0,1,xa,w_own,())
    own,a1,p3=join(own,a1,p3)
    b1=send(a1,even_odd); c1=send(a1,core_flip); a3=over(p3)
    own=forward(1,pages-1,xt,w_own,own)
    own,b1,c1,a2,p4=join(own,b1,c1,a2,p4)
    d1=send(b1,core_flip); b2=send(a2,even_odd); a4=over(p4)
    wt_both,wl_both,bt_o,bl_o=unpack_first(scal,(a1,b1,c1,d1),text_qkv,wl)
    wt_both,wl_both,bt_o,bl_o,a2=join(wt_both,wl_both,bt_o,bl_o,a2)
    e2=send(a2,odd_even)
    w_oth=(wt_both,wl_both,bt_o,bl_o)
    oth=forward(0,1,xt,w_oth,())
    oth,b2,e2,a3=join(oth,b2,e2,a3)
    f2=send(b2,odd_even); b3=send(a3,even_odd); c3=send(a3,core_flip)
    oth=forward(1,pages-1,xt,w_oth,oth)
    oth,f2,b3,c3,a4=join(oth,f2,b3,c3,a4)
    b4=send(a4,even_odd); c4=send(a4,core_flip)
    second=(a2,b2,e2,f2)+tuple(send(v,core_flip) for v in (a2,b2,e2,f2))
    d3=send(b3,core_flip); d4=send(b4,core_flip)
    (to,lo,dr1,dr1l,dO,dOl,keep,out)=ffn(n,scal,[xt,xl,own[6],oth[6],own[7],oth[7],text_cot,layout_cot.T,tm,lm],
        [v.astype(F32) for v in (text_shifts,text_gains,layout_shifts,layout_gains)],
        [text_up,text_out_w,text_down,layout_out_w,layout_up,layout_down,upb,upbl],second,((a3,a4),(b3,b4),(c3,c4),(d3,d4)))
    steps=stages(n)
    wts=[wt_both,wl_both]
    tile=text_in.shape[0]//4
    mine_p=lambda p,c,d: attn_bwd(p,c,lengths,mp[None],own,dO,dOl,d)
    other_p=lambda p,d: attn_bwd(p,1,lengths,1-mp[None],oth,dO,dOl,d)
    sums=lambda d: qkv_grad(n,jnp.stack([mp,dp]),pages,xt,xl,*d,sel,*wts)
    inputs=lambda d: input_grad(tile,d,wts,dr1,dr1l,tm,lm)
    if n==16:
        out=send(out,steps[0])
        d_own=mine_p(0,1,())
        d_own,out,keep=join(d_own,out,keep)
        keep,out=halve(keep,out)
        out=send(out,steps[1])
        d_own=mine_p(1,pages-1,d_own)
        qkeep,qout=sums(d_own)
        qkeep,qout,keep,out=join(qkeep,qout,keep,out)
        qout=send(qout,steps[0])
        keep,out=halve(keep,out)
        out=send(out,steps[2])
        d_oth=other_p(0,d_own)
        d_oth,qkeep,qout,keep,out=join(d_oth,qkeep,qout,keep,out)
        keep,out=halve(keep,out)
        qkeep,qout=halve(qkeep,qout)
        half=keep.shape[0]//2
        outs=[send(out[:half],steps[3]),out[half:]]
        qout=send(qout,steps[1])
        d_oth=other_p(1,d_oth)
        d_oth,qkeep,qout,outs[0],outs[1]=join(d_oth,qkeep,qout,*outs)
        outs[1]=send(outs[1],steps[3])
        qkeep,qout=halve(qkeep,qout)
        qout=send(qout,steps[2])
        d_oth=other_p(2,d_oth)
        d_oth,qkeep,qout,outs[1]=join(d_oth,qkeep,qout,outs[1])
        qkeep,qout=halve(qkeep,qout)
        qout=send(qout,steps[3])
        g=keep+jnp.concatenate(outs,0)
        d_in=inputs(d_oth)
        d_in,qkeep,qout=join(d_in,qkeep,qout)
        qg=qkeep+qout
        small=jnp.concatenate([g[:,3456:],qg[:,1152:]],1)[None]
        for bit in (8,2,4,1):
            got=send(small,flip(n,bit))
            low=(dp&bit)==0
            small=jnp.stack([jnp.where(low,small,got),jnp.where(low,got,small)])
        small=small.reshape(2,2,2,2,-1,384).transpose(3,1,2,0,4,5).reshape(-1,384)
    else:
        d_own=mine_p(0,pages,())
        qkeep,qout=sums(d_own)
        rs=lambda v: lax.psum_scatter(v,"dp",scatter_dimension=0,tiled=True)
        g=rs(keep); qg=rs(qkeep)
        d_oth=d_own
        for p in range(pages): d_oth=other_p(p,d_oth)
        d_in=inputs(d_oth)
        small=lax.all_gather(jnp.concatenate([g[:,3456:],qg[:,1152:]],1),"dp",tiled=True)
    tg,lg=d_in
    r=g.shape[0]
    early=small[:,:256]; mine=small[:,256:]
    block=lambda i: early[192*(i%4):192*(i%4)+192,128*(i//4):128*(i//4)+128]
    wide=lambda v,r,k: jnp.concatenate([v[r+8*j:r+8*j+8] for j in range(k)],1)
    gupl=jnp.concatenate([block(j) for j in range(3)],1); gdnl=jnp.concatenate([block(3+j) for j in range(3)],1)
    rest=block(7)
    st=wide(rest,0,6); bst=wide(rest,48,12); stl=wide(rest,144,2)[:,:192]; bstl=wide(rest,160,3)
    sums=mine[576:]
    cs=jnp.stack([wide(sums,32*c,3)[0] for c in (0,2)]); csl=jnp.stack([sums[32*c+24,:96] for c in (0,2)])
    vec=jnp.concatenate([wide(sums,96,6)[1],wide(sums,144,2)[2,:192]])[None]
    vec=vec+over(vec)
    tvec=vec[0,:768]+st[6]; lvec=vec[0,768:]+stl[6]
    qgl=jnp.stack([mine[192*c:192*c+192,:96] for c in range(3)])
    qg=jnp.moveaxis(qg[:,:1152].reshape(r,3,384),1,0)
    return (to,lo.T,tg,lg.T,tvec,lvec,qg,cs,g[:,3072:3456].T,st[:4],st[4:6],g[:,:1536],bst[0],g[:,1536:3072].T,
            qgl,csl,block(6)[:,:96].T,stl[:4],stl[4:6],gupl,bstl[0],gdnl.T)


def solution(mesh):
    rows=P("dp",None); cols=P(None,"mp"); lead=P("mp",None); cube=P(None,None,"mp")
    weights=(cube,cols,lead,P(),P(),cols,P("mp"),lead)
    return jax.shard_map(shards,mesh=mesh,
        in_specs=(rows,rows,P("dp"),P("dp"),P("dp"),P(),P())+weights+weights+(rows,rows),
        out_specs=(rows,rows,rows,rows,P(),P(),P(None,"dp","mp"),cols,P("mp","dp"),P(),P(),P("dp","mp"),P("mp"),P("mp","dp"),
                   cube,cols,lead,P(),P(),cols,P("mp"),lead),
        check_vma=False)
```

```python
import functools
import jax, jax.numpy as jnp
from jax import lax
from jax.experimental import pallas as pl
from jax.experimental.pallas import tpu as pltpu
F32=jnp.float32; BF=jnp.bfloat16
NT=(((1,),(1,)),((),()))
TN=(((0,),(0,)),((),()))
def dot(a,b): return jnp.dot(a,b,preferred_element_type=F32)
def dotg(a,b,dn): return lax.dot_general(a,b,dn,preferred_element_type=F32)
VLIM=60*1024*1024

def cost(us): return pl.CostEstimate(flops=int(us*1e7),bytes_accessed=1024,transcendentals=0)

def lane_iota(shape): return lax.broadcasted_iota(jnp.int32,shape,len(shape)-1)

def row_masks():
    i=lax.broadcasted_iota(jnp.int32,(1,128),1)
    return lambda f: jnp.where(f(i),1.0,0.0).astype(BF)


def attn_fwd_kernel(first, len_ref, half_ref, xt_ref, xl_ref, wt_ref, wl_ref, bt_ref, bl_ref, *rest):
    qt_ref, kt_ref, vt_ref, ql_ref, kl_ref, vl_ref, ot_ref, ol_ref, lse_ref, olT, lseT=rest[-11:]
    page=first+pl.program_id(0)
    seq=xt_ref.shape[0]
    xt=xt_ref[...]; xl=xl_ref[...]
    for c,(t,l) in enumerate(((qt_ref,ql_ref),(kt_ref,kl_ref),(vt_ref,vl_ref))):
        t[...]=(dot(xt,wt_ref[c])+bt_ref[c:c+1,:]).astype(BF)
        l[...]=(dot(xl,wl_ref[c])+bl_ref[c:c+1,:]).astype(BF)
    lane=lane_iota((seq,128))
    row=lax.broadcasted_iota(jnp.int32,(seq,128),0)
    length=len_ref[page]
    bias=jnp.where(row<length,0.0,-1e9).astype(BF)
    one=jnp.ones((seq,128),BF)
    ql=jnp.where(lane==96,one,ql_ref[...]*BF(0.25))
    kl=jnp.where(lane==96,bias,kl_ref[...])
    vlT=vl_ref[...].T; qlT=ql.T
    keep=row_masks()
    olT[...]=jnp.zeros_like(olT); lseT[...]=jnp.zeros_like(lseT)
    def scores(h):
        j,s=h//2,h%2
        cols=slice(128*j,128*j+128)
        qbig=jnp.concatenate([(qt_ref[:,cols]*BF(0.125)).T,qlT],0)
        kbig=jnp.concatenate([kt_ref[:,cols]*keep(lambda i: i//64==s),kl*keep(lambda i: (i//16==h)|(i==96))],1)
        return dot(kbig,qbig)
    halves=[]
    def finish(h,e,m,ssum):
        j,s=h//2,h%2
        vT=vt_ref[:,128*j:128*j+128].T
        v80=jnp.concatenate([vT[64*s:64*s+64],vlT[16*h:16*h+16]],0)
        o=dot(v80,e)*(1.0/ssum)
        halves.append(o[:64])
        olT[16*h:16*h+16,:]=o[64:]
        lseT[h:h+1,:]=m+jnp.log(ssum)
        if s==1: ot_ref[:,128*j:128*j+128]=jnp.concatenate(halves[-2:],0).T.astype(BF)
    ahead=scores(0); behind=None
    for h in range(6):
        S=ahead
        if h<5: ahead=scores(h+1)
        if behind is not None: finish(*behind)
        m=jnp.max(S,0,keepdims=True)
        e=jnp.exp(S-m)
        behind=(h,e.astype(BF),m,jnp.sum(e,0,keepdims=True))
    finish(*behind)
    ol_ref[...]=olT[...].T.astype(BF)
    lse_ref[...]=pltpu.roll(lseT[...].T,97,1)

def attn_fwd(first, count, lengths, half, xt, xl, wt, wl, bt, bl, prev):
    rows=xt.shape[0]; pages=lengths.shape[0]; seq=rows//pages
    rb=lambda n: pl.BlockSpec((seq,n),lambda p,*_:(first+p,0))
    full=lambda a: pl.BlockSpec((None,)*(a.ndim-3)+a.shape[-3:],lambda p,l,h:(h[0],0,0,0)[4-a.ndim:]) if a.ndim>2 else pl.BlockSpec(a.shape,lambda p,*_:(0,0))
    whole=pl.BlockSpec(memory_space=pl.ANY)
    o=lambda n,d=BF: jax.ShapeDtypeStruct((rows,n),d)
    return pl.pallas_call(functools.partial(attn_fwd_kernel,first),
        grid_spec=pltpu.PrefetchScalarGridSpec(num_scalar_prefetch=2,grid=(count,),
            in_specs=[rb(768),rb(192),full(wt),full(wl),full(bt),full(bl)]+[whole]*len(prev),
            out_specs=[rb(384)]*3+[rb(128)]*3+[rb(384),rb(128),rb(128)],
            scratch_shapes=[pltpu.VMEM((128,seq),F32),pltpu.VMEM((128,seq),F32)]),
        out_shape=[o(384)]*3+[o(128)]*3+[o(384),o(128),o(128,F32)],
        input_output_aliases={8+i:i for i in range(len(prev))},
        compiler_params=pltpu.CompilerParams(vmem_limit_bytes=VLIM),cost_estimate=cost(6.2*count),name="attn_fwd")(lengths,half,xt,xl,wt,wl,bt,bl,*prev)

def ind_matrix(j):
    r=lax.broadcasted_iota(jnp.int32,(256,128),0)%128
    l=lax.broadcasted_iota(jnp.int32,(256,128),1)
    h=(r//64+2*j) if j is not None else r//16
    return jnp.where((l==97+h)&(h<6),1.0,0.0).astype(BF)

def split2(v):
    hi=v.astype(BF)
    return hi,(v-hi.astype(F32)).astype(BF)

def bwd_page(length, qt_ref, kt_ref, vt_ref, ql_ref, kl_ref, vl_ref, ot_ref, ol_ref, lse_ref, dot_ref, dol_ref,
                    dpt_ref, dpl_ref, dqlT, lay):
    seq=qt_ref.shape[0]
    lane=lane_iota((seq,128))
    row=lax.broadcasted_iota(jnp.int32,(seq,128),0)
    bias=jnp.where(row<length,0.0,-1e9).astype(BF)
    zero=jnp.zeros((seq,128),BF); one=jnp.ones((seq,128),BF)
    nl=-lse_ref[...]
    hi=nl.astype(BF); r1=nl-hi.astype(F32); mid=r1.astype(BF); lo=r1-mid.astype(F32)
    ext=hi+pltpu.roll(mid.astype(F32),7,1).astype(BF)+pltpu.roll(lo,14,1).astype(BF)
    qle=jnp.where(lane<96,ql_ref[...]*BF(0.25),jnp.where(lane==96,one,ext))
    kl=kl_ref[...]; vl=vl_ref[...]; ql=ql_ref[...]
    klT=kl.T
    dqlT[...]=jnp.zeros_like(dqlT)
    def sums(a,b,m):
        p=a.astype(F32)*b.astype(F32)
        h_,l_=split2(p)
        return dot(jnp.concatenate([h_,l_],1),m)
    dol=dol_ref[...]
    d_l=sums(dol,ol_ref[...],ind_matrix(None))
    d_t=d_l
    for j in range(3):
        cols=slice(128*j,128*j+128)
        d_t=d_t+sums(dot_ref[:,cols],ot_ref[:,cols],ind_matrix(j))
    def ext_delta(d):
        h_=d.astype(BF); l_=d-h_.astype(F32)
        return h_+pltpu.roll(l_,7,1).astype(BF)
    dol1=jnp.where(lane<96,dol*BF(0.125),ext_delta(d_t*-0.125))
    dol2=jnp.where(lane<96,dol*BF(0.25),ext_delta(d_l*-0.25))
    keep=row_masks()
    kle=jnp.where(lane==96,bias,jnp.where(lane>96,one,kl))
    vle=jnp.where(lane>96,one,vl)
    qleT=qle.T; dol1T=dol1.T; dol2T=dol2.T
    rows2=lambda x,masks: jnp.concatenate([x*m for m in masks],0)
    for j in range(3):
        cols=slice(128*j,128*j+128)
        qt=qt_ref[:,cols]; kt=kt_ref[:,cols]; vt=vt_ref[:,cols]; dO=dot_ref[:,cols]
        qbig=jnp.concatenate([(qt*BF(0.125)).T,qleT],0)
        dbig=jnp.concatenate([(dO*BF(0.125)).T,dol1T],0)
        ktT=kt.T
        heads=(2*j,2*j+1)
        tms=[keep(lambda i: i//64==s) for s in range(2)]
        lms=[keep(lambda i: i//16==h) for h in heads]
        R1s=[]; R2s=[]; Ps=[]; dqs=[]
        for s,h in enumerate(heads):
            kbig=jnp.concatenate([kt*tms[s],kle*keep(lambda i: (i//16==h)|(i==96)|(i==97+h)|(i==104+h)|(i==111+h))],1)
            vleh=vle*keep(lambda i: (i//16==h)|(i==97+h)|(i==104+h))
            vbig=jnp.concatenate([vt*tms[s],vleh],1)
            S=dot(kbig,qbig)
            M1=dot(vbig,dbig)
            M2=dot(vleh,dol2T)
            Pm=jnp.exp(S)
            R1=(Pm*M1).astype(BF); R2=(Pm*M2).astype(BF)
            Ps.append(Pm.astype(BF)); R1s.append(R1); R2s.append(R2)
            dqs.append(dot(ktT[64*s:64*s+64],R1))
            dqlT[16*h:16*h+16,:]=dot(klT[16*h:16*h+16],R2)
        dpt_ref[0,:,cols]=jnp.concatenate(dqs,0).T.astype(BF)
        dpt_ref[1,:,cols]=dot(jnp.concatenate(R1s,1),rows2(qt,tms)).astype(BF)
        dv=dot(jnp.concatenate(Ps,1),jnp.concatenate([rows2(dO,tms),rows2(dol,lms)],1))
        dpt_ref[2,:,cols]=dv[:,:128].astype(BF)
        dkl=dot(jnp.concatenate(R2s,1),rows2(ql,lms))
        if j==0: lay[0]=dkl; lay[1]=dv[:,128:]
        else: lay[0]+=dkl; lay[1]+=dv[:,128:]
    dpl_ref[0]=dqlT[...].T.astype(BF)
    dpl_ref[1]=lay[0].astype(BF); dpl_ref[2]=lay[1].astype(BF)


def bwd_kernel(first, len_ref, half_ref, qt, kt, vt, ql, kl, vl, ot, ol, lse, dO, dOl, *rest):
    dpt,dpl,dqlT,lay=rest[-4:]
    bwd_page(len_ref[first+pl.program_id(0)],qt,kt,vt,ql,kl,vl,ot,ol,lse,dO.at[0],dOl.at[0],dpt,dpl,dqlT,lay)


def attn_bwd(first,count,lengths,half,saved,dO,dOl,prev):
    rows=saved[0].shape[0]; seq=rows//lengths.shape[0]
    rb=lambda n: pl.BlockSpec((seq,n),lambda i,*_:(first+i,0))
    hb=lambda n: pl.BlockSpec((1,seq,n),lambda i,l,h:(h[0],first+i,0))
    pb=lambda n: pl.BlockSpec((3,seq,n),lambda i,l,h:(h[0],first+i,0))
    whole=pl.BlockSpec(memory_space=pl.ANY)
    return pl.pallas_call(functools.partial(bwd_kernel,first),
        grid_spec=pltpu.PrefetchScalarGridSpec(num_scalar_prefetch=2,grid=(count,),
            in_specs=[rb(384)]*3+[rb(128)]*3+[rb(384),rb(128),rb(128),hb(384),hb(128)]+[whole]*len(prev),
            out_specs=[pb(384),pb(128)],scratch_shapes=[pltpu.VMEM((128,seq),F32),pltpu.VMEM((2,seq,128),F32)]),
        out_shape=[jax.ShapeDtypeStruct((6,rows,384),BF),jax.ShapeDtypeStruct((6,rows,128),BF)],
        input_output_aliases={13+i:i for i in range(len(prev))},
        compiler_params=pltpu.CompilerParams(vmem_limit_bytes=VLIM),cost_estimate=cost(9*count),name="attn_bwd")(lengths,half,*saved,dO,dOl,*prev)


def dx_kernel(dpt, dpl, wt, wl, dr1, dr1l, sel, dx, dxl, wts, wls):
    @pl.when(pl.program_id(0)==0)
    def _():
        for h in range(2):
            for c in range(3):
                i=3*h+c
                wts[:,384*i:384*i+384]=wt[h,c]
                wls[:,128*i:128*i+128]=wl[h,c]
    def back(d,w,base,flag):
        v=dotg(jnp.concatenate([d[i] for i in range(6)],1),w[...],NT)+base[...]
        return jnp.where(flag>0.5,0.0,v)
    flags=sel[...].astype(F32).T
    dx[...]=back(dpt,wts,dr1,flags[:,1:2])
    dxl[...]=back(dpl,wls,dr1l,flags[:,2:3]).T


def input_grad(tile,dp,wts,dr1,dr1l,sel):
    rows=dr1.shape[0]
    rb=lambda n: pl.BlockSpec((tile,n),lambda i:(i,0))
    pb=lambda n: pl.BlockSpec((6,tile,n),lambda i:(0,i,0))
    full=lambda a: pl.BlockSpec(a.shape,lambda i:(0,0,0,0))
    return pl.pallas_call(dx_kernel,grid=(rows//tile,),
        in_specs=[pb(384),pb(128)]+[full(w) for w in wts]+[rb(768),rb(192),pl.BlockSpec((8,tile),lambda i:(0,i))],
        out_specs=[rb(768),pl.BlockSpec((192,tile),lambda i:(0,i))],
        scratch_shapes=[pltpu.VMEM((768,2304),BF),pltpu.VMEM((192,768),BF)],
        out_shape=[jax.ShapeDtypeStruct((rows,768),F32),jax.ShapeDtypeStruct((192,rows),F32)],
        compiler_params=pltpu.CompilerParams(vmem_limit_bytes=VLIM),cost_estimate=cost(5),name="input_grad")(*dp,*wts,dr1,dr1l,sel)


def place_blocks(acc, keep, send, sem, position, n):
    if n!=16:
        cp=pltpu.make_async_copy(acc,keep,sem); cp.start(); cp.wait()
        return
    c=position&1; x=(position>>1)&1; z0=(position>>2)&1; z1=(position>>3)&1
    rows=acc.shape[0]//16
    copies=[]
    for out,core in ((keep,c),(send,1-c)):
        for q in range(8):
            r2,r3,r4=q>>2,(q>>1)&1,q&1
            fx=jnp.where(core==0,r2,r3); fz=jnp.where(core==0,r3,r2)
            block=(z1^r4)*8+(z0^fz)*4+(x^fx)*2+core
            copies.append(pltpu.make_async_copy(acc.at[pl.ds(pl.multiple_of(block*rows,8),rows)],out.at[pl.ds(q*rows,rows)],sem))
    for cp in copies: cp.start()
    for cp in copies: cp.wait()


def block_shapes(rows,cols,n):
    S=jax.ShapeDtypeStruct
    if n!=16: return [S((rows,cols),F32),S((8,128),F32)]
    return [S((rows//2,cols),F32)]*2


def qkv_grad_kernel(n, pos_ref, xt, xl, dpt, dpl, sel, wt, wl, st, bst, extra, keep, send, acc, sums, suml, sem):
    x=xt[...]; s=sel[...]; xv=xl[...]
    def add(first):
        def put(ref,v):
            if first: ref[...]=v
            else: ref[...]+=v
        cat=lambda d: jnp.concatenate([d[0],d[1],d[2]],1)
        t=cat(dpt); l=cat(dpl)
        put(acc.at[:,:1152],dotg(x,t,TN))
        g=dotg(xv,l,TN); a=dot(s,t); b=dot(s,l)
        for c in range(3):
            put(acc.at[192*c:192*c+192,1152:1280],g[:,128*c:128*c+128])
            put(sums.at[c],a[:,384*c:384*c+384]); put(suml.at[c],b[:,128*c:128*c+128])
    first=pl.program_id(0)==0
    pl.when(first)(lambda: add(True))
    pl.when(jnp.logical_not(first))(lambda: add(False))
    @pl.when(pl.program_id(0)==pl.num_programs(0)-1)
    def _():
        t=jnp.zeros((8,768),F32); l=jnp.zeros((8,192),F32)
        for c in range(3):
            for v,w,text in ((sums[c],wt,True),(suml[c],wl,False)):
                hi,lo=split2(v)
                lo2=(v-hi.astype(F32)-lo.astype(F32)).astype(BF)
                y=dotg(jnp.concatenate([hi,lo,lo2],0),w[0,c],NT)
                y=y[0:8]+y[8:16]+y[16:24]
                if text: t=t+y
                else: l=l+y
        acc[576:768,1152:1280]=jnp.zeros((192,128),F32)
        rows=[st[i:i+1,128*j:128*j+128] for i in range(7) for j in range(6)]+[bst[0:1,128*j:128*j+128] for j in range(12)]
        rows+=[sums[c][0:1,128*j:128*j+128] for c in (0,2) for j in range(3)]+[suml[c][0:1] for c in (0,2)]
        rows+=[t[1:2,128*j:128*j+128] for j in range(6)]+[l[2:3,0:128],jnp.concatenate([l[2:3,128:],jnp.zeros((1,64),F32)],1)]
        for i,v in enumerate(rows): acc[576+i:577+i,1152:1280]=v
        acc[:,1280:]=extra[...]
        place_blocks(acc,keep,send,sem,pos_ref[1],n)


def qkv_grad(n,pos,pages,xt,xl,dpt,dpl,sel,wt,wl,st,bst,extra):
    seq=xt.shape[0]//pages
    rb=lambda m: pl.BlockSpec((seq,m),lambda i,s:(i,0))
    pb=lambda m: pl.BlockSpec((3,seq,m),lambda i,s:(s[0],i,0))
    wb=lambda a: pl.BlockSpec((1,)+a.shape[1:],lambda i,s:(s[0],0,0,0))
    whole=pl.BlockSpec(memory_space=pl.ANY)
    return pl.pallas_call(functools.partial(qkv_grad_kernel,n),
        grid_spec=pltpu.PrefetchScalarGridSpec(num_scalar_prefetch=1,grid=(pages,),
            in_specs=[rb(768),rb(192),pb(384),pb(128),pl.BlockSpec((8,seq),lambda i,s:(0,i)),wb(wt),wb(wl)]+[pl.BlockSpec(a.shape,lambda i,s:(0,0)) for a in (st,bst,extra)],
            out_specs=[whole,whole],
            scratch_shapes=[pltpu.VMEM((768,1536),F32),pltpu.VMEM((3,8,384),F32),pltpu.VMEM((3,8,128),F32),pltpu.SemaphoreType.DMA]),
        out_shape=block_shapes(768,1536,n),
        compiler_params=pltpu.CompilerParams(vmem_limit_bytes=VLIM),cost_estimate=cost(8),name="qkv_grad")(pos,xt,xl,dpt,dpl,sel,wt,wl,st,bst,extra)


EPS=1e-5
def gelu_parts(x):
    cdf=0.5+0.5*lax.erf(x*0.7071067811865476)
    phi=jnp.exp2(x*x*-0.7213475204444817-1.3257480647361593)
    return cdf, cdf+x*phi

def norm(v):
    mu=jnp.mean(v,-1,keepdims=True)
    c=v-mu
    inv=lax.rsqrt(jnp.mean(c*c,-1,keepdims=True)+EPS)
    return c*inv,inv

def norm_back(g,u,inv,gain):
    s=g*gain
    return inv*(s-jnp.mean(s,-1,keepdims=True)-u*jnp.mean(s*u,-1,keepdims=True))

def stream(own_off, x, o, o_own, cot, outw, up, down, shift, gain, upb, act, gp, out_ref, dr1_ref, dos, gup, gdn, gout, stat, bstat, chunk, flag):
    d=x.shape[1]; F=up.shape[1]; half=F//2
    h1u,i1=norm(x.astype(F32)+dot(o,outw[...])+shift[2:3])
    h1=h1u*gain[0:1]+shift[0:1]
    h1b=h1.astype(BF)
    for f in range(0,F,chunk):
        cs=slice(f,f+chunk)
        pre=dot(h1b,up[:,cs])+upb[:,cs]
        cdf,der=gelu_parts(pre)
        act[:,cs]=(pre*cdf).astype(BF)
        gp[:,cs]=der.astype(BF)
    yield
    r2=h1+dot(act[...],down[...])+shift[3:4]
    u2,i2=norm(r2)
    y=u2*gain[1:2]+shift[1:2]
    out_ref[...]=y if out_ref.shape==y.shape else y.T
    g=cot.astype(F32)
    dr2=norm_back(g,u2,i2,gain[1:2])
    dr2b=dr2.astype(BF)
    for f in range(0,F,chunk):
        cs=slice(f,f+chunk)
        da=dotg(dr2b,down[cs,:],NT)
        gp[:,cs]=(da*gp[:,cs].astype(F32)).astype(BF)
    dh1=dotg(gp[...],up[...],NT)+dr2
    dr1=norm_back(dh1,h1u,i1,gain[0:1])
    dr1_ref[...]=dr1
    dr1b=dr1.astype(BF)
    dO=dotg(dr1b,outw[...],NT).astype(BF)
    w=dO.shape[1]//2
    dos[0]=dO[:,:w]; dos[1]=dO[:,w:]
    osl=pl.ds(pl.multiple_of(own_off,128),half)
    dpo=gp[:,osl]
    rs=lambda v: jnp.sum(v,0,keepdims=True)
    stat[...]+=jnp.concatenate([rs(dh1),rs(g),rs(dr1),rs(dr2),rs(dh1*h1u),rs(g*u2),rs(jnp.where(flag>0.5,dr1,0.0)),jnp.zeros((1,d),F32)],0)
    bstat[...]+=dot(jnp.ones((8,x.shape[0]),BF),dpo)
    gup[...]+=dotg(h1b,dpo,TN)
    gdn[...]+=dotg(dr2b,act[:,osl],TN)
    gout[...]+=dotg(dr1b,o_own,TN)
    yield


def halves_of(mp, a, b):
    a=a[...]; b=b[...]
    z=mp==0
    return jnp.concatenate([jnp.where(z,a,b),jnp.where(z,b,a)],1)


def half(k, m): return pl.ds(pl.multiple_of(k*m,m),m)


def side_kernel(s_ref, xl, ola, olb, cl, lm, little, shl, gal, outl_own, upl_own, downl_own, upbl_own, pa, pb, pc, pd,
                lo, dr1l, dosl, extra, actl, gpl, outwl, upl, downl, upbl, gupl, gdnl, goutl, stl, bstl, outs):
    mp=s_ref[0]; other=1-mp
    @pl.when(pl.program_id(0)==0)
    def _():
        upbl[:,half(mp,384)]=upbl_own[...]
        upl[:,half(mp,384)]=upl_own[...]
        downl[half(mp,384),:]=downl_own[...]
        outwl[half(mp,128),:]=jnp.concatenate([outl_own[...],jnp.zeros((32,192),BF)],0)
        outs[...]=jnp.zeros_like(outs)
        for i,v in enumerate((pa,pb,pc,pd)):
            p=s_ref[2+i]
            rows=pl.ds(pl.multiple_of(p*24,8),24)
            outs[rows,0:128]=v[0:24]; outs[rows,128:192]=v[24:48,0:64]
            for j in range(3):
                upl[half(p,48),pl.ds(pl.multiple_of(other*384+128*j,128),128)]=v[48+48*j:96+48*j].astype(BF)
            rows=pl.ds(pl.multiple_of(other*384+p*96,16),96)
            downl[rows,0:128]=v[192:288].astype(BF)
            downl[rows,128:192]=v[288:384,0:64].astype(BF)
        outwl[half(other,128),:]=outs[...].astype(BF)
        for j in range(3):
            upbl[:,pl.ds(pl.multiple_of(other*384+128*j,128),128)]=little[12+j:13+j]
        for ref in (gupl,gdnl,goutl,stl,bstl): ref[...]=jnp.zeros_like(ref)
    phases=stream(mp*384,xl[...],halves_of(mp,ola,olb),ola[...],cl[...].T,outwl,upl,downl,shl,gal,upbl,actl,gpl,lo,dr1l,dosl,gupl,gdnl,goutl,stl,bstl,768,lm[...].astype(F32).T[:,2:3])
    next(phases); next(phases)
    @pl.when(pl.program_id(0)==pl.num_programs(0)-1)
    def _():
        blocks=[gupl[:,128*j:128*j+128] for j in range(3)]+[gdnl[:,128*j:128*j+128] for j in range(3)]+[goutl[...]]
        rest=[stl[:,0:128],jnp.concatenate([stl[:,128:192],jnp.zeros((8,64),F32)],1)]
        rest+=[bstl[:,128*j:128*j+128] for j in range(3)]+[jnp.zeros((152,128),F32)]
        blocks.append(jnp.concatenate(rest,0))
        for i,v in enumerate(blocks):
            extra[192*(i%4):192*(i%4)+192,128*(i//4):128*(i//4)+128]=v


def side(scal,xl,ola,olb,cl,lm,little,params,own,pieces,tile=768):
    rows=xl.shape[0]
    rb=lambda n: pl.BlockSpec((tile,n),lambda p,*_:(p,0))
    cb=pl.BlockSpec((192,tile),lambda p,*_:(0,p))
    full=lambda a: pl.BlockSpec(a.shape,lambda p,*_:(0,)*len(a.shape))
    S=jax.ShapeDtypeStruct; V=pltpu.VMEM
    last=pl.BlockSpec((400,128),lambda p,*_:(0,0))
    return pl.pallas_call(side_kernel,
        grid_spec=pltpu.PrefetchScalarGridSpec(num_scalar_prefetch=1,grid=(rows//tile,),
            in_specs=[rb(192),rb(128),rb(128),cb,pl.BlockSpec((8,tile),lambda p,*_:(0,p)),pl.BlockSpec((16,128),lambda p,*_:(90,0))]+[full(a) for a in params+own]+[last]*4,
            out_specs=[cb,rb(192),pl.BlockSpec((2,tile,128),lambda p,*_:(0,p,0)),pl.BlockSpec((768,256),lambda p,*_:(0,0))],
            scratch_shapes=[V((tile,768),BF),V((tile,768),BF),V((256,192),BF),V((192,768),BF),V((768,192),BF),V((1,768),F32),
                V((192,384),F32),V((192,384),F32),V((192,128),F32),V((8,192),F32),V((8,384),F32),V((128,192),F32)]),
        out_shape=[S((192,rows),F32),S((rows,192),F32),S((2,rows,128),BF),S((768,256),F32)],
        compiler_params=pltpu.CompilerParams(vmem_limit_bytes=VLIM),cost_estimate=cost(10),name="side")(scal,xl,ola,olb,cl,lm,little,*params,*own,*pieces)


def ffn_kernel(n, s_ref, *refs):
    (xt, oa, ob, ct, tm, sh, ga, upb_own)=refs[:8]
    (up_own, outw_own, down_own)=refs[8:11]
    second=refs[11:19]; third=refs[19:23]; little=refs[23]
    (to, dr1, dos, keep, send, st, bst)=refs[24:31]
    (act, gp, acc, up, outw, down, upb, gbias, sem, sem_own, sem2, sem3, sem4)=refs[31:]
    mp=s_ref[0]; other=1-mp
    first=pl.program_id(0)==0
    column=lambda k: acc.at[:,128*k:128*k+128]
    own=[pltpu.make_async_copy(src,dst,sem_own.at[i]) for i,(src,dst) in enumerate((
        (outw_own,outw.at[half(mp,384),:]),(up_own,up.at[:,half(mp,1536)]),(down_own,down.at[half(mp,1536),:])))]
    two=[]; three=[]
    for i,src in enumerate(second):
        two.append([pltpu.make_async_copy(src.at[a:b],column(2*i+k).at[0:b-a],sem2.at[i,k]) for k,(a,b) in enumerate(((0,768),(768,1440)))])
    for i,src in enumerate(third):
        base=16+4*i if i<3 else 0
        three.append([pltpu.make_async_copy(src.at[768*k:768*k+768],column(base+k),sem3.at[i,k]) for k in range(3)])
    bias=[pltpu.make_async_copy(little.at[1440:1456],gbias,sem4)]
    @pl.when(first)
    def _():
        for cp in own: cp.start()
        for cp in bias: cp.start()
        for cps in two+three[:3]:
            for cp in cps: cp.start()
        for i,cps in enumerate(two):
            for cp in cps: cp.wait()
            p=s_ref[6+i]
            a,b=column(2*i),column(2*i+1)
            for j in range(12):
                src=a[96*j:96*j+96] if j<8 else b[96*(j-8):96*(j-8)+96]
                up[half(p,96),pl.ds(pl.multiple_of(other*1536+128*j,128),128)]=src.astype(BF)
            for j in range(6):
                outw[pl.ds(pl.multiple_of(other*384+p*48,16),48),128*j:128*j+128]=b[384+48*j:432+48*j].astype(BF)
        for cp in three[3]: cp.start()
        bias[0].wait()
        for j in range(12):
            upb[:,pl.ds(pl.multiple_of(other*1536+128*j,128),128)]=gbias[j:j+1]
        upb[:,half(mp,1536)]=upb_own[...]
        own[0].wait(); own[1].wait()
    phases=stream(mp*1536,xt[...],halves_of(mp,oa,ob),oa[...],ct[...],outw,up,down,sh,ga,upb,act,gp,to,dr1,dos,
        acc.at[:,0:1536],acc.at[:,1536:3072],acc.at[:,3072:3456],st,bst,512,tm[...].astype(F32).T[:,1:2])
    next(phases)
    @pl.when(first)
    def _():
        own[2].wait()
        for i,cps in enumerate(three):
            for cp in cps: cp.wait()
            p=s_ref[2+i]
            base=16+4*i if i<3 else 0
            for j in range(6):
                down[pl.ds(pl.multiple_of(other*1536+p*384,16),384),128*j:128*j+128]=column(base+j//2)[384*(j%2):384*(j%2)+384].astype(BF)
        for ref in (acc,st,bst): ref[...]=jnp.zeros_like(ref)
    next(phases)
    @pl.when(pl.program_id(0)==pl.num_programs(0)-1)
    def _():
        place_blocks(acc.at[:,0:3456],keep,send,sem,s_ref[1],n)


def ffn(n,scal,rowed,params,own,second,third,little,tile=384):
    rows=rowed[0].shape[0]
    rb=lambda a: pl.BlockSpec((tile,a.shape[1]),lambda p,*_:(p,0))
    full=lambda a: pl.BlockSpec(a.shape,lambda p,*_:(0,)*len(a.shape),pipeline_mode=pl.Buffered(1))
    whole=pl.BlockSpec(memory_space=pl.ANY)
    S=jax.ShapeDtypeStruct; V=pltpu.VMEM; D=pltpu.SemaphoreType.DMA
    rowout=[S((rows,768),F32),S((rows,768),F32)]
    dos=[S((2,rows,384),BF)]
    return pl.pallas_call(functools.partial(ffn_kernel,n),
        grid_spec=pltpu.PrefetchScalarGridSpec(num_scalar_prefetch=1,grid=(rows//tile,),
            in_specs=[rb(a) for a in rowed[:-1]]+[pl.BlockSpec((8,tile),lambda p,*_:(0,p))]+[full(w) for w in params]+[whole]*(len(own)+13),
            out_specs=[rb(a) for a in rowout]+[pl.BlockSpec((2,tile,384),lambda p,*_:(0,p,0)),whole,whole]+[pl.BlockSpec((8,m),lambda p,*_:(0,0)) for m in (768,1536)],
            scratch_shapes=[V((tile,3072),BF),V((tile,3072),BF),V((768,3712),F32),V((768,3072),BF),V((768,768),BF),V((3072,768),BF),
                V((1,3072),F32),V((16,128),F32),D,D((3,)),D((8,2)),D((4,3)),D]),
        out_shape=rowout+dos+block_shapes(768,3456,n)+[S((8,768),F32),S((8,1536),F32)],
        compiler_params=pltpu.CompilerParams(vmem_limit_bytes=VLIM),cost_estimate=cost(80),name="middle")(scal,*rowed,*params,*own,*second,*third,little)


from jax.sharding import PartitionSpec as P


def pack_kernel(starts, idx_ref, *refs):
    out=refs[-1]
    out[...]=jnp.zeros_like(out)
    r=0
    for k,src in enumerate(refs[:-1]):
        r=starts.get(k,r)
        lead=src.shape[0] if len(src.shape)==3 else None
        for c in range(lead or 1):
            w=src[c] if lead else src[...]
            n,m=w.shape
            for j in range(0,m,128):
                e=min(128,m-j)
                out[r:r+n,:e]=w[:,j:j+e].astype(F32)
                r+=n


def pack(idx, groups, parts, part=(0,1)):
    specs=[]; n=0; arrays=[]; starts=[]
    for split,whole in groups:
        starts.append((len(arrays),n))
        for a in split:
            rows=a.shape[-2]//parts
            width=a.shape[-1]//part[1]
            blocks=-(-width//128)
            if a.ndim==3:
                specs.append(pl.BlockSpec((a.shape[0],rows,a.shape[2]),lambda i,s:(0,s[0],0)))
                n+=a.shape[0]*rows*blocks
            else:
                specs.append(pl.BlockSpec((rows,width),lambda i,s:(s[0],part[0])))
                n+=rows*blocks
        for a in whole:
            specs.append(pl.BlockSpec(a.shape,lambda i,s:(0,0)))
            n+=a.shape[0]*(-(-a.shape[1]//128))
        n=-(-n//8)*8
        arrays+=split+whole
    return pl.pallas_call(functools.partial(pack_kernel,dict(starts)),
        grid_spec=pltpu.PrefetchScalarGridSpec(num_scalar_prefetch=1,grid=(1,),in_specs=specs,
            out_specs=pl.BlockSpec((n,128),lambda i,s:(0,0))),
        out_shape=jax.ShapeDtypeStruct((n,128),F32),
        compiler_params=pltpu.CompilerParams(vmem_limit_bytes=VLIM),cost_estimate=cost(2),name="pack")(idx,*arrays)


def unpack_first_kernel(s_ref, pa, pb, pc, pd, wt_own, wl_own, wt, wl, bt, bl):
    mine=s_ref[0]; other=1-mine
    wl[...]=jnp.zeros_like(wl)
    wt[mine]=wt_own[...]
    wl[mine]=wl_own[...]
    bt[...]=jnp.zeros_like(bt); bl[...]=jnp.zeros_like(bl)
    for p,ref in enumerate((pa,pb,pc,pd)):
        i=s_ref[2+p]
        at=lambda n: pl.ds(pl.multiple_of(i*n,n),n)
        r=400
        for c in range(3):
            for j in range(3):
                wt[other,c,at(192),128*j:128*j+128]=ref[r:r+192].astype(BF); r+=192
        for c in range(3):
            wl[other,c,at(48),:]=ref[r:r+48].astype(BF); r+=48
        if p==0:
            for c in range(2):
                for j in range(3):
                    bt[2*c:2*c+1,128*j:128*j+128]=ref[r+2*j+c:r+2*j+c+1]
            r+=6
            for c in range(2):
                bl[2*c:2*c+1,:]=ref[r+c:r+c+1]


def unpack_first(scal, pieces, wt, wl):
    S=jax.ShapeDtypeStruct
    full=lambda a: pl.BlockSpec(a.shape,lambda i,*_:(0,)*len(a.shape))
    outs=[S((2,3,768,384),BF),S((2,3,192,128),BF),S((3,384),F32),S((3,128),F32)]
    ins=[*pieces,wt,wl]
    return pl.pallas_call(unpack_first_kernel,
        grid_spec=pltpu.PrefetchScalarGridSpec(num_scalar_prefetch=1,grid=(1,),in_specs=[full(a) for a in ins],
            out_specs=[full(a) for a in outs]),
        out_shape=outs,compiler_params=pltpu.CompilerParams(vmem_limit_bytes=VLIM),cost_estimate=cost(4),name="unpack")(scal,*ins)


def flip(n, bit):
    return [(i,i^bit) for i in range(n)]


def cross(n, even, odd):
    return [(i,i^(even if i%2==0 else odd)) for i in range(n)]


def gather4(piece, n):
    a=lax.ppermute(piece,"mp",[(0,1),(1,0)])
    b=lax.ppermute(a,"dp",cross(n,2,4))
    c=lax.ppermute(a,"dp",flip(n,1))
    d=lax.ppermute(b,"dp",flip(n,1))
    return a,b,c,d


def gather8(piece, n):
    a=lax.ppermute(piece,"mp",[(0,1),(1,0)])
    b=lax.ppermute(a,"dp",cross(n,2,4))
    e=lax.ppermute(a,"dp",cross(n,4,2))
    f=lax.ppermute(b,"dp",cross(n,4,2))
    return (a,b,e,f)+tuple(lax.ppermute(v,"dp",flip(n,1)) for v in (a,b,e,f))


def ids8(dp):
    base=dp&7; odd=dp&1
    near=jnp.where(odd==0,2,4); far=6-near
    return [base,base^near,base^far,base^6,base^1,base^1^far,base^1^near,base^7]


def join(*values):
    return lax.optimization_barrier(values)


def stages(n):
    return (flip(n,1),cross(n,2,4),cross(n,4,2),flip(n,8))


def halve(keep, recv):
    half=keep.shape[0]//2
    return keep[:half]+recv[:half],keep[half:]+recv[half:]


def bias_rows(pair):
    b=pair.astype(F32)
    return jnp.stack([b[0],jnp.zeros_like(b[0]),b[1]])


def shards(text_in, layout_in, token_mask, box_mask, lengths, text_mask_vec, layout_mask_vec,
           text_qkv, text_qv_bias, text_out_w, text_shifts, text_gains, text_up, text_up_bias, text_down,
           layout_qkv, layout_qv_bias, layout_out_w, layout_shifts, layout_gains, layout_up, layout_up_bias, layout_down,
           text_cot, layout_cot):
    n=lax.axis_size("dp")
    mp=lax.axis_index("mp").astype(jnp.int32); dp=lax.axis_index("dp").astype(jnp.int32)
    core=dp&1; color=((dp>>1)^(dp>>2))&1
    ids=[2*color+core,2*(1-color)+core,2*color+1-core,2*(1-color)+1-core]
    scal=jnp.stack([mp,dp]+ids+ids8(dp))
    idx=ids[0][None]; idx8=(dp&7)[None]
    even_odd=cross(n,2,4); odd_even=cross(n,4,2); core_flip=flip(n,1)
    over=lambda v: lax.ppermute(v,"mp",[(0,1),(1,0)])
    send=lambda v,pairs: lax.ppermute(v,"dp",pairs)
    upb=text_up_bias.astype(F32)[None]; upbl=layout_up_bias.astype(F32)[None]
    p1=pack(idx,[([layout_out_w,layout_up,layout_down],[jnp.zeros((16,128),BF)]),([text_qkv,layout_qkv],[text_qv_bias,layout_qv_bias])],4)
    p2=pack(idx8,[([text_up,text_out_w],[upb,upbl])],8)
    p3=pack(idx,[([text_down],[])],4)
    xt=jnp.where(token_mask[:,None]==1,text_mask_vec[None],text_in)
    xl=jnp.where(box_mask[:,None]==1,layout_mask_vec[None],layout_in)
    sel=jnp.concatenate([jnp.ones_like(token_mask)[None],(token_mask==1).astype(jnp.int32)[None],(box_mask==1).astype(jnp.int32)[None],
        jnp.zeros((5,token_mask.shape[0]),jnp.int32)],0).astype(BF)
    pad=lambda v: jnp.pad(v,((0,0),)*(v.ndim-1)+((0,32),))
    wl=pad(layout_qkv)
    a1=over(p1)
    bt=bias_rows(text_qv_bias); bl=pad(bias_rows(layout_qv_bias))
    pages=lengths.shape[0]
    forward=lambda first,count,x,w,prev: attn_fwd(first,count,lengths,1-mp[None],x,xl,*w,prev)
    xa,p2,sel=join(xt,p2,sel)
    w_own=(text_qkv,wl,bt,bl)
    own=forward(0,pages-1,xa,w_own,())
    own,a1,p2=join(own,a1,p2)
    b1=send(a1,even_odd); c1=send(a1,core_flip); a2=over(p2)
    own=forward(pages-1,1,xt,w_own,own)
    own,b1,c1,a2,p3=join(own,b1,c1,a2,p3)
    d1=send(b1,core_flip); b2=send(a2,even_odd)
    wt_both,wl_both,bt_o,bl_o=unpack_first(scal,(a1,b1,c1,d1),text_qkv,wl)
    wt_both,wl_both,bt_o,bl_o,a2,b2,p3=join(wt_both,wl_both,bt_o,bl_o,a2,b2,p3)
    e2=send(a2,odd_even); f2=send(b2,odd_even); a3=over(p3)
    cores=[send(v,core_flip) for v in (a2,b2)]
    oth=forward(0,pages,xt,(wt_both,wl_both,bt_o,bl_o),())
    oth,e2,f2,a3,cores=join(oth,e2,f2,a3,cores)
    b3=send(a3,even_odd); c3=send(a3,core_flip)
    cores+=[send(v,core_flip) for v in (e2,f2)]
    beside=side(scal,xl,own[7],oth[7],layout_cot.T,sel,a2,[layout_shifts.astype(F32),layout_gains.astype(F32)],
        [layout_out_w,layout_up,layout_down,upbl],[a1,b1,c1,d1])
    beside,b3,c3,cores=join(beside,b3,c3,cores)
    lo,dr1l,dOl,extra=beside
    second=(a2,b2,e2,f2,*cores)
    d3=send(b3,core_flip)
    to,dr1,dO,keep,out,st,bst=ffn(n,scal,[xt,own[6],oth[6],text_cot,sel],[text_shifts.astype(F32),text_gains.astype(F32),upb],
        [text_up,text_out_w,text_down],second,(a3,b3,c3,d3),a2)
    steps=stages(n)
    wts=[wt_both,wl_both]
    tile=text_in.shape[0]//3
    mine_p=lambda p,c,d: attn_bwd(p,c,lengths,mp[None],own,dO,dOl,d)
    other_p=lambda p,d: attn_bwd(p,1,lengths,1-mp[None],oth,dO,dOl,d)
    sums=lambda d: qkv_grad(n,jnp.stack([mp,dp]),pages,xt,xl,*d,sel,*wts,st,bst,extra)
    inputs=lambda d: input_grad(tile,d,wts,dr1,dr1l,sel)
    if n==16:
        out=send(out,steps[0])
        d_own=mine_p(0,1,())
        d_own,out,keep=join(d_own,out,keep)
        keep,out=halve(keep,out)
        out=send(out,steps[1])
        d_own=mine_p(1,pages-1,d_own)
        qkeep,qout=sums(d_own)
        qkeep,qout,keep,out=join(qkeep,qout,keep,out)
        qout=send(qout,steps[0])
        keep,out=halve(keep,out)
        out=send(out,steps[2])
        d_oth=other_p(0,d_own)
        d_oth,qkeep,qout,keep,out=join(d_oth,qkeep,qout,keep,out)
        keep,out=halve(keep,out)
        qkeep,qout=halve(qkeep,qout)
        half=keep.shape[0]//2
        outs=[send(out[:half],steps[3]),out[half:]]
        qout=send(qout,steps[1])
        d_oth=other_p(1,d_oth)
        d_oth,qkeep,qout,outs[0],outs[1]=join(d_oth,qkeep,qout,*outs)
        outs[1]=send(outs[1],steps[3])
        qkeep,qout=halve(qkeep,qout)
        qout=send(qout,steps[2])
        d_oth=other_p(2,d_oth)
        d_oth,qkeep,qout,outs[1]=join(d_oth,qkeep,qout,outs[1])
        qkeep,qout=halve(qkeep,qout)
        qout=send(qout,steps[3])
        g=keep+jnp.concatenate(outs,0)
        d_in=inputs(d_oth)
        d_in,qkeep,qout=join(d_in,qkeep,qout)
        qg=qkeep+qout
        small=qg[:,1152:][None]
        for bit in (8,2,4,1):
            got=send(small,flip(n,bit))
            low=(dp&bit)==0
            small=jnp.stack([jnp.where(low,small,got),jnp.where(low,got,small)])
        small=small.reshape(2,2,2,2,-1,384).transpose(3,1,2,0,4,5).reshape(-1,384)
    else:
        d_own=mine_p(0,pages,())
        qkeep,qout=sums(d_own)
        rs=lambda v: lax.psum_scatter(v,"dp",scatter_dimension=0,tiled=True)
        g=rs(keep); qg=rs(qkeep)
        d_oth=d_own
        for p in range(pages): d_oth=other_p(p,d_oth)
        d_in=inputs(d_oth)
        small=lax.all_gather(qg[:,1152:],"dp",tiled=True)
    tg,lg=d_in
    r=g.shape[0]
    mine=small[:,:128]; early=small[:,128:]
    block=lambda i: early[192*(i%4):192*(i%4)+192,128*(i//4):128*(i//4)+128]
    gupl=jnp.concatenate([block(j) for j in range(3)],1); gdnl=jnp.concatenate([block(3+j) for j in range(3)],1)
    wide=lambda r,k: jnp.concatenate([block(7)[r+8*j:r+8*j+8] for j in range(k)],1)
    stl=wide(0,2)[:,:192]; bstl=wide(16,3)
    sums=mine[576:652].reshape(-1)
    st=sums[:5376].reshape(7,768); bst=sums[5376:6912]
    cs=sums[6912:7680].reshape(2,384); csl=sums[7680:7936].reshape(2,128)[:,:96]
    vec=sums[7936:8896]
    vec=vec+over(vec)
    tvec=vec[:768]+st[6]; lvec=vec[768:]+stl[6]
    qgl=jnp.stack([mine[192*c:192*c+192,:96] for c in range(3)])
    qg=jnp.moveaxis(qg[:,:1152].reshape(r,3,384),1,0)
    return (to,lo.T,tg,lg.T,tvec,lvec,qg,cs,g[:,3072:3456].T,st[:4],st[4:6],g[:,:1536],bst,g[:,1536:3072].T,
            qgl,csl,block(6)[:,:96].T,stl[:4],stl[4:6],gupl,bstl[0],gdnl.T)


def solution(mesh):
    rows=P("dp",None); cols=P(None,"mp"); lead=P("mp",None); cube=P(None,None,"mp")
    weights=(cube,cols,lead,P(),P(),cols,P("mp"),lead)
    return jax.shard_map(shards,mesh=mesh,
        in_specs=(rows,rows,P("dp"),P("dp"),P("dp"),P(),P())+weights+weights+(rows,rows),
        out_specs=(rows,rows,rows,rows,P(),P(),P(None,"dp","mp"),cols,P("mp","dp"),P(),P(),P("dp","mp"),P("mp"),P("mp","dp"),
                   cube,cols,lead,P(),P(),cols,P("mp"),lead),
        check_vma=False)
```

```python
import functools
import jax, jax.numpy as jnp
from jax import lax
from jax.experimental import pallas as pl
from jax.experimental.pallas import tpu as pltpu
F32=jnp.float32; BF=jnp.bfloat16
NT=(((1,),(1,)),((),()))
TN=(((0,),(0,)),((),()))
def dot(a,b): return jnp.dot(a,b,preferred_element_type=F32)
def dotg(a,b,dn): return lax.dot_general(a,b,dn,preferred_element_type=F32)
VLIM=60*1024*1024
SMALL=40*1024*1024

def cost(us): return pl.CostEstimate(flops=int(us*1e7),bytes_accessed=1024,transcendentals=0)

def lane_iota(shape): return lax.broadcasted_iota(jnp.int32,shape,len(shape)-1)

def row_masks():
    i=lax.broadcasted_iota(jnp.int32,(1,128),1)
    return lambda f: jnp.where(f(i),1.0,0.0).astype(BF)


def attn_fwd_kernel(first, len_ref, half_ref, xt_ref, xl_ref, wt_ref, wl_ref, bt_ref, bl_ref, *rest):
    qt_ref, kt_ref, vt_ref, ql_ref, kl_ref, vl_ref, ot_ref, ol_ref, lse_ref, olT, lseT=rest[-11:]
    page=first+pl.program_id(0)
    seq=xt_ref.shape[0]
    xt=xt_ref[...]; xl=xl_ref[...]
    for c,(t,l) in enumerate(((qt_ref,ql_ref),(kt_ref,kl_ref),(vt_ref,vl_ref))):
        t[...]=(dot(xt,wt_ref[c])+bt_ref[c:c+1,:]).astype(BF)
        l[...]=(dot(xl,wl_ref[c])+bl_ref[c:c+1,:]).astype(BF)
    lane=lane_iota((seq,128))
    row=lax.broadcasted_iota(jnp.int32,(seq,128),0)
    length=len_ref[page]
    bias=jnp.where(row<length,0.0,-1e9).astype(BF)
    one=jnp.ones((seq,128),BF)
    ql=jnp.where(lane==96,one,ql_ref[...]*BF(0.25))
    kl=jnp.where(lane==96,bias,kl_ref[...])
    vlT=vl_ref[...].T; qlT=ql.T
    keep=row_masks()
    olT[...]=jnp.zeros_like(olT); lseT[...]=jnp.zeros_like(lseT)
    def scores(h):
        j,s=h//2,h%2
        cols=slice(128*j,128*j+128)
        qbig=jnp.concatenate([(qt_ref[:,cols]*BF(0.125)).T,qlT],0)
        kbig=jnp.concatenate([kt_ref[:,cols]*keep(lambda i: i//64==s),kl*keep(lambda i: (i//16==h)|(i==96))],1)
        return dot(kbig,qbig)
    halves=[]
    def finish(h,e,m,ssum):
        j,s=h//2,h%2
        vT=vt_ref[:,128*j:128*j+128].T
        v80=jnp.concatenate([vT[64*s:64*s+64],vlT[16*h:16*h+16]],0)
        o=dot(v80,e)*(1.0/ssum)
        halves.append(o[:64])
        olT[16*h:16*h+16,:]=o[64:]
        lseT[h:h+1,:]=m+jnp.log(ssum)
        if s==1: ot_ref[:,128*j:128*j+128]=jnp.concatenate(halves[-2:],0).T.astype(BF)
    ahead=scores(0); behind=None
    for h in range(6):
        S=ahead
        if h<5: ahead=scores(h+1)
        if behind is not None: finish(*behind)
        m=jnp.max(S,0,keepdims=True)
        e=jnp.exp(S-m)
        behind=(h,e.astype(BF),m,jnp.sum(e,0,keepdims=True))
    finish(*behind)
    ol_ref[...]=olT[...].T.astype(BF)
    lse_ref[...]=pltpu.roll(lseT[...].T,97,1)

def attn_fwd(first, count, lengths, half, xt, xl, wt, wl, bt, bl, prev):
    rows=xt.shape[0]; pages=lengths.shape[0]; seq=rows//pages
    rb=lambda n: pl.BlockSpec((seq,n),lambda p,*_:(first+p,0))
    full=lambda a: pl.BlockSpec((None,)*(a.ndim-3)+a.shape[-3:],lambda p,l,h:(h[0],0,0,0)[4-a.ndim:]) if a.ndim>2 else pl.BlockSpec(a.shape,lambda p,*_:(0,0))
    whole=pl.BlockSpec(memory_space=pl.ANY)
    o=lambda n,d=BF: jax.ShapeDtypeStruct((rows,n),d)
    return pl.pallas_call(functools.partial(attn_fwd_kernel,first),
        grid_spec=pltpu.PrefetchScalarGridSpec(num_scalar_prefetch=2,grid=(count,),
            in_specs=[rb(768),rb(192),full(wt),full(wl),full(bt),full(bl)]+[whole]*len(prev),
            out_specs=[rb(384)]*3+[rb(128)]*3+[rb(384),rb(128),rb(128)],
            scratch_shapes=[pltpu.VMEM((128,seq),F32),pltpu.VMEM((128,seq),F32)]),
        out_shape=[o(384)]*3+[o(128)]*3+[o(384),o(128),o(128,F32)],
        input_output_aliases={8+i:i for i in range(len(prev))},
        compiler_params=pltpu.CompilerParams(vmem_limit_bytes=VLIM),cost_estimate=cost(6.2*count),name="attn_fwd")(lengths,half,xt,xl,wt,wl,bt,bl,*prev)

def ind_matrix(j):
    r=lax.broadcasted_iota(jnp.int32,(256,128),0)%128
    l=lax.broadcasted_iota(jnp.int32,(256,128),1)
    h=(r//64+2*j) if j is not None else r//16
    return jnp.where((l==97+h)&(h<6),1.0,0.0).astype(BF)

def split2(v):
    hi=v.astype(BF)
    return hi,(v-hi.astype(F32)).astype(BF)

def bwd_page(length, qt_ref, kt_ref, vt_ref, ql_ref, kl_ref, vl_ref, ot_ref, ol_ref, lse_ref, dot_ref, dol_ref,
                    dpt_ref, dpl_ref, dqlT, lay):
    seq=qt_ref.shape[0]
    lane=lane_iota((seq,128))
    row=lax.broadcasted_iota(jnp.int32,(seq,128),0)
    bias=jnp.where(row<length,0.0,-1e9).astype(BF)
    zero=jnp.zeros((seq,128),BF); one=jnp.ones((seq,128),BF)
    nl=-lse_ref[...]
    hi=nl.astype(BF); r1=nl-hi.astype(F32); mid=r1.astype(BF); lo=r1-mid.astype(F32)
    ext=hi+pltpu.roll(mid.astype(F32),7,1).astype(BF)+pltpu.roll(lo,14,1).astype(BF)
    qle=jnp.where(lane<96,ql_ref[...]*BF(0.25),jnp.where(lane==96,one,ext))
    kl=kl_ref[...]; vl=vl_ref[...]; ql=ql_ref[...]
    klT=kl.T
    dqlT[...]=jnp.zeros_like(dqlT)
    def sums(a,b,m):
        p=a.astype(F32)*b.astype(F32)
        h_,l_=split2(p)
        return dot(jnp.concatenate([h_,l_],1),m)
    dol=dol_ref[...]
    d_l=sums(dol,ol_ref[...],ind_matrix(None))
    d_t=d_l
    for j in range(3):
        cols=slice(128*j,128*j+128)
        d_t=d_t+sums(dot_ref[:,cols],ot_ref[:,cols],ind_matrix(j))
    def ext_delta(d):
        h_=d.astype(BF); l_=d-h_.astype(F32)
        return h_+pltpu.roll(l_,7,1).astype(BF)
    dol1=jnp.where(lane<96,dol*BF(0.125),ext_delta(d_t*-0.125))
    dol2=jnp.where(lane<96,dol*BF(0.25),ext_delta(d_l*-0.25))
    keep=row_masks()
    kle=jnp.where(lane==96,bias,jnp.where(lane>96,one,kl))
    vle=jnp.where(lane>96,one,vl)
    qleT=qle.T; dol1T=dol1.T; dol2T=dol2.T
    rows2=lambda x,masks: jnp.concatenate([x*m for m in masks],0)
    for j in range(3):
        cols=slice(128*j,128*j+128)
        qt=qt_ref[:,cols]; kt=kt_ref[:,cols]; vt=vt_ref[:,cols]; dO=dot_ref[:,cols]
        qbig=jnp.concatenate([(qt*BF(0.125)).T,qleT],0)
        dbig=jnp.concatenate([(dO*BF(0.125)).T,dol1T],0)
        ktT=kt.T
        heads=(2*j,2*j+1)
        tms=[keep(lambda i: i//64==s) for s in range(2)]
        lms=[keep(lambda i: i//16==h) for h in heads]
        R1s=[]; R2s=[]; Ps=[]; dqs=[]
        for s,h in enumerate(heads):
            kbig=jnp.concatenate([kt*tms[s],kle*keep(lambda i: (i//16==h)|(i==96)|(i==97+h)|(i==104+h)|(i==111+h))],1)
            vleh=vle*keep(lambda i: (i//16==h)|(i==97+h)|(i==104+h))
            vbig=jnp.concatenate([vt*tms[s],vleh],1)
            S=dot(kbig,qbig)
            M1=dot(vbig,dbig)
            M2=dot(vleh,dol2T)
            Pm=jnp.exp(S)
            R1=(Pm*M1).astype(BF); R2=(Pm*M2).astype(BF)
            Ps.append(Pm.astype(BF)); R1s.append(R1); R2s.append(R2)
            dqs.append(dot(ktT[64*s:64*s+64],R1))
            dqlT[16*h:16*h+16,:]=dot(klT[16*h:16*h+16],R2)
        dpt_ref[0,:,cols]=jnp.concatenate(dqs,0).T.astype(BF)
        dpt_ref[1,:,cols]=dot(jnp.concatenate(R1s,1),rows2(qt,tms)).astype(BF)
        dv=dot(jnp.concatenate(Ps,1),jnp.concatenate([rows2(dO,tms),rows2(dol,lms)],1))
        dpt_ref[2,:,cols]=dv[:,:128].astype(BF)
        dkl=dot(jnp.concatenate(R2s,1),rows2(ql,lms))
        if j==0: lay[0]=dkl; lay[1]=dv[:,128:]
        else: lay[0]+=dkl; lay[1]+=dv[:,128:]
    dpl_ref[0]=dqlT[...].T.astype(BF)
    dpl_ref[1]=lay[0].astype(BF); dpl_ref[2]=lay[1].astype(BF)


def bwd_kernel(first, len_ref, half_ref, qt, kt, vt, ql, kl, vl, ot, ol, lse, dO, dOl, *rest):
    dpt,dpl,dqlT,lay=rest[-4:]
    bwd_page(len_ref[first+pl.program_id(0)],qt,kt,vt,ql,kl,vl,ot,ol,lse,dO.at[0],dOl.at[0],dpt,dpl,dqlT,lay)


def attn_bwd(first,count,lengths,half,saved,dO,dOl,prev):
    rows=saved[0].shape[0]; seq=rows//lengths.shape[0]
    rb=lambda n: pl.BlockSpec((seq,n),lambda i,*_:(first+i,0))
    hb=lambda n: pl.BlockSpec((1,seq,n),lambda i,l,h:(h[0],first+i,0))
    pb=lambda n: pl.BlockSpec((3,seq,n),lambda i,l,h:(h[0],first+i,0))
    whole=pl.BlockSpec(memory_space=pl.ANY)
    return pl.pallas_call(functools.partial(bwd_kernel,first),
        grid_spec=pltpu.PrefetchScalarGridSpec(num_scalar_prefetch=2,grid=(count,),
            in_specs=[rb(384)]*3+[rb(128)]*3+[rb(384),rb(128),rb(128),hb(384),hb(128)]+[whole]*len(prev),
            out_specs=[pb(384),pb(128)],scratch_shapes=[pltpu.VMEM((128,seq),F32),pltpu.VMEM((2,seq,128),F32)]),
        out_shape=[jax.ShapeDtypeStruct((6,rows,384),BF),jax.ShapeDtypeStruct((6,rows,128),BF)],
        input_output_aliases={13+i:i for i in range(len(prev))},
        compiler_params=pltpu.CompilerParams(vmem_limit_bytes=SMALL if prev else VLIM),cost_estimate=cost(9*count),name="attn_bwd")(lengths,half,*saved,dO,dOl,*prev)


def dx_kernel(dpt, dpl, wt, wl, dr1, dr1l, sel, dx, dxl, wts, wls):
    @pl.when(pl.program_id(0)==0)
    def _():
        for h in range(2):
            for c in range(3):
                i=3*h+c
                wts[:,384*i:384*i+384]=wt[h,c]
                wls[:,128*i:128*i+128]=wl[h,c]
    def back(d,w,base,flag):
        v=dotg(jnp.concatenate([d[i] for i in range(6)],1),w[...],NT)+base[...]
        return jnp.where(flag>0.5,0.0,v)
    flags=sel[...].astype(F32).T
    dx[...]=back(dpt,wts,dr1,flags[:,1:2])
    dxl[...]=back(dpl,wls,dr1l,flags[:,2:3]).T


def input_grad(tile,dp,wts,dr1,dr1l,sel):
    rows=dr1.shape[0]
    rb=lambda n: pl.BlockSpec((tile,n),lambda i:(i,0))
    pb=lambda n: pl.BlockSpec((6,tile,n),lambda i:(0,i,0))
    full=lambda a: pl.BlockSpec(a.shape,lambda i:(0,0,0,0))
    return pl.pallas_call(dx_kernel,grid=(rows//tile,),
        in_specs=[pb(384),pb(128)]+[full(w) for w in wts]+[rb(768),rb(192),pl.BlockSpec((8,tile),lambda i:(0,i))],
        out_specs=[rb(768),pl.BlockSpec((192,tile),lambda i:(0,i))],
        scratch_shapes=[pltpu.VMEM((768,2304),BF),pltpu.VMEM((192,768),BF)],
        out_shape=[jax.ShapeDtypeStruct((rows,768),F32),jax.ShapeDtypeStruct((192,rows),F32)],
        compiler_params=pltpu.CompilerParams(vmem_limit_bytes=44*1024*1024),cost_estimate=cost(5),name="input_grad")(*dp,*wts,dr1,dr1l,sel)


def move_blocks(acc, keep, send, sem, position, n, left, width, start):
    cols=pl.ds(left,width)
    if n!=16:
        cp=pltpu.make_async_copy(acc,keep.at[:,cols],sem)
        if start: cp.start()
        else: cp.wait()
        return
    c=position&1; x=(position>>1)&1; z0=(position>>2)&1; z1=(position>>3)&1
    rows=acc.shape[0]//16
    for out,core in ((keep,c),(send,1-c)):
        for q in range(8):
            r2,r3,r4=q>>2,(q>>1)&1,q&1
            fx=jnp.where(core==0,r2,r3); fz=jnp.where(core==0,r3,r2)
            block=(z1^r4)*8+(z0^fz)*4+(x^fx)*2+core
            cp=pltpu.make_async_copy(acc.at[pl.ds(pl.multiple_of(block*rows,8),rows)],out.at[pl.ds(q*rows,rows),cols],sem)
            if start: cp.start()
            else: cp.wait()


def place_blocks(acc, keep, send, sem, position, n):
    for start in (True,False): move_blocks(acc,keep,send,sem,position,n,0,acc.shape[1],start)


def block_shapes(rows,cols,n):
    S=jax.ShapeDtypeStruct
    if n!=16: return [S((rows,cols),F32),S((8,128),F32)]
    return [S((rows//2,cols),F32)]*2


def qkv_grad_kernel(n, pos_ref, xt, xl, dpt, dpl, sel, wt, wl, st, bst, keep, send, acc, sums, suml, sem):
    x=xt[...]; s=sel[...]; xv=xl[...]
    def add(first):
        def put(ref,v):
            if first: ref[...]=v
            else: ref[...]+=v
        cat=lambda d: jnp.concatenate([d[0],d[1],d[2]],1)
        t=cat(dpt); l=cat(dpl)
        put(acc.at[:,:1152],dotg(x,t,TN))
        g=dotg(xv,l,TN); a=dot(s,t); b=dot(s,l)
        for c in range(3):
            put(acc.at[192*c:192*c+192,1152:1280],g[:,128*c:128*c+128])
            put(sums.at[c],a[:,384*c:384*c+384]); put(suml.at[c],b[:,128*c:128*c+128])
    first=pl.program_id(0)==0
    pl.when(first)(lambda: add(True))
    pl.when(jnp.logical_not(first))(lambda: add(False))
    @pl.when(pl.program_id(0)==pl.num_programs(0)-1)
    def _():
        t=jnp.zeros((8,768),F32); l=jnp.zeros((8,192),F32)
        for c in range(3):
            for v,w,text in ((sums[c],wt,True),(suml[c],wl,False)):
                hi,lo=split2(v)
                lo2=(v-hi.astype(F32)-lo.astype(F32)).astype(BF)
                y=dotg(jnp.concatenate([hi,lo,lo2],0),w[0,c],NT)
                y=y[0:8]+y[8:16]+y[16:24]
                if text: t=t+y
                else: l=l+y
        acc[576:768,1152:1280]=jnp.zeros((192,128),F32)
        rows=[st[i:i+1,128*j:128*j+128] for i in range(7) for j in range(6)]+[bst[0:1,128*j:128*j+128] for j in range(12)]
        rows+=[sums[c][0:1,128*j:128*j+128] for c in (0,2) for j in range(3)]+[suml[c][0:1] for c in (0,2)]
        rows+=[t[1:2,128*j:128*j+128] for j in range(6)]+[l[2:3,0:128],jnp.concatenate([l[2:3,128:],jnp.zeros((1,64),F32)],1)]
        for i,v in enumerate(rows): acc[576+i:577+i,1152:1280]=v
        place_blocks(acc,keep,send,sem,pos_ref[1],n)


def qkv_grad(n,pos,pages,xt,xl,dpt,dpl,sel,wt,wl,st,bst):
    seq=xt.shape[0]//pages
    rb=lambda m: pl.BlockSpec((seq,m),lambda i,s:(i,0))
    pb=lambda m: pl.BlockSpec((3,seq,m),lambda i,s:(s[0],i,0))
    wb=lambda a: pl.BlockSpec((1,)+a.shape[1:],lambda i,s:(s[0],0,0,0))
    whole=pl.BlockSpec(memory_space=pl.ANY)
    return pl.pallas_call(functools.partial(qkv_grad_kernel,n),
        grid_spec=pltpu.PrefetchScalarGridSpec(num_scalar_prefetch=1,grid=(pages,),
            in_specs=[rb(768),rb(192),pb(384),pb(128),pl.BlockSpec((8,seq),lambda i,s:(0,i)),wb(wt),wb(wl)]+[pl.BlockSpec(a.shape,lambda i,s:(0,0)) for a in (st,bst)],
            out_specs=[whole,whole],
            scratch_shapes=[pltpu.VMEM((768,1280),F32),pltpu.VMEM((3,8,384),F32),pltpu.VMEM((3,8,128),F32),pltpu.SemaphoreType.DMA]),
        out_shape=block_shapes(768,1280,n),
        compiler_params=pltpu.CompilerParams(vmem_limit_bytes=SMALL),cost_estimate=cost(8),name="qkv_grad")(pos,xt,xl,dpt,dpl,sel,wt,wl,st,bst)


EPS=1e-5
def gelu_parts(x):
    cdf=0.5+0.5*lax.erf(x*0.7071067811865476)
    phi=jnp.exp2(x*x*-0.7213475204444817-1.3257480647361593)
    return cdf, cdf+x*phi

def norm(v):
    mu=jnp.mean(v,-1,keepdims=True)
    c=v-mu
    inv=lax.rsqrt(jnp.mean(c*c,-1,keepdims=True)+EPS)
    return c*inv,inv

def norm_back(g,u,inv,gain):
    s=g*gain
    return inv*(s-jnp.mean(s,-1,keepdims=True)-u*jnp.mean(s*u,-1,keepdims=True))

def stream(own_off, x, o, o_own, cot, outw, up, down, shift, gain, upb, act, gp, out_ref, dr1_ref, dos, gup, gdn, gout, stat, bstat, chunk, flag, kept=None):
    d=x.shape[1]; F=up.shape[1]; half=F//2
    h1u,i1=norm(x.astype(F32)+dot(o,outw[...])+shift[2:3])
    h1=h1u*gain[0:1]+shift[0:1]
    h1b=h1.astype(BF)
    yield
    def units(i,carry):
        cs=pl.ds(pl.multiple_of(i*chunk,chunk),chunk)
        pre=dot(h1b,up[:,cs])+upb[:,cs]
        cdf,der=gelu_parts(pre)
        act[:,cs]=(pre*cdf).astype(BF)
        gp[:,cs]=der.astype(BF)
        return carry
    lax.fori_loop(0,F//chunk,units,0)
    yield
    r2=h1+dot(act[...],down[...])+shift[3:4]
    u2,i2=norm(r2)
    y=u2*gain[1:2]+shift[1:2]
    out_ref[...]=y if out_ref.shape==y.shape else y.T
    g=cot.astype(F32)
    dr2=norm_back(g,u2,i2,gain[1:2])
    dr2b=dr2.astype(BF)
    def units_back(i,carry):
        cs=pl.ds(pl.multiple_of(i*chunk,chunk),chunk)
        da=dotg(dr2b,down[cs,:],NT)
        gp[:,cs]=(da*gp[:,cs].astype(F32)).astype(BF)
        return carry
    lax.fori_loop(0,F//chunk,units_back,0)
    dh1=dotg(gp[...],up[...],NT)+dr2
    dr1=norm_back(dh1,h1u,i1,gain[0:1])
    dr1_ref[...]=dr1
    dr1b=dr1.astype(BF)
    dO=dotg(dr1b,outw[...],NT).astype(BF)
    w=dO.shape[1]//2
    dos[0]=dO[:,:w]; dos[1]=dO[:,w:]
    osl=pl.ds(pl.multiple_of(own_off,128),half)
    dpo=gp[:,osl]
    rs=lambda v: jnp.sum(v,0,keepdims=True)
    stat[...]+=jnp.concatenate([rs(dh1),rs(g),rs(dr1),rs(dr2),rs(dh1*h1u),rs(g*u2),rs(jnp.where(flag>0.5,dr1,0.0)),jnp.zeros((1,d),F32)],0)
    bstat[...]+=dot(jnp.ones((8,x.shape[0]),BF),dpo)
    if kept is not None:
        for ref,v in zip(kept,(h1b,dr2b,dr1b,o_own)): ref[...]=v
    else:
        gup[...]+=dotg(h1b,dpo,TN)
        gdn[...]+=dotg(dr2b,act[:,osl],TN)
        gout[...]+=dotg(dr1b,o_own,TN)
    yield


def halves_of(mp, a, b):
    a=a[...]; b=b[...]
    z=mp==0
    return jnp.concatenate([jnp.where(z,a,b),jnp.where(z,b,a)],1)


def half(k, m): return pl.ds(pl.multiple_of(k*m,m),m)


def side_kernel(s_ref, xl, ola, olb, cl, lm, little, shl, gal, outl_own, upl_own, downl_own, upbl_own, pa, pb, pc, pd,
                lo, dr1l, dosl, extra, actl, gpl, outwl, upl, downl, upbl, gupl, gdnl, goutl, stl, bstl, outs):
    mp=s_ref[0]; other=1-mp
    @pl.when(pl.program_id(0)==0)
    def _():
        upbl[:,half(mp,384)]=upbl_own[...]
        upl[:,half(mp,384)]=upl_own[...]
        downl[half(mp,384),:]=downl_own[...]
        outwl[half(mp,128),:]=jnp.concatenate([outl_own[...],jnp.zeros((32,192),BF)],0)
        outs[...]=jnp.zeros_like(outs)
        for i,v in enumerate((pa,pb,pc,pd)):
            p=s_ref[2+i]
            rows=pl.ds(pl.multiple_of(p*24,8),24)
            outs[rows,0:128]=v[0:24]; outs[rows,128:192]=v[24:48,0:64]
            for j in range(3):
                upl[half(p,48),pl.ds(pl.multiple_of(other*384+128*j,128),128)]=v[48+48*j:96+48*j].astype(BF)
            rows=pl.ds(pl.multiple_of(other*384+p*96,16),96)
            downl[rows,0:128]=v[192:288].astype(BF)
            downl[rows,128:192]=v[288:384,0:64].astype(BF)
        outwl[half(other,128),:]=outs[...].astype(BF)
        for j in range(3):
            upbl[:,pl.ds(pl.multiple_of(other*384+128*j,128),128)]=little[12+j:13+j]
        for ref in (gupl,gdnl,goutl,stl,bstl): ref[...]=jnp.zeros_like(ref)
    phases=stream(mp*384,xl[...],halves_of(mp,ola,olb),ola[...],cl[...].T,outwl,upl,downl,shl,gal,upbl,actl,gpl,lo,dr1l,dosl,gupl,gdnl,goutl,stl,bstl,768,lm[...].astype(F32).T[:,2:3])
    next(phases); next(phases); next(phases)
    @pl.when(pl.program_id(0)==pl.num_programs(0)-1)
    def _():
        blocks=[gupl[:,128*j:128*j+128] for j in range(3)]+[gdnl[:,128*j:128*j+128] for j in range(3)]+[goutl[...]]
        rest=[stl[:,0:128],jnp.concatenate([stl[:,128:192],jnp.zeros((8,64),F32)],1)]
        rest+=[bstl[:,128*j:128*j+128] for j in range(3)]+[jnp.zeros((152,128),F32)]
        blocks.append(jnp.concatenate(rest,0))
        for i,v in enumerate(blocks):
            extra[192*(i%4):192*(i%4)+192,128*(i//4):128*(i//4)+128]=v


def side(scal,xl,ola,olb,cl,lm,little,params,own,pieces,tile=768):
    rows=xl.shape[0]
    rb=lambda n: pl.BlockSpec((tile,n),lambda p,*_:(p,0))
    cb=pl.BlockSpec((192,tile),lambda p,*_:(0,p))
    full=lambda a: pl.BlockSpec(a.shape,lambda p,*_:(0,)*len(a.shape))
    S=jax.ShapeDtypeStruct; V=pltpu.VMEM
    last=pl.BlockSpec((400,128),lambda p,*_:(0,0))
    return pl.pallas_call(side_kernel,
        grid_spec=pltpu.PrefetchScalarGridSpec(num_scalar_prefetch=1,grid=(rows//tile,),
            in_specs=[rb(192),rb(128),rb(128),cb,pl.BlockSpec((8,tile),lambda p,*_:(0,p)),pl.BlockSpec((16,128),lambda p,*_:(36,0))]+[full(a) for a in params+own]+[last]*4,
            out_specs=[cb,rb(192),pl.BlockSpec((2,tile,128),lambda p,*_:(0,p,0)),pl.BlockSpec((768,256),lambda p,*_:(0,0))],
            scratch_shapes=[V((tile,768),BF),V((tile,768),BF),V((256,192),BF),V((192,768),BF),V((768,192),BF),V((1,768),F32),
                V((192,384),F32),V((192,384),F32),V((192,128),F32),V((8,192),F32),V((8,384),F32),V((128,192),F32)]),
        out_shape=[S((192,rows),F32),S((rows,192),F32),S((2,rows,128),BF),S((768,256),F32)],
        compiler_params=pltpu.CompilerParams(vmem_limit_bytes=VLIM),cost_estimate=cost(10),name="side")(scal,xl,ola,olb,cl,lm,little,*params,*own,*pieces)


def ffn_kernel(n, s_ref, *refs):
    (xt, oa, ob, ct, tm, sh, ga, upb_own)=refs[:8]
    (up_own, outw_own, down_own)=refs[8:11]
    second=refs[11:19]; third=[refs[19+2*i:21+2*i] for i in range(4)]; extra=refs[27]
    (to, dr1, dos, keep, send, st, bst)=refs[28:35]
    (act2, gp2, hb2, rb2, sb2, ob2, acc, up, outw, down, upb, gbias, sem, sem_own, sem2, sem3, sem4)=refs[35:]
    step=pl.program_id(0); odd=step%2; tile=xt.shape[0]
    part=pl.ds(pl.multiple_of(odd*tile,tile),tile)
    act=act2.at[part]; gp=gp2.at[part]
    mp=s_ref[0]; other=1-mp
    first=pl.program_id(0)==0
    column=lambda k: acc.at[:,128*k:128*k+128]
    own=[pltpu.make_async_copy(src,dst,sem_own.at[i]) for i,(src,dst) in enumerate((
        (outw_own,outw.at[half(mp,384),:]),(up_own,up.at[:,half(mp,1536)]),(down_own,down.at[half(mp,1536),:])))]
    two=[]; three=[]
    for i,src in enumerate(second):
        two.append([pltpu.make_async_copy(src.at[a:b],column(2*i+k).at[0:b-a],sem2.at[i,k]) for k,(a,b) in enumerate(((0,768),(768,1152)))])
    outs=[]
    for i,src in enumerate(third):
        base=16+4*i if i<3 else 0
        three.append([pltpu.make_async_copy(src[s].at[r:r+768],column(base+k),sem3.at[i,k]) for k,(s,r) in enumerate(((0,0),(1,592),(1,1360)))])
        outs.append(pltpu.make_async_copy(src[1].at[0:576],column(19+4*i if i<3 else 28).at[0:576],sem3.at[i,3]))
    bias=[pltpu.make_async_copy(third[0][1].at[576:592],gbias,sem4)]
    @pl.when(first)
    def _():
        for cp in outs+own[:1]+bias: cp.start()
        for cps in two:
            for cp in cps: cp.start()
        own[1].start()
        for cps in three[:3]:
            for cp in cps: cp.start()
        own[2].start()
        for cp in outs: cp.wait()
        for i in range(4):
            for j in range(6):
                v=column(19+4*i if i<3 else 28)[96*j:96*j+96]
                outw[pl.ds(pl.multiple_of(other*384+s_ref[2+i]*96,16),96),128*j:128*j+128]=v.astype(BF)
        own[0].wait()
    phases=stream(mp*1536,xt[...],halves_of(mp,oa,ob),oa[...],ct[...],outw,up,down,sh,ga,upb,act,gp,to,dr1,dos,
        None,None,None,st,bst,1536,tm[...].astype(F32).T[:,1:2],[r.at[part] for r in (hb2,rb2,sb2,ob2)])
    next(phases)
    @pl.when(first)
    def _():
        for cps in two:
            for cp in cps: cp.wait()
        def unpack_second(i,carry):
            p=s_ref[6+i]
            left=pl.ds(pl.multiple_of(256*i,128),128); right=pl.ds(pl.multiple_of(256*i+128,128),128)
            for j in range(12):
                v=acc[96*j:96*j+96,left] if j<8 else acc[96*(j-8):96*(j-8)+96,right]
                up[half(p,96),pl.ds(pl.multiple_of(other*1536+128*j,128),128)]=v.astype(BF)
            return carry
        lax.fori_loop(0,8,unpack_second,0)
        for cp in three[3]: cp.start()
        bias[0].wait()
        for j in range(12):
            upb[:,pl.ds(pl.multiple_of(other*1536+128*j,128),128)]=gbias[j:j+1]
        upb[:,half(mp,1536)]=upb_own[...]
        own[1].wait()
    next(phases)
    @pl.when(first)
    def _():
        own[2].wait()
        for cps in three:
            for cp in cps: cp.wait()
        def unpack_third(i,carry):
            p=s_ref[2+i]
            base=jnp.where(i<3,2048+512*i,0)
            for j in range(6):
                v=acc[384*(j%2):384*(j%2)+384,pl.ds(pl.multiple_of(base+128*(j//2),128),128)]
                down[pl.ds(pl.multiple_of(other*1536+p*384,16),384),128*j:128*j+128]=v.astype(BF)
            return carry
        lax.fori_loop(0,4,unpack_third,0)
        def clear(i,carry):
            acc[pl.ds(pl.multiple_of(16*i,16),16),:]=jnp.zeros((16,acc.shape[1]),F32)
            return carry
        lax.fori_loop(0,48,clear,0)
        st[...]=jnp.zeros_like(st); bst[...]=jnp.zeros_like(bst)
    next(phases)
    last=step==pl.num_programs(0)-1
    osl=half(mp,1536)
    copies=[]
    def into(left,width,lhs,rhs):
        acc[:,left:left+width]+=dotg(lhs,rhs,TN)
        @pl.when(last)
        def _(): move_blocks(acc.at[:,left:left+width],keep,send,sem,s_ref[1],n,left,width,True)
    @pl.when(odd==1)
    def _():
        @pl.when(last)
        def _():
            cp=pltpu.make_async_copy(extra,acc.at[:,3456:3712],sem4)
            cp.start(); cp.wait()
            move_blocks(acc.at[:,3456:3712],keep,send,sem,s_ref[1],n,3456,256,True)
        into(0,1536,hb2[...],gp2[:,osl])
        into(1536,1536,rb2[...],act2[:,osl])
        into(3072,384,sb2[...],ob2[...])
        @pl.when(last)
        def _(): move_blocks(acc,keep,send,sem,s_ref[1],n,0,3712,False)


def ffn(n,scal,rowed,params,own,second,third,extra,tile=384):
    rows=rowed[0].shape[0]
    rb=lambda a: pl.BlockSpec((tile,a.shape[1]),lambda p,*_:(p,0))
    full=lambda a: pl.BlockSpec(a.shape,lambda p,*_:(0,)*len(a.shape),pipeline_mode=pl.Buffered(1))
    whole=pl.BlockSpec(memory_space=pl.ANY)
    S=jax.ShapeDtypeStruct; V=pltpu.VMEM; D=pltpu.SemaphoreType.DMA
    rowout=[S((rows,768),F32),S((rows,768),F32)]
    dos=[S((2,rows,384),BF)]
    return pl.pallas_call(functools.partial(ffn_kernel,n),
        grid_spec=pltpu.PrefetchScalarGridSpec(num_scalar_prefetch=1,grid=(rows//tile,),
            in_specs=[rb(a) for a in rowed[:-1]]+[pl.BlockSpec((8,tile),lambda p,*_:(0,p))]+[full(w) for w in params]+[whole]*(len(own)+17),
            out_specs=[rb(a) for a in rowout]+[pl.BlockSpec((2,tile,384),lambda p,*_:(0,p,0)),whole,whole]+[pl.BlockSpec((8,m),lambda p,*_:(0,0)) for m in (768,1536)],
            scratch_shapes=[V((2*tile,3072),BF),V((2*tile,3072),BF),V((2*tile,768),BF),V((2*tile,768),BF),V((2*tile,768),BF),V((2*tile,384),BF),V((768,3712),F32),V((768,3072),BF),V((768,768),BF),V((3072,768),BF),
                V((1,3072),F32),V((16,128),F32),D,D((3,)),D((8,2)),D((4,4)),D]),
        out_shape=rowout+dos+block_shapes(768,3712,n)+[S((8,768),F32),S((8,1536),F32)],
        compiler_params=pltpu.CompilerParams(vmem_limit_bytes=VLIM),cost_estimate=cost(80),name="middle")(scal,*rowed,*params,*own,*second,*[v for pair in third for v in pair],extra)


from jax.sharding import PartitionSpec as P


def pack_kernel(starts, idx_ref, *refs):
    out=refs[-1]
    out[...]=jnp.zeros_like(out)
    r=0
    for k,src in enumerate(refs[:-1]):
        r=starts.get(k,r)
        lead=src.shape[0] if len(src.shape)==3 else None
        for c in range(lead or 1):
            w=src[c] if lead else src[...]
            n,m=w.shape
            for j in range(0,m,128):
                e=min(128,m-j)
                out[r:r+n,:e]=w[:,j:j+e].astype(F32)
                r+=n


def pack(idx, groups, parts):
    specs=[]; n=0; arrays=[]; starts=[]
    for split,whole in groups:
        starts.append((len(arrays),n))
        split=[a if isinstance(a,tuple) else (a,(0,1)) for a in split]
        for a,part in split:
            rows=a.shape[-2]//parts
            width=a.shape[-1]//part[1]
            blocks=-(-width//128)
            if a.ndim==3:
                specs.append(pl.BlockSpec((a.shape[0],rows,a.shape[2]),lambda i,s:(0,s[0],0)))
                n+=a.shape[0]*rows*blocks
            else:
                specs.append(pl.BlockSpec((rows,width),functools.partial(lambda k,i,s:(s[0],k),part[0])))
                n+=rows*blocks
        for a in whole:
            specs.append(pl.BlockSpec(a.shape,lambda i,s:(0,0)))
            n+=a.shape[0]*(-(-a.shape[1]//128))
        n=-(-n//8)*8
        arrays+=[a for a,_ in split]+whole
    return pl.pallas_call(functools.partial(pack_kernel,dict(starts)),
        grid_spec=pltpu.PrefetchScalarGridSpec(num_scalar_prefetch=1,grid=(1,),in_specs=specs,
            out_specs=pl.BlockSpec((n,128),lambda i,s:(0,0))),
        out_shape=jax.ShapeDtypeStruct((n,128),F32),
        compiler_params=pltpu.CompilerParams(vmem_limit_bytes=VLIM),cost_estimate=cost(2),name="pack")(idx,*arrays)


def unpack_first_kernel(s_ref, pa, pb, pc, pd, wt_own, wl_own, wt, wl, bt, bl):
    mine=s_ref[0]; other=1-mine
    wl[...]=jnp.zeros_like(wl)
    wt[mine]=wt_own[...]
    wl[mine]=wl_own[...]
    bt[...]=jnp.zeros_like(bt); bl[...]=jnp.zeros_like(bl)
    for p,ref in enumerate((pa,pb,pc,pd)):
        i=s_ref[2+p]
        at=lambda n: pl.ds(pl.multiple_of(i*n,n),n)
        r=400
        for c in range(3):
            for j in range(3):
                wt[other,c,at(192),128*j:128*j+128]=ref[r:r+192].astype(BF); r+=192
        for c in range(3):
            wl[other,c,at(48),:]=ref[r:r+48].astype(BF); r+=48
        if p==0:
            for c in range(2):
                for j in range(3):
                    bt[2*c:2*c+1,128*j:128*j+128]=ref[r+2*j+c:r+2*j+c+1]
            r+=6
            for c in range(2):
                bl[2*c:2*c+1,:]=ref[r+c:r+c+1]


def unpack_first(scal, pieces, wt, wl):
    S=jax.ShapeDtypeStruct
    full=lambda a: pl.BlockSpec(a.shape,lambda i,*_:(0,)*len(a.shape))
    outs=[S((2,3,768,384),BF),S((2,3,192,128),BF),S((3,384),F32),S((3,128),F32)]
    ins=[*pieces,wt,wl]
    return pl.pallas_call(unpack_first_kernel,
        grid_spec=pltpu.PrefetchScalarGridSpec(num_scalar_prefetch=1,grid=(1,),in_specs=[full(a) for a in ins],
            out_specs=[full(a) for a in outs]),
        out_shape=outs,compiler_params=pltpu.CompilerParams(vmem_limit_bytes=VLIM),cost_estimate=cost(4),name="unpack")(scal,*ins)


def flip(n, bit):
    return [(i,i^bit) for i in range(n)]


def cross(n, even, odd):
    return [(i,i^(even if i%2==0 else odd)) for i in range(n)]


def gather4(piece, n):
    a=lax.ppermute(piece,"mp",[(0,1),(1,0)])
    b=lax.ppermute(a,"dp",cross(n,2,4))
    c=lax.ppermute(a,"dp",flip(n,1))
    d=lax.ppermute(b,"dp",flip(n,1))
    return a,b,c,d


def gather8(piece, n):
    a=lax.ppermute(piece,"mp",[(0,1),(1,0)])
    b=lax.ppermute(a,"dp",cross(n,2,4))
    e=lax.ppermute(a,"dp",cross(n,4,2))
    f=lax.ppermute(b,"dp",cross(n,4,2))
    return (a,b,e,f)+tuple(lax.ppermute(v,"dp",flip(n,1)) for v in (a,b,e,f))


def ids8(dp):
    base=dp&7; odd=dp&1
    near=jnp.where(odd==0,2,4); far=6-near
    return [base,base^near,base^far,base^6,base^1,base^1^far,base^1^near,base^7]


def join(*values):
    return lax.optimization_barrier(values)


def stages(n):
    return (flip(n,1),cross(n,2,4),cross(n,4,2),flip(n,8))


def halve(keep, recv):
    half=keep.shape[0]//2
    return keep[:half]+recv[:half],keep[half:]+recv[half:]


def finish_kernel(order, c_ref, small, other, early, early_other, tv, lv, cs, sh, ga, bst, gl, csl, ol, shl, gal, ul, bl, dl, buf):
    rows=small.shape[1]
    for ref,ref2,(a,b) in ((small,other,((0,128),(384,512))),(early,early_other,((128,256),(256,384)))):
        if not order:
            v=ref[0]
            buf[:,a[0]:a[1]]=v[:,:128]; buf[:,b[0]:b[1]]=v[:,128:]
        low=c_ref[0]==0
        for i,k in enumerate(order):
            mine,got=ref[k],ref2[k]
            v=jnp.where(low,mine,got) if i%2==0 else jnp.where(low,got,mine)
            buf[rows*i:rows*i+rows,a[0]:a[1]]=v[:,:128]; buf[rows*i:rows*i+rows,b[0]:b[1]]=v[:,128:]
    block=lambda i: buf[192*(i%4):192*(i%4)+192,128+128*(i//4):256+128*(i//4)]
    for j in range(3):
        ul[:,128*j:128*j+128]=block(j)
        dl[:,128*j:128*j+128]=block(3+j)
        gl[j]=buf[192*j:192*j+192,0:96]
    ol[...]=block(6).T[0:96]
    last=block(7)
    for ref,r0 in ((shl,0),(gal,4)):
        n=ref.shape[0]
        ref[:,0:128]=last[r0:r0+n]; ref[:,128:192]=last[8+r0:8+r0+n,0:64]
    for j in range(3): bl[128*j:128*j+128]=last[16+8*j]
    row=lambda i,c=0: buf[576+i:577+i,128*c:128*c+128]
    for j in range(6):
        s=slice(128*j,128*j+128)
        for i in range(4): sh[i:i+1,s]=row(6*i+j)
        for i in range(2): ga[i:i+1,s]=row(24+6*i+j)
        tv[s]=((row(62+j)+row(62+j,3))+row(36+j))[0]
    for j in range(12): bst[128*j:128*j+128]=row(42+j)[0]
    for i in range(2):
        for j in range(3): cs[i:i+1,128*j:128*j+128]=row(54+3*i+j)
        csl[i:i+1,:]=row(60+i)[:,0:96]
    lv[0:128]=((row(68)+row(68,3))+last[6:7])[0]
    lv[128:192]=((row(69)+row(69,3))[:,0:64]+last[14:15,0:64])[0]


def finish(order, core, *parts):
    S=lambda *shape: jax.ShapeDtypeStruct(shape,F32)
    outs=[S(768),S(192),S(2,384),S(4,768),S(2,768),S(1536),S(3,192,96),S(2,96),S(96,192),S(4,192),S(2,192),S(192,384),S(384),S(192,384)]
    full=lambda a: pl.BlockSpec(a.shape,lambda i,*_:(0,)*len(a.shape))
    return pl.pallas_call(functools.partial(finish_kernel,order),
        grid_spec=pltpu.PrefetchScalarGridSpec(num_scalar_prefetch=1,grid=(1,),in_specs=[full(a) for a in parts],
            out_specs=[full(a) for a in outs],scratch_shapes=[pltpu.VMEM((768,512),F32)]),
        out_shape=outs,
        compiler_params=pltpu.CompilerParams(vmem_limit_bytes=VLIM),cost_estimate=cost(2),name="finish")(core,*parts)


def bias_rows(pair):
    b=pair.astype(F32)
    return jnp.stack([b[0],jnp.zeros_like(b[0]),b[1]])


def shards(text_in, layout_in, token_mask, box_mask, lengths, text_mask_vec, layout_mask_vec,
           text_qkv, text_qv_bias, text_out_w, text_shifts, text_gains, text_up, text_up_bias, text_down,
           layout_qkv, layout_qv_bias, layout_out_w, layout_shifts, layout_gains, layout_up, layout_up_bias, layout_down,
           text_cot, layout_cot):
    n=lax.axis_size("dp")
    mp=lax.axis_index("mp").astype(jnp.int32); dp=lax.axis_index("dp").astype(jnp.int32)
    core=dp&1; color=((dp>>1)^(dp>>2))&1
    ids=[2*color+core,2*(1-color)+core,2*color+1-core,2*(1-color)+1-core]
    scal=jnp.stack([mp,dp]+ids+ids8(dp))
    idx=ids[0][None]; idx8=(dp&7)[None]
    even_odd=cross(n,2,4); odd_even=cross(n,4,2); core_flip=flip(n,1)
    over=lambda v: lax.ppermute(v,"mp",[(0,1),(1,0)])
    send=lambda v,pairs: lax.ppermute(v,"dp",pairs)
    upb=text_up_bias.astype(F32)[None]; upbl=layout_up_bias.astype(F32)[None]
    p1=pack(idx,[([layout_out_w,layout_up,layout_down],[jnp.zeros((16,128),BF)]),([text_qkv,layout_qkv],[text_qv_bias,layout_qv_bias])],4)
    p2=pack(idx8,[([text_up],[])],8)
    p3=pack(idx,[([(text_down,(0,3))],[])],4)
    p4=pack(idx,[([text_out_w],[upb,upbl]),([(text_down,(1,3)),(text_down,(2,3))],[])],4)
    xt=jnp.where(token_mask[:,None]==1,text_mask_vec[None],text_in)
    xl=jnp.where(box_mask[:,None]==1,layout_mask_vec[None],layout_in)
    sel=jnp.concatenate([jnp.ones_like(token_mask)[None],(token_mask==1).astype(jnp.int32)[None],(box_mask==1).astype(jnp.int32)[None],
        jnp.zeros((5,token_mask.shape[0]),jnp.int32)],0).astype(BF)
    pad=lambda v: jnp.pad(v,((0,0),)*(v.ndim-1)+((0,32),))
    wl=pad(layout_qkv)
    a1=over(p1)
    bt=bias_rows(text_qv_bias); bl=pad(bias_rows(layout_qv_bias))
    pages=lengths.shape[0]
    forward=lambda first,count,x,w,prev: attn_fwd(first,count,lengths,1-mp[None],x,xl,*w,prev)
    xa,p2,sel=join(xt,p2,sel)
    w_own=(text_qkv,wl,bt,bl)
    own=forward(0,pages-1,xa,w_own,())
    own,a1,p2=join(own,a1,p2)
    b1=send(a1,even_odd); c1=send(a1,core_flip); a2=over(p2)
    own=forward(pages-1,1,xt,w_own,own)
    own,b1,c1,a2,p3,p4=join(own,b1,c1,a2,p3,p4)
    d1=send(b1,core_flip); b2=send(a2,even_odd); a3=over(p3)
    cores=[send(a2,core_flip)]
    wt_both,wl_both,bt_o,bl_o=unpack_first(scal,(a1,b1,c1,d1),text_qkv,wl)
    wt_both,wl_both,bt_o,bl_o,a2,b2,a3,p4,cores=join(wt_both,wl_both,bt_o,bl_o,a2,b2,a3,p4,cores)
    e2=send(a2,odd_even); f2=send(b2,odd_even); a4=over(p4); b3=send(a3,even_odd)
    cores+=[send(b2,core_flip)]
    w_oth=(wt_both,wl_both,bt_o,bl_o)
    oth=forward(0,1,xt,w_oth,())
    oth=forward(1,pages-1,xt,w_oth,oth)
    oth,e2,f2,a4,b3,cores=join(oth,e2,f2,a4,b3,cores)
    b4=send(a4,even_odd); c4=send(a4,core_flip); c3=send(a3,core_flip)
    cores+=[send(v,core_flip) for v in (e2,f2)]
    beside=side(scal,xl,own[7],oth[7],layout_cot.T,sel,a4,[layout_shifts.astype(F32),layout_gains.astype(F32)],
        [layout_out_w,layout_up,layout_down,upbl],[a1,b1,c1,d1])
    beside,b4,c4,c3,cores=join(beside,b4,c4,c3,cores)
    lo,dr1l,dOl,extra=beside
    second=(a2,b2,e2,f2,*cores)
    d3=send(b3,core_flip); d4=send(b4,core_flip)
    to,dr1,dO,keep,out,st,bst=ffn(n,scal,[xt,own[6],oth[6],text_cot,sel],[text_shifts.astype(F32),text_gains.astype(F32),upb],
        [text_up,text_out_w,text_down],second,((a3,a4),(b3,b4),(c3,c4),(d3,d4)),extra)
    steps=stages(n)
    wts=[wt_both,wl_both]
    tile=text_in.shape[0]//3
    mine_p=lambda p,c,d: attn_bwd(p,c,lengths,mp[None],own,dO,dOl,d)
    other_p=lambda p,d: attn_bwd(p,1,lengths,1-mp[None],oth,dO,dOl,d)
    sums=lambda d: qkv_grad(n,jnp.stack([mp,dp]),pages,xt,xl,*d,sel,*wts,st,bst)
    inputs=lambda d: input_grad(tile,d,wts,dr1,dr1l,sel)
    if n==16:
        out=send(out,steps[0])
        d_own=mine_p(0,1,())
        d_own,out,keep=join(d_own,out,keep)
        keep,out=halve(keep,out)
        out=send(out,steps[1])
        d_own=mine_p(1,pages-1,d_own)
        qkeep,qout=sums(d_own)
        qkeep,qout,keep,out=join(qkeep,qout,keep,out)
        qout=send(qout,steps[0])
        keep,out=halve(keep,out)
        half=keep.shape[0]//2
        far=send(out[half:],steps[2])
        d_oth=other_p(0,d_own)
        d_oth,qkeep,qout,keep,out,far=join(d_oth,qkeep,qout,keep,out,far)
        out_far=keep[half:]+far
        cut=out_far.shape[0]//2
        outs=[send(out_far[:cut],steps[3]),out_far[cut:]]
        qkeep,qout=halve(qkeep,qout)
        qout=send(qout,steps[1])
        d_oth=other_p(1,d_oth)
        d_oth,qkeep,qout,keep,out,outs[0],outs[1]=join(d_oth,qkeep,qout,keep,out,*outs)
        outs[1]=send(outs[1],steps[3])
        near_small=send(out[:half,3456:],steps[2])
        qkeep,qout=halve(qkeep,qout)
        qout=send(qout,steps[2])
        d_oth=other_p(2,d_oth)
        d_oth,qkeep,qout,keep,out,near_small,*outs=join(d_oth,qkeep,qout,keep,out,near_small,*outs)
        qkeep,qout_sent=halve(qkeep,qout)
        qout=send(qout_sent,steps[3])
        got_far=jnp.concatenate(outs,0)
        early=(keep[:half,3456:]+near_small)+got_far[:,3456:]
        early_got=send(early,steps[3])
        peer=over(jnp.concatenate([qkeep[:,1152:1280],qout_sent[:,1152:1280]],0))
        near=send(out[:half,:3456],steps[2])
        pair=lambda bit,x,y: (lambda low: jnp.stack([jnp.where(low,x,y),jnp.where(low,y,x)]))((dp&bit)==0)
        d_in=inputs(d_oth)
        d_in,qkeep,qout,peer,early_got,near=join(d_in,qkeep,qout,peer,early_got,near)
        g=(keep[:half,:3456]+near)+got_far[:,:3456]
        qg=qkeep+qout
        small=qg[:,1152:]
        got=send(small,steps[3]); peer_got=send(peer,steps[3])
        early=pair(8,early,early_got)
        early=pair(2,early,send(early,flip(n,2)))
        r=qg.shape[0]
        small=jnp.concatenate([pair(8,small,got),pair(8,peer[:r]+peer_got[r:],peer_got[:r]+peer[r:])],2)
        early=pair(4,early,send(early,flip(n,4))).reshape(8,-1,256)
        small=pair(2,small,send(small,flip(n,2)))
        early=(early,send(early,core_flip))
        small=pair(4,small,send(small,flip(n,4))).reshape(8,-1,256)
        small=(small,send(small,core_flip))
        order=[(i>>2&1)*4+(i>>1&1)*2+(i>>3) for i in range(16)]
    else:
        d_own=mine_p(0,pages,())
        qkeep,qout=sums(d_own)
        rs=lambda v: lax.psum_scatter(v,"dp",scatter_dimension=0,tiled=True)
        g=rs(keep); qg=rs(qkeep)
        d_oth=d_own
        for p in range(pages): d_oth=other_p(p,d_oth)
        d_in=inputs(d_oth)
        whole=lambda v: (lambda w: (w[None],w[None,:8]))(lax.all_gather(v,"dp",tiled=True))
        small=whole(jnp.concatenate([qg[:,1152:],over(qg[:,1152:])],1)); early=whole(g[:,3456:])
        order=[]
    tg,lg=d_in
    r=g.shape[0]
    tvec,lvec,cs,shifts,gains,bst,qgl,csl,outl,shl,gal,upl,bstl,downl=finish(order,core[None],*small,*early)
    qg=jnp.moveaxis(qg[:,:1152].reshape(r,3,384),1,0)
    return (to,lo.T,tg,lg.T,tvec,lvec,qg,cs,g[:,3072:3456].T,shifts,gains,g[:,:1536],bst,g[:,1536:3072].T,
            qgl,csl,outl,shl,gal,upl,bstl,downl.T)


def solution(mesh):
    rows=P("dp",None); cols=P(None,"mp"); lead=P("mp",None); cube=P(None,None,"mp")
    weights=(cube,cols,lead,P(),P(),cols,P("mp"),lead)
    return jax.shard_map(shards,mesh=mesh,
        in_specs=(rows,rows,P("dp"),P("dp"),P("dp"),P(),P())+weights+weights+(rows,rows),
        out_specs=(rows,rows,rows,rows,P(),P(),P(None,"dp","mp"),cols,P("mp","dp"),P(),P(),P("dp","mp"),P("mp"),P("mp","dp"),
                   cube,cols,lead,P(),P(),cols,P("mp"),lead),
        check_vma=False)
```

```python
import functools
import jax, jax.numpy as jnp
from jax import lax
from jax.experimental import pallas as pl
from jax.experimental.pallas import tpu as pltpu
F32=jnp.float32; BF=jnp.bfloat16
NT=(((1,),(1,)),((),()))
TN=(((0,),(0,)),((),()))
def dot(a,b): return jnp.dot(a,b,preferred_element_type=F32)
def dotg(a,b,dn): return lax.dot_general(a,b,dn,preferred_element_type=F32)
VLIM=60*1024*1024
SMALL=36*1024*1024

def cost(us): return pl.CostEstimate(flops=int(us*1e7),bytes_accessed=1024,transcendentals=0)

def lane_iota(shape): return lax.broadcasted_iota(jnp.int32,shape,len(shape)-1)

def row_masks():
    i=lax.broadcasted_iota(jnp.int32,(1,128),1)
    return lambda f: jnp.where(f(i),1.0,0.0).astype(BF)


def attn_fwd_kernel(first, len_ref, half_ref, xt_ref, xl_ref, wt_ref, wl_ref, bt_ref, bl_ref, *rest):
    qt_ref, kt_ref, vt_ref, ql_ref, kl_ref, vl_ref, ot_ref, ol_ref, lse_ref, olT, lseT=rest[-11:]
    page=first+pl.program_id(0)
    seq=xt_ref.shape[0]
    xt=xt_ref[...]; xl=xl_ref[...]
    for c,(t,l) in enumerate(((qt_ref,ql_ref),(kt_ref,kl_ref),(vt_ref,vl_ref))):
        t[...]=(dot(xt,wt_ref[c])+bt_ref[c:c+1,:]).astype(BF)
        l[...]=(dot(xl,wl_ref[c])+bl_ref[c:c+1,:]).astype(BF)
    lane=lane_iota((seq,128))
    row=lax.broadcasted_iota(jnp.int32,(seq,128),0)
    length=len_ref[page]
    bias=jnp.where(row<length,0.0,-1e9).astype(BF)
    one=jnp.ones((seq,128),BF)
    ql=jnp.where(lane==96,one,ql_ref[...]*BF(0.25))
    kl=jnp.where(lane==96,bias,kl_ref[...])
    vlT=vl_ref[...].T; qlT=ql.T
    keep=row_masks()
    olT[...]=jnp.zeros_like(olT); lseT[...]=jnp.zeros_like(lseT)
    def scores(h):
        j,s=h//2,h%2
        cols=slice(128*j,128*j+128)
        qbig=jnp.concatenate([(qt_ref[:,cols]*BF(0.125)).T,qlT],0)
        kbig=jnp.concatenate([kt_ref[:,cols]*keep(lambda i: i//64==s),kl*keep(lambda i: (i//16==h)|(i==96))],1)
        return dot(kbig,qbig)
    halves=[]
    def finish(h,e,m,ssum):
        j,s=h//2,h%2
        vT=vt_ref[:,128*j:128*j+128].T
        v80=jnp.concatenate([vT[64*s:64*s+64],vlT[16*h:16*h+16]],0)
        o=dot(v80,e)*(1.0/ssum)
        halves.append(o[:64])
        olT[16*h:16*h+16,:]=o[64:]
        lseT[h:h+1,:]=m+jnp.log(ssum)
        if s==1: ot_ref[:,128*j:128*j+128]=jnp.concatenate(halves[-2:],0).T.astype(BF)
    ahead=scores(0); behind=None
    for h in range(6):
        S=ahead
        if h<5: ahead=scores(h+1)
        if behind is not None: finish(*behind)
        m=jnp.max(S,0,keepdims=True)
        e=jnp.exp(S-m)
        behind=(h,e.astype(BF),m,jnp.sum(e,0,keepdims=True))
    finish(*behind)
    ol_ref[...]=olT[...].T.astype(BF)
    lse_ref[...]=pltpu.roll(lseT[...].T,97,1)

def attn_fwd(first, count, lengths, half, xt, xl, wt, wl, bt, bl, prev):
    rows=xt.shape[0]; pages=lengths.shape[0]; seq=rows//pages
    rb=lambda n: pl.BlockSpec((seq,n),lambda p,*_:(first+p,0))
    full=lambda a: pl.BlockSpec((None,)*(a.ndim-3)+a.shape[-3:],lambda p,l,h:(h[0],0,0,0)[4-a.ndim:]) if a.ndim>2 else pl.BlockSpec(a.shape,lambda p,*_:(0,0))
    whole=pl.BlockSpec(memory_space=pl.ANY)
    o=lambda n,d=BF: jax.ShapeDtypeStruct((rows,n),d)
    return pl.pallas_call(functools.partial(attn_fwd_kernel,first),
        grid_spec=pltpu.PrefetchScalarGridSpec(num_scalar_prefetch=2,grid=(count,),
            in_specs=[rb(768),rb(192),full(wt),full(wl),full(bt),full(bl)]+[whole]*len(prev),
            out_specs=[rb(384)]*3+[rb(128)]*3+[rb(384),rb(128),rb(128)],
            scratch_shapes=[pltpu.VMEM((128,seq),F32),pltpu.VMEM((128,seq),F32)]),
        out_shape=[o(384)]*3+[o(128)]*3+[o(384),o(128),o(128,F32)],
        input_output_aliases={8+i:i for i in range(len(prev))},
        compiler_params=pltpu.CompilerParams(vmem_limit_bytes=VLIM),cost_estimate=cost(6.2*count),name="attn_fwd")(lengths,half,xt,xl,wt,wl,bt,bl,*prev)

def ind_matrix(j):
    r=lax.broadcasted_iota(jnp.int32,(256,128),0)%128
    l=lax.broadcasted_iota(jnp.int32,(256,128),1)
    h=(r//64+2*j) if j is not None else r//16
    return jnp.where((l==97+h)&(h<6),1.0,0.0).astype(BF)

def split2(v):
    hi=v.astype(BF)
    return hi,(v-hi.astype(F32)).astype(BF)

def bwd_page(length, qt_ref, kt_ref, vt_ref, ql_ref, kl_ref, vl_ref, ot_ref, ol_ref, lse_ref, dot_ref, dol_ref,
                    dpt_ref, dpl_ref, dqlT, lay):
    seq=qt_ref.shape[0]
    lane=lane_iota((seq,128))
    row=lax.broadcasted_iota(jnp.int32,(seq,128),0)
    bias=jnp.where(row<length,0.0,-1e9).astype(BF)
    zero=jnp.zeros((seq,128),BF); one=jnp.ones((seq,128),BF)
    nl=-lse_ref[...]
    hi=nl.astype(BF); r1=nl-hi.astype(F32); mid=r1.astype(BF); lo=r1-mid.astype(F32)
    ext=hi+pltpu.roll(mid.astype(F32),7,1).astype(BF)+pltpu.roll(lo,14,1).astype(BF)
    qle=jnp.where(lane<96,ql_ref[...]*BF(0.25),jnp.where(lane==96,one,ext))
    kl=kl_ref[...]; vl=vl_ref[...]; ql=ql_ref[...]
    klT=kl.T
    dqlT[...]=jnp.zeros_like(dqlT)
    def sums(a,b,m):
        p=a.astype(F32)*b.astype(F32)
        h_,l_=split2(p)
        return dot(jnp.concatenate([h_,l_],1),m)
    dol=dol_ref[...]
    d_l=sums(dol,ol_ref[...],ind_matrix(None))
    d_t=d_l
    for j in range(3):
        cols=slice(128*j,128*j+128)
        d_t=d_t+sums(dot_ref[:,cols],ot_ref[:,cols],ind_matrix(j))
    def ext_delta(d):
        h_=d.astype(BF); l_=d-h_.astype(F32)
        return h_+pltpu.roll(l_,7,1).astype(BF)
    dol1=jnp.where(lane<96,dol*BF(0.125),ext_delta(d_t*-0.125))
    dol2=jnp.where(lane<96,dol*BF(0.25),ext_delta(d_l*-0.25))
    keep=row_masks()
    kle=jnp.where(lane==96,bias,jnp.where(lane>96,one,kl))
    vle=jnp.where(lane>96,one,vl)
    qleT=qle.T; dol1T=dol1.T; dol2T=dol2.T
    rows2=lambda x,masks: jnp.concatenate([x*m for m in masks],0)
    for j in range(3):
        cols=slice(128*j,128*j+128)
        qt=qt_ref[:,cols]; kt=kt_ref[:,cols]; vt=vt_ref[:,cols]; dO=dot_ref[:,cols]
        qbig=jnp.concatenate([(qt*BF(0.125)).T,qleT],0)
        dbig=jnp.concatenate([(dO*BF(0.125)).T,dol1T],0)
        ktT=kt.T
        heads=(2*j,2*j+1)
        tms=[keep(lambda i: i//64==s) for s in range(2)]
        lms=[keep(lambda i: i//16==h) for h in heads]
        R1s=[]; R2s=[]; Ps=[]; dqs=[]
        for s,h in enumerate(heads):
            kbig=jnp.concatenate([kt*tms[s],kle*keep(lambda i: (i//16==h)|(i==96)|(i==97+h)|(i==104+h)|(i==111+h))],1)
            vleh=vle*keep(lambda i: (i//16==h)|(i==97+h)|(i==104+h))
            vbig=jnp.concatenate([vt*tms[s],vleh],1)
            S=dot(kbig,qbig)
            M1=dot(vbig,dbig)
            M2=dot(vleh,dol2T)
            Pm=jnp.exp(S)
            R1=(Pm*M1).astype(BF); R2=(Pm*M2).astype(BF)
            Ps.append(Pm.astype(BF)); R1s.append(R1); R2s.append(R2)
            dqs.append(dot(ktT[64*s:64*s+64],R1))
            dqlT[16*h:16*h+16,:]=dot(klT[16*h:16*h+16],R2)
        dpt_ref[0,:,cols]=jnp.concatenate(dqs,0).T.astype(BF)
        dpt_ref[1,:,cols]=dot(jnp.concatenate(R1s,1),rows2(qt,tms)).astype(BF)
        dv=dot(jnp.concatenate(Ps,1),jnp.concatenate([rows2(dO,tms),rows2(dol,lms)],1))
        dpt_ref[2,:,cols]=dv[:,:128].astype(BF)
        dkl=dot(jnp.concatenate(R2s,1),rows2(ql,lms))
        if j==0: lay[0]=dkl; lay[1]=dv[:,128:]
        else: lay[0]+=dkl; lay[1]+=dv[:,128:]
    dpl_ref[0]=dqlT[...].T.astype(BF)
    dpl_ref[1]=lay[0].astype(BF); dpl_ref[2]=lay[1].astype(BF)


def bwd_kernel(first, len_ref, half_ref, qt, kt, vt, ql, kl, vl, ot, ol, lse, dO, dOl, *rest):
    dpt,dpl,dqlT,lay=rest[-4:]
    bwd_page(len_ref[first+pl.program_id(0)],qt,kt,vt,ql,kl,vl,ot,ol,lse,dO.at[0],dOl.at[0],dpt,dpl,dqlT,lay)


def attn_bwd(first,count,lengths,half,saved,dO,dOl,prev):
    rows=saved[0].shape[0]; seq=rows//lengths.shape[0]
    rb=lambda n: pl.BlockSpec((seq,n),lambda i,*_:(first+i,0))
    hb=lambda n: pl.BlockSpec((1,seq,n),lambda i,l,h:(h[0],first+i,0))
    pb=lambda n: pl.BlockSpec((3,seq,n),lambda i,l,h:(h[0],first+i,0))
    whole=pl.BlockSpec(memory_space=pl.ANY)
    return pl.pallas_call(functools.partial(bwd_kernel,first),
        grid_spec=pltpu.PrefetchScalarGridSpec(num_scalar_prefetch=2,grid=(count,),
            in_specs=[rb(384)]*3+[rb(128)]*3+[rb(384),rb(128),rb(128),hb(384),hb(128)]+[whole]*len(prev),
            out_specs=[pb(384),pb(128)],scratch_shapes=[pltpu.VMEM((128,seq),F32),pltpu.VMEM((2,seq,128),F32)]),
        out_shape=[jax.ShapeDtypeStruct((6,rows,384),BF),jax.ShapeDtypeStruct((6,rows,128),BF)],
        input_output_aliases={13+i:i for i in range(len(prev))},
        compiler_params=pltpu.CompilerParams(vmem_limit_bytes=SMALL if prev else VLIM),cost_estimate=cost(9*count),name="attn_bwd")(lengths,half,*saved,dO,dOl,*prev)


def dx_kernel(dpt, dpl, wt, wl, dr1, dr1l, sel, dx, dxl, wts, wls):
    @pl.when(pl.program_id(0)==0)
    def _():
        for h in range(2):
            for c in range(3):
                i=3*h+c
                wts[:,384*i:384*i+384]=wt[h,c]
                wls[:,128*i:128*i+128]=wl[h,c]
    def back(d,w,base,flag):
        v=dotg(jnp.concatenate([d[i] for i in range(6)],1),w[...],NT)+base[...]
        return jnp.where(flag>0.5,0.0,v)
    flags=sel[...].astype(F32).T
    dx[...]=back(dpt,wts,dr1,flags[:,1:2])
    dxl[...]=back(dpl,wls,dr1l,flags[:,2:3]).T


def input_grad(tile,dp,wts,dr1,dr1l,sel):
    rows=dr1.shape[0]
    rb=lambda n: pl.BlockSpec((tile,n),lambda i:(i,0))
    pb=lambda n: pl.BlockSpec((6,tile,n),lambda i:(0,i,0))
    full=lambda a: pl.BlockSpec(a.shape,lambda i:(0,0,0,0))
    return pl.pallas_call(dx_kernel,grid=(rows//tile,),
        in_specs=[pb(384),pb(128)]+[full(w) for w in wts]+[rb(768),rb(192),pl.BlockSpec((8,tile),lambda i:(0,i))],
        out_specs=[rb(768),pl.BlockSpec((192,tile),lambda i:(0,i))],
        scratch_shapes=[pltpu.VMEM((768,2304),BF),pltpu.VMEM((192,768),BF)],
        out_shape=[jax.ShapeDtypeStruct((rows,768),F32),jax.ShapeDtypeStruct((192,rows),F32)],
        compiler_params=pltpu.CompilerParams(vmem_limit_bytes=44*1024*1024),cost_estimate=cost(5),name="input_grad")(*dp,*wts,dr1,dr1l,sel)


def move_blocks(acc, keep, send, sem, position, n, left, width, start):
    cols=pl.ds(left,width)
    if n!=16:
        cp=pltpu.make_async_copy(acc,keep.at[:,cols],sem)
        if start: cp.start()
        else: cp.wait()
        return
    c=position&1; x=(position>>1)&1; z0=(position>>2)&1; z1=(position>>3)&1
    rows=acc.shape[0]//16
    for out,core in ((keep,c),(send,1-c)):
        for q in range(8):
            r2,r3,r4=q>>2,(q>>1)&1,q&1
            fx=jnp.where(core==0,r2,r3); fz=jnp.where(core==0,r3,r2)
            block=(z1^r4)*8+(z0^fz)*4+(x^fx)*2+core
            cp=pltpu.make_async_copy(acc.at[pl.ds(pl.multiple_of(block*rows,8),rows)],out.at[pl.ds(q*rows,rows),cols],sem)
            if start: cp.start()
            else: cp.wait()


def place_blocks(acc, keep, send, sem, position, n):
    for start in (True,False): move_blocks(acc,keep,send,sem,position,n,0,acc.shape[1],start)


def block_shapes(rows,cols,n):
    S=jax.ShapeDtypeStruct
    if n!=16: return [S((rows,cols),F32),S((8,128),F32)]
    return [S((rows//2,cols),F32)]*2


def qkv_grad_kernel(n, pos_ref, xt, xl, dpt, dpl, sel, wt, wl, st, bst, keep, send, acc, sums, suml, sem):
    x=xt[...]; s=sel[...]; xv=xl[...]
    def add(first):
        def put(ref,v):
            if first: ref[...]=v
            else: ref[...]+=v
        cat=lambda d: jnp.concatenate([d[0],d[1],d[2]],1)
        t=cat(dpt); l=cat(dpl)
        put(acc.at[:,:1152],dotg(x,t,TN))
        g=dotg(xv,l,TN); a=dot(s,t); b=dot(s,l)
        for c in range(3):
            put(acc.at[192*c:192*c+192,1152:1280],g[:,128*c:128*c+128])
            put(sums.at[c],a[:,384*c:384*c+384]); put(suml.at[c],b[:,128*c:128*c+128])
    first=pl.program_id(0)==0
    pl.when(first)(lambda: add(True))
    pl.when(jnp.logical_not(first))(lambda: add(False))
    @pl.when(pl.program_id(0)==pl.num_programs(0)-1)
    def _():
        t=jnp.zeros((8,768),F32); l=jnp.zeros((8,192),F32)
        for c in range(3):
            for v,w,text in ((sums[c],wt,True),(suml[c],wl,False)):
                hi,lo=split2(v)
                lo2=(v-hi.astype(F32)-lo.astype(F32)).astype(BF)
                y=dotg(jnp.concatenate([hi,lo,lo2],0),w[0,c],NT)
                y=y[0:8]+y[8:16]+y[16:24]
                if text: t=t+y
                else: l=l+y
        acc[576:768,1152:1280]=jnp.zeros((192,128),F32)
        rows=[st[i:i+1,128*j:128*j+128] for i in range(7) for j in range(6)]+[bst[0:1,128*j:128*j+128] for j in range(12)]
        rows+=[sums[c][0:1,128*j:128*j+128] for c in (0,2) for j in range(3)]+[suml[c][0:1] for c in (0,2)]
        rows+=[t[1:2,128*j:128*j+128] for j in range(6)]+[l[2:3,0:128],jnp.concatenate([l[2:3,128:],jnp.zeros((1,64),F32)],1)]
        for i,v in enumerate(rows): acc[576+i:577+i,1152:1280]=v
        place_blocks(acc,keep,send,sem,pos_ref[1],n)


def qkv_grad(n,pos,pages,xt,xl,dpt,dpl,sel,wt,wl,st,bst):
    seq=xt.shape[0]//pages
    rb=lambda m: pl.BlockSpec((seq,m),lambda i,s:(i,0))
    pb=lambda m: pl.BlockSpec((3,seq,m),lambda i,s:(s[0],i,0))
    wb=lambda a: pl.BlockSpec((1,)+a.shape[1:],lambda i,s:(s[0],0,0,0))
    whole=pl.BlockSpec(memory_space=pl.ANY)
    return pl.pallas_call(functools.partial(qkv_grad_kernel,n),
        grid_spec=pltpu.PrefetchScalarGridSpec(num_scalar_prefetch=1,grid=(pages,),
            in_specs=[rb(768),rb(192),pb(384),pb(128),pl.BlockSpec((8,seq),lambda i,s:(0,i)),wb(wt),wb(wl)]+[pl.BlockSpec(a.shape,lambda i,s:(0,0)) for a in (st,bst)],
            out_specs=[whole,whole],
            scratch_shapes=[pltpu.VMEM((768,1280),F32),pltpu.VMEM((3,8,384),F32),pltpu.VMEM((3,8,128),F32),pltpu.SemaphoreType.DMA]),
        out_shape=block_shapes(768,1280,n),
        compiler_params=pltpu.CompilerParams(vmem_limit_bytes=SMALL),cost_estimate=cost(8),name="qkv_grad")(pos,xt,xl,dpt,dpl,sel,wt,wl,st,bst)


EPS=1e-5
def gelu_parts(x):
    cdf=0.5+0.5*lax.erf(x*0.7071067811865476)
    phi=jnp.exp2(x*x*-0.7213475204444817-1.3257480647361593)
    return cdf, cdf+x*phi

def norm(v):
    mu=jnp.mean(v,-1,keepdims=True)
    c=v-mu
    inv=lax.rsqrt(jnp.mean(c*c,-1,keepdims=True)+EPS)
    return c*inv,inv

def norm_back(g,u,inv,gain):
    s=g*gain
    return inv*(s-jnp.mean(s,-1,keepdims=True)-u*jnp.mean(s*u,-1,keepdims=True))

def stream(own_off, x, o, o_own, cot, outw, up, down, shift, gain, upb, act, gp, out_ref, dr1_ref, dos, gup, gdn, gout, stat, bstat, chunk, flag, kept=None):
    d=x.shape[1]; F=up.shape[1]; half=F//2
    h1u,i1=norm(x.astype(F32)+dot(o,outw[...])+shift[2:3])
    h1=h1u*gain[0:1]+shift[0:1]
    h1b=h1.astype(BF)
    yield
    def units(i,carry):
        cs=pl.ds(pl.multiple_of(i*chunk,chunk),chunk)
        pre=dot(h1b,up[:,cs])+upb[:,cs]
        cdf,der=gelu_parts(pre)
        act[:,cs]=(pre*cdf).astype(BF)
        gp[:,cs]=der.astype(BF)
        return carry
    lax.fori_loop(0,F//chunk,units,0)
    yield
    r2=h1+dot(act[...],down[...])+shift[3:4]
    u2,i2=norm(r2)
    y=u2*gain[1:2]+shift[1:2]
    out_ref[...]=y if out_ref.shape==y.shape else y.T
    g=cot.astype(F32)
    dr2=norm_back(g,u2,i2,gain[1:2])
    dr2b=dr2.astype(BF)
    def units_back(i,carry):
        cs=pl.ds(pl.multiple_of(i*chunk,chunk),chunk)
        da=dotg(dr2b,down[cs,:],NT)
        gp[:,cs]=(da*gp[:,cs].astype(F32)).astype(BF)
        return carry
    lax.fori_loop(0,F//chunk,units_back,0)
    dh1=dotg(gp[...],up[...],NT)+dr2
    dr1=norm_back(dh1,h1u,i1,gain[0:1])
    dr1_ref[...]=dr1
    dr1b=dr1.astype(BF)
    dO=dotg(dr1b,outw[...],NT).astype(BF)
    w=dO.shape[1]//2
    dos[0]=dO[:,:w]; dos[1]=dO[:,w:]
    osl=pl.ds(pl.multiple_of(own_off,128),half)
    dpo=gp[:,osl]
    rs=lambda v: jnp.sum(v,0,keepdims=True)
    stat[...]+=jnp.concatenate([rs(dh1),rs(g),rs(dr1),rs(dr2),rs(dh1*h1u),rs(g*u2),rs(jnp.where(flag>0.5,dr1,0.0)),jnp.zeros((1,d),F32)],0)
    bstat[...]+=dot(jnp.ones((8,x.shape[0]),BF),dpo)
    if kept is not None:
        for ref,v in zip(kept,(h1b,dr2b,dr1b,o_own)): ref[...]=v
    else:
        gup[...]+=dotg(h1b,dpo,TN)
        gdn[...]+=dotg(dr2b,act[:,osl],TN)
        gout[...]+=dotg(dr1b,o_own,TN)
    yield


def halves_of(mp, a, b):
    a=a[...]; b=b[...]
    z=mp==0
    return jnp.concatenate([jnp.where(z,a,b),jnp.where(z,b,a)],1)


def half(k, m): return pl.ds(pl.multiple_of(k*m,m),m)


def side_kernel(s_ref, xl, ola, olb, cl, lm, little, shl, gal, outl_own, upl_own, downl_own, upbl_own, pa, pb, pc, pd,
                lo, dr1l, dosl, extra, actl, gpl, outwl, upl, downl, upbl, gupl, gdnl, goutl, stl, bstl, outs):
    mp=s_ref[0]; other=1-mp
    @pl.when(pl.program_id(0)==0)
    def _():
        upbl[:,half(mp,384)]=upbl_own[...]
        upl[:,half(mp,384)]=upl_own[...]
        downl[half(mp,384),:]=downl_own[...]
        outwl[half(mp,128),:]=jnp.concatenate([outl_own[...],jnp.zeros((32,192),BF)],0)
        outs[...]=jnp.zeros_like(outs)
        for i,v in enumerate((pa,pb,pc,pd)):
            p=s_ref[2+i]
            rows=pl.ds(pl.multiple_of(p*24,8),24)
            outs[rows,0:128]=v[0:24]; outs[rows,128:192]=v[24:48,0:64]
            for j in range(3):
                upl[half(p,48),pl.ds(pl.multiple_of(other*384+128*j,128),128)]=v[48+48*j:96+48*j].astype(BF)
            rows=pl.ds(pl.multiple_of(other*384+p*96,16),96)
            downl[rows,0:128]=v[192:288].astype(BF)
            downl[rows,128:192]=v[288:384,0:64].astype(BF)
        outwl[half(other,128),:]=outs[...].astype(BF)
        for j in range(3):
            upbl[:,pl.ds(pl.multiple_of(other*384+128*j,128),128)]=little[12+j:13+j]
        for ref in (gupl,gdnl,goutl,stl,bstl): ref[...]=jnp.zeros_like(ref)
    phases=stream(mp*384,xl[...],halves_of(mp,ola,olb),ola[...],cl[...].T,outwl,upl,downl,shl,gal,upbl,actl,gpl,lo,dr1l,dosl,gupl,gdnl,goutl,stl,bstl,768,lm[...].astype(F32).T[:,2:3])
    next(phases); next(phases); next(phases)
    @pl.when(pl.program_id(0)==pl.num_programs(0)-1)
    def _():
        blocks=[gupl[:,128*j:128*j+128] for j in range(3)]+[gdnl[:,128*j:128*j+128] for j in range(3)]+[goutl[...]]
        rest=[stl[:,0:128],jnp.concatenate([stl[:,128:192],jnp.zeros((8,64),F32)],1)]
        rest+=[bstl[:,128*j:128*j+128] for j in range(3)]+[jnp.zeros((152,128),F32)]
        blocks.append(jnp.concatenate(rest,0))
        for i,v in enumerate(blocks):
            extra[192*(i%4):192*(i%4)+192,128*(i//4):128*(i//4)+128]=v


def side(scal,xl,ola,olb,cl,lm,little,params,own,pieces,tile=768):
    rows=xl.shape[0]
    rb=lambda n: pl.BlockSpec((tile,n),lambda p,*_:(p,0))
    cb=pl.BlockSpec((192,tile),lambda p,*_:(0,p))
    full=lambda a: pl.BlockSpec(a.shape,lambda p,*_:(0,)*len(a.shape))
    S=jax.ShapeDtypeStruct; V=pltpu.VMEM
    last=pl.BlockSpec((400,128),lambda p,*_:(0,0))
    return pl.pallas_call(side_kernel,
        grid_spec=pltpu.PrefetchScalarGridSpec(num_scalar_prefetch=1,grid=(rows//tile,),
            in_specs=[rb(192),rb(128),rb(128),cb,pl.BlockSpec((8,tile),lambda p,*_:(0,p)),pl.BlockSpec((16,128),lambda p,*_:(36,0))]+[full(a) for a in params+own]+[last]*4,
            out_specs=[cb,rb(192),pl.BlockSpec((2,tile,128),lambda p,*_:(0,p,0)),pl.BlockSpec((768,256),lambda p,*_:(0,0))],
            scratch_shapes=[V((tile,768),BF),V((tile,768),BF),V((256,192),BF),V((192,768),BF),V((768,192),BF),V((1,768),F32),
                V((192,384),F32),V((192,384),F32),V((192,128),F32),V((8,192),F32),V((8,384),F32),V((128,192),F32)]),
        out_shape=[S((192,rows),F32),S((rows,192),F32),S((2,rows,128),BF),S((768,256),F32)],
        compiler_params=pltpu.CompilerParams(vmem_limit_bytes=VLIM),cost_estimate=cost(10),name="side")(scal,xl,ola,olb,cl,lm,little,*params,*own,*pieces)


def ffn_kernel(n, s_ref, *refs):
    (xt, oa, ob, ct, tm, sh, ga, upb_own)=refs[:8]
    (up_own, outw_own, down_own)=refs[8:11]
    second=refs[11:19]; third=[refs[19+2*i:21+2*i] for i in range(4)]; extra=refs[27]
    (to, dr1, dos, keep, send, st, bst)=refs[28:35]
    (act2, gp2, hb2, rb2, sb2, ob2, acc, up, outw, down, upb, gbias, sem, sem_own, sem2, sem3, sem4)=refs[35:]
    step=pl.program_id(0); odd=step%2; tile=xt.shape[0]
    part=pl.ds(pl.multiple_of(odd*tile,tile),tile)
    act=act2.at[part]; gp=gp2.at[part]
    mp=s_ref[0]; other=1-mp
    first=pl.program_id(0)==0
    column=lambda k: acc.at[:,128*k:128*k+128]
    own=[pltpu.make_async_copy(src,dst,sem_own.at[i]) for i,(src,dst) in enumerate((
        (outw_own,outw.at[half(mp,384),:]),(up_own,up.at[:,half(mp,1536)]),(down_own,down.at[half(mp,1536),:])))]
    two=[]; three=[]
    for i,src in enumerate(second):
        two.append([pltpu.make_async_copy(src.at[a:b],column(2*i+k).at[0:b-a],sem2.at[i,k]) for k,(a,b) in enumerate(((0,768),(768,1152)))])
    outs=[]
    for i,src in enumerate(third):
        base=16+4*i if i<3 else 0
        three.append([pltpu.make_async_copy(src[s].at[r:r+768],column(base+k),sem3.at[i,k]) for k,(s,r) in enumerate(((0,0),(1,592),(1,1360)))])
        outs.append(pltpu.make_async_copy(src[1].at[0:576],column(19+4*i if i<3 else 28).at[0:576],sem3.at[i,3]))
    bias=[pltpu.make_async_copy(third[0][1].at[576:592],gbias,sem4)]
    @pl.when(first)
    def _():
        for cp in outs+own[:1]+bias: cp.start()
        for cps in two:
            for cp in cps: cp.start()
        own[1].start()
        for cps in three[:3]:
            for cp in cps: cp.start()
        own[2].start()
        for cp in outs: cp.wait()
        for i in range(4):
            for j in range(6):
                v=column(19+4*i if i<3 else 28)[96*j:96*j+96]
                outw[pl.ds(pl.multiple_of(other*384+s_ref[2+i]*96,16),96),128*j:128*j+128]=v.astype(BF)
        own[0].wait()
    phases=stream(mp*1536,xt[...],halves_of(mp,oa,ob),oa[...],ct[...],outw,up,down,sh,ga,upb,act,gp,to,dr1,dos,
        None,None,None,st,bst,1536,tm[...].astype(F32).T[:,1:2],[r.at[part] for r in (hb2,rb2,sb2,ob2)])
    next(phases)
    @pl.when(first)
    def _():
        for cps in two:
            for cp in cps: cp.wait()
        def unpack_second(i,carry):
            p=s_ref[6+i]
            left=pl.ds(pl.multiple_of(256*i,128),128); right=pl.ds(pl.multiple_of(256*i+128,128),128)
            for j in range(12):
                v=acc[96*j:96*j+96,left] if j<8 else acc[96*(j-8):96*(j-8)+96,right]
                up[half(p,96),pl.ds(pl.multiple_of(other*1536+128*j,128),128)]=v.astype(BF)
            return carry
        lax.fori_loop(0,8,unpack_second,0)
        for cp in three[3]: cp.start()
        bias[0].wait()
        for j in range(12):
            upb[:,pl.ds(pl.multiple_of(other*1536+128*j,128),128)]=gbias[j:j+1]
        upb[:,half(mp,1536)]=upb_own[...]
        own[1].wait()
    next(phases)
    @pl.when(first)
    def _():
        own[2].wait()
        for cps in three:
            for cp in cps: cp.wait()
        def unpack_third(i,carry):
            p=s_ref[2+i]
            base=jnp.where(i<3,2048+512*i,0)
            for j in range(6):
                v=acc[384*(j%2):384*(j%2)+384,pl.ds(pl.multiple_of(base+128*(j//2),128),128)]
                down[pl.ds(pl.multiple_of(other*1536+p*384,16),384),128*j:128*j+128]=v.astype(BF)
            return carry
        lax.fori_loop(0,4,unpack_third,0)
        def clear(i,carry):
            acc[pl.ds(pl.multiple_of(16*i,16),16),:]=jnp.zeros((16,acc.shape[1]),F32)
            return carry
        lax.fori_loop(0,48,clear,0)
        st[...]=jnp.zeros_like(st); bst[...]=jnp.zeros_like(bst)
    next(phases)
    last=step==pl.num_programs(0)-1
    osl=half(mp,1536)
    copies=[]
    def into(left,width,lhs,rhs):
        acc[:,left:left+width]+=dotg(lhs,rhs,TN)
        @pl.when(last)
        def _(): move_blocks(acc.at[:,left:left+width],keep,send,sem,s_ref[1],n,left,width,True)
    @pl.when(odd==1)
    def _():
        @pl.when(last)
        def _():
            cp=pltpu.make_async_copy(extra,acc.at[:,3456:3712],sem4)
            cp.start(); cp.wait()
            move_blocks(acc.at[:,3456:3712],keep,send,sem,s_ref[1],n,3456,256,True)
        into(0,1536,hb2[...],gp2[:,osl])
        into(1536,1536,rb2[...],act2[:,osl])
        into(3072,384,sb2[...],ob2[...])
        @pl.when(last)
        def _(): move_blocks(acc,keep,send,sem,s_ref[1],n,0,3712,False)


def ffn(n,scal,rowed,params,own,second,third,extra,tile=384):
    rows=rowed[0].shape[0]
    rb=lambda a: pl.BlockSpec((tile,a.shape[1]),lambda p,*_:(p,0))
    full=lambda a: pl.BlockSpec(a.shape,lambda p,*_:(0,)*len(a.shape),pipeline_mode=pl.Buffered(1))
    whole=pl.BlockSpec(memory_space=pl.ANY)
    S=jax.ShapeDtypeStruct; V=pltpu.VMEM; D=pltpu.SemaphoreType.DMA
    rowout=[S((rows,768),F32),S((rows,768),F32)]
    dos=[S((2,rows,384),BF)]
    return pl.pallas_call(functools.partial(ffn_kernel,n),
        grid_spec=pltpu.PrefetchScalarGridSpec(num_scalar_prefetch=1,grid=(rows//tile,),
            in_specs=[rb(a) for a in rowed[:-1]]+[pl.BlockSpec((8,tile),lambda p,*_:(0,p))]+[full(w) for w in params]+[whole]*(len(own)+17),
            out_specs=[rb(a) for a in rowout]+[pl.BlockSpec((2,tile,384),lambda p,*_:(0,p,0)),whole,whole]+[pl.BlockSpec((8,m),lambda p,*_:(0,0)) for m in (768,1536)],
            scratch_shapes=[V((2*tile,3072),BF),V((2*tile,3072),BF),V((2*tile,768),BF),V((2*tile,768),BF),V((2*tile,768),BF),V((2*tile,384),BF),V((768,3712),F32),V((768,3072),BF),V((768,768),BF),V((3072,768),BF),
                V((1,3072),F32),V((16,128),F32),D,D((3,)),D((8,2)),D((4,4)),D]),
        out_shape=rowout+dos+block_shapes(768,3712,n)+[S((8,768),F32),S((8,1536),F32)],
        compiler_params=pltpu.CompilerParams(vmem_limit_bytes=VLIM),cost_estimate=cost(80),name="middle")(scal,*rowed,*params,*own,*second,*[v for pair in third for v in pair],extra)


from jax.sharding import PartitionSpec as P


def pack_kernel(starts, idx_ref, *refs):
    out=refs[-1]
    out[...]=jnp.zeros_like(out)
    r=0
    for k,src in enumerate(refs[:-1]):
        r=starts.get(k,r)
        lead=src.shape[0] if len(src.shape)==3 else None
        for c in range(lead or 1):
            w=src[c] if lead else src[...]
            n,m=w.shape
            for j in range(0,m,128):
                e=min(128,m-j)
                out[r:r+n,:e]=w[:,j:j+e].astype(F32)
                r+=n


def pack(idx, groups, parts):
    specs=[]; n=0; arrays=[]; starts=[]
    for split,whole in groups:
        starts.append((len(arrays),n))
        split=[a if isinstance(a,tuple) else (a,(0,1)) for a in split]
        for a,part in split:
            rows=a.shape[-2]//parts
            width=a.shape[-1]//part[1]
            blocks=-(-width//128)
            if a.ndim==3:
                specs.append(pl.BlockSpec((a.shape[0],rows,a.shape[2]),lambda i,s:(0,s[0],0)))
                n+=a.shape[0]*rows*blocks
            else:
                specs.append(pl.BlockSpec((rows,width),functools.partial(lambda k,i,s:(s[0],k),part[0])))
                n+=rows*blocks
        for a in whole:
            specs.append(pl.BlockSpec(a.shape,lambda i,s:(0,0)))
            n+=a.shape[0]*(-(-a.shape[1]//128))
        n=-(-n//8)*8
        arrays+=[a for a,_ in split]+whole
    return pl.pallas_call(functools.partial(pack_kernel,dict(starts)),
        grid_spec=pltpu.PrefetchScalarGridSpec(num_scalar_prefetch=1,grid=(1,),in_specs=specs,
            out_specs=pl.BlockSpec((n,128),lambda i,s:(0,0))),
        out_shape=jax.ShapeDtypeStruct((n,128),F32),
        compiler_params=pltpu.CompilerParams(vmem_limit_bytes=VLIM),cost_estimate=cost(2),name="pack")(idx,*arrays)


def unpack_first_kernel(s_ref, pa, pb, pc, pd, wt_own, wl_own, wt, wl, bt, bl):
    mine=s_ref[0]; other=1-mine
    wl[...]=jnp.zeros_like(wl)
    wt[mine]=wt_own[...]
    wl[mine]=wl_own[...]
    bt[...]=jnp.zeros_like(bt); bl[...]=jnp.zeros_like(bl)
    for p,ref in enumerate((pa,pb,pc,pd)):
        i=s_ref[2+p]
        at=lambda n: pl.ds(pl.multiple_of(i*n,n),n)
        r=400
        for c in range(3):
            for j in range(3):
                wt[other,c,at(192),128*j:128*j+128]=ref[r:r+192].astype(BF); r+=192
        for c in range(3):
            wl[other,c,at(48),:]=ref[r:r+48].astype(BF); r+=48
        if p==0:
            for c in range(2):
                for j in range(3):
                    bt[2*c:2*c+1,128*j:128*j+128]=ref[r+2*j+c:r+2*j+c+1]
            r+=6
            for c in range(2):
                bl[2*c:2*c+1,:]=ref[r+c:r+c+1]


def unpack_first(scal, pieces, wt, wl):
    S=jax.ShapeDtypeStruct
    full=lambda a: pl.BlockSpec(a.shape,lambda i,*_:(0,)*len(a.shape))
    outs=[S((2,3,768,384),BF),S((2,3,192,128),BF),S((3,384),F32),S((3,128),F32)]
    ins=[*pieces,wt,wl]
    return pl.pallas_call(unpack_first_kernel,
        grid_spec=pltpu.PrefetchScalarGridSpec(num_scalar_prefetch=1,grid=(1,),in_specs=[full(a) for a in ins],
            out_specs=[full(a) for a in outs]),
        out_shape=outs,compiler_params=pltpu.CompilerParams(vmem_limit_bytes=VLIM),cost_estimate=cost(4),name="unpack")(scal,*ins)


def flip(n, bit):
    return [(i,i^bit) for i in range(n)]


def cross(n, even, odd):
    return [(i,i^(even if i%2==0 else odd)) for i in range(n)]


def gather4(piece, n):
    a=lax.ppermute(piece,"mp",[(0,1),(1,0)])
    b=lax.ppermute(a,"dp",cross(n,2,4))
    c=lax.ppermute(a,"dp",flip(n,1))
    d=lax.ppermute(b,"dp",flip(n,1))
    return a,b,c,d


def gather8(piece, n):
    a=lax.ppermute(piece,"mp",[(0,1),(1,0)])
    b=lax.ppermute(a,"dp",cross(n,2,4))
    e=lax.ppermute(a,"dp",cross(n,4,2))
    f=lax.ppermute(b,"dp",cross(n,4,2))
    return (a,b,e,f)+tuple(lax.ppermute(v,"dp",flip(n,1)) for v in (a,b,e,f))


def ids8(dp):
    base=dp&7; odd=dp&1
    near=jnp.where(odd==0,2,4); far=6-near
    return [base,base^near,base^far,base^6,base^1,base^1^far,base^1^near,base^7]


def join(*values):
    return lax.optimization_barrier(values)


def stages(n):
    return (flip(n,1),cross(n,2,4),cross(n,4,2),flip(n,8))


def halve(keep, recv):
    half=keep.shape[0]//2
    return keep[:half]+recv[:half],keep[half:]+recv[half:]


def finish_kernel(order, c_ref, small, other, early, early_other, tv, lv, cs, sh, ga, bst, gl, csl, ol, shl, gal, ul, bl, dl, buf):
    rows=small.shape[1]
    for ref,ref2,(a,b) in ((small,other,((0,128),(384,512))),(early,early_other,((128,256),(256,384)))):
        if not order:
            v=ref[0]
            buf[:,a[0]:a[1]]=v[:,:128]; buf[:,b[0]:b[1]]=v[:,128:]
        low=c_ref[0]==0
        for i,k in enumerate(order):
            mine,got=ref[k],ref2[k]
            v=jnp.where(low,mine,got) if i%2==0 else jnp.where(low,got,mine)
            buf[rows*i:rows*i+rows,a[0]:a[1]]=v[:,:128]; buf[rows*i:rows*i+rows,b[0]:b[1]]=v[:,128:]
    block=lambda i: buf[192*(i%4):192*(i%4)+192,128+128*(i//4):256+128*(i//4)]
    for j in range(3):
        ul[:,128*j:128*j+128]=block(j)
        dl[:,128*j:128*j+128]=block(3+j)
        gl[j]=buf[192*j:192*j+192,0:96]
    ol[...]=block(6).T[0:96]
    last=block(7)
    for ref,r0 in ((shl,0),(gal,4)):
        n=ref.shape[0]
        ref[:,0:128]=last[r0:r0+n]; ref[:,128:192]=last[8+r0:8+r0+n,0:64]
    for j in range(3): bl[128*j:128*j+128]=last[16+8*j]
    row=lambda i,c=0: buf[576+i:577+i,128*c:128*c+128]
    for j in range(6):
        s=slice(128*j,128*j+128)
        for i in range(4): sh[i:i+1,s]=row(6*i+j)
        for i in range(2): ga[i:i+1,s]=row(24+6*i+j)
        tv[s]=((row(62+j)+row(62+j,3))+row(36+j))[0]
    for j in range(12): bst[128*j:128*j+128]=row(42+j)[0]
    for i in range(2):
        for j in range(3): cs[i:i+1,128*j:128*j+128]=row(54+3*i+j)
        csl[i:i+1,:]=row(60+i)[:,0:96]
    lv[0:128]=((row(68)+row(68,3))+last[6:7])[0]
    lv[128:192]=((row(69)+row(69,3))[:,0:64]+last[14:15,0:64])[0]


def finish(order, core, *parts):
    S=lambda *shape: jax.ShapeDtypeStruct(shape,F32)
    outs=[S(768),S(192),S(2,384),S(4,768),S(2,768),S(1536),S(3,192,96),S(2,96),S(96,192),S(4,192),S(2,192),S(192,384),S(384),S(192,384)]
    full=lambda a: pl.BlockSpec(a.shape,lambda i,*_:(0,)*len(a.shape))
    return pl.pallas_call(functools.partial(finish_kernel,order),
        grid_spec=pltpu.PrefetchScalarGridSpec(num_scalar_prefetch=1,grid=(1,),in_specs=[full(a) for a in parts],
            out_specs=[full(a) for a in outs],scratch_shapes=[pltpu.VMEM((768,512),F32)]),
        out_shape=outs,
        compiler_params=pltpu.CompilerParams(vmem_limit_bytes=VLIM),cost_estimate=cost(2),name="finish")(core,*parts)


def bias_rows(pair):
    b=pair.astype(F32)
    return jnp.stack([b[0],jnp.zeros_like(b[0]),b[1]])


def shards(text_in, layout_in, token_mask, box_mask, lengths, text_mask_vec, layout_mask_vec,
           text_qkv, text_qv_bias, text_out_w, text_shifts, text_gains, text_up, text_up_bias, text_down,
           layout_qkv, layout_qv_bias, layout_out_w, layout_shifts, layout_gains, layout_up, layout_up_bias, layout_down,
           text_cot, layout_cot):
    n=lax.axis_size("dp")
    mp=lax.axis_index("mp").astype(jnp.int32); dp=lax.axis_index("dp").astype(jnp.int32)
    core=dp&1; color=((dp>>1)^(dp>>2))&1
    ids=[2*color+core,2*(1-color)+core,2*color+1-core,2*(1-color)+1-core]
    scal=jnp.stack([mp,dp]+ids+ids8(dp))
    idx=ids[0][None]; idx8=(dp&7)[None]
    even_odd=cross(n,2,4); odd_even=cross(n,4,2); core_flip=flip(n,1)
    over=lambda v: lax.ppermute(v,"mp",[(0,1),(1,0)])
    send=lambda v,pairs: lax.ppermute(v,"dp",pairs)
    upb=text_up_bias.astype(F32)[None]; upbl=layout_up_bias.astype(F32)[None]
    p1=pack(idx,[([layout_out_w,layout_up,layout_down],[jnp.zeros((16,128),BF)]),([text_qkv,layout_qkv],[text_qv_bias,layout_qv_bias])],4)
    p2=pack(idx8,[([text_up],[])],8)
    p3=pack(idx,[([(text_down,(0,3))],[])],4)
    p4=pack(idx,[([text_out_w],[upb,upbl]),([(text_down,(1,3)),(text_down,(2,3))],[])],4)
    xt=jnp.where(token_mask[:,None]==1,text_mask_vec[None],text_in)
    xl=jnp.where(box_mask[:,None]==1,layout_mask_vec[None],layout_in)
    sel=jnp.concatenate([jnp.ones_like(token_mask)[None],(token_mask==1).astype(jnp.int32)[None],(box_mask==1).astype(jnp.int32)[None],
        jnp.zeros((5,token_mask.shape[0]),jnp.int32)],0).astype(BF)
    pad=lambda v: jnp.pad(v,((0,0),)*(v.ndim-1)+((0,32),))
    wl=pad(layout_qkv)
    a1=over(p1)
    bt=bias_rows(text_qv_bias); bl=pad(bias_rows(layout_qv_bias))
    pages=lengths.shape[0]
    forward=lambda first,count,x,w,prev: attn_fwd(first,count,lengths,1-mp[None],x,xl,*w,prev)
    xa,p2,sel=join(xt,p2,sel)
    w_own=(text_qkv,wl,bt,bl)
    own=forward(0,pages-1,xa,w_own,())
    own,a1,p2=join(own,a1,p2)
    b1=send(a1,even_odd); c1=send(a1,core_flip); a2=over(p2)
    own=forward(pages-1,1,xt,w_own,own)
    own,b1,c1,a2,p3,p4=join(own,b1,c1,a2,p3,p4)
    d1=send(b1,core_flip); b2=send(a2,even_odd); a3=over(p3)
    cores=[send(a2,core_flip)]
    wt_both,wl_both,bt_o,bl_o=unpack_first(scal,(a1,b1,c1,d1),text_qkv,wl)
    wt_both,wl_both,bt_o,bl_o,a2,b2,a3,p4,cores=join(wt_both,wl_both,bt_o,bl_o,a2,b2,a3,p4,cores)
    e2=send(a2,odd_even); f2=send(b2,odd_even); a4=over(p4); b3=send(a3,even_odd)
    cores+=[send(b2,core_flip)]
    w_oth=(wt_both,wl_both,bt_o,bl_o)
    oth=forward(0,pages-1,xt,w_oth,())
    oth=forward(pages-1,1,xt,w_oth,oth)
    oth,e2,f2,a4,b3,cores=join(oth,e2,f2,a4,b3,cores)
    b4=send(a4,even_odd); c4=send(a4,core_flip); c3=send(a3,core_flip)
    cores+=[send(v,core_flip) for v in (e2,f2)]
    beside=side(scal,xl,own[7],oth[7],layout_cot.T,sel,a4,[layout_shifts.astype(F32),layout_gains.astype(F32)],
        [layout_out_w,layout_up,layout_down,upbl],[a1,b1,c1,d1])
    beside,b4,c4,c3,cores=join(beside,b4,c4,c3,cores)
    lo,dr1l,dOl,extra=beside
    second=(a2,b2,e2,f2,*cores)
    d3=send(b3,core_flip); d4=send(b4,core_flip)
    to,dr1,dO,keep,out,st,bst=ffn(n,scal,[xt,own[6],oth[6],text_cot,sel],[text_shifts.astype(F32),text_gains.astype(F32),upb],
        [text_up,text_out_w,text_down],second,((a3,a4),(b3,b4),(c3,c4),(d3,d4)),extra)
    steps=stages(n)
    wts=[wt_both,wl_both]
    tile=text_in.shape[0]//3
    mine_p=lambda p,c,d: attn_bwd(p,c,lengths,mp[None],own,dO,dOl,d)
    other_p=lambda p,d: attn_bwd(p,1,lengths,1-mp[None],oth,dO,dOl,d)
    sums=lambda d: qkv_grad(n,jnp.stack([mp,dp]),pages,xt,xl,*d,sel,*wts,st,bst)
    inputs=lambda d: input_grad(tile,d,wts,dr1,dr1l,sel)
    if n==16:
        out=send(out,steps[0])
        d_own=mine_p(0,1,())
        d_own,out,keep=join(d_own,out,keep)
        keep,out=halve(keep,out)
        out=send(out,steps[1])
        d_own=mine_p(1,pages-1,d_own)
        qkeep,qout=sums(d_own)
        qkeep,qout,keep,out=join(qkeep,qout,keep,out)
        qout=send(qout,steps[0])
        keep,out=halve(keep,out)
        half=keep.shape[0]//2
        far=send(out[half:],steps[2])
        d_oth=other_p(0,d_own)
        d_oth,qkeep,qout,keep,out,far=join(d_oth,qkeep,qout,keep,out,far)
        out_far=keep[half:]+far
        cut=out_far.shape[0]//2
        outs=[send(out_far[:cut],steps[3]),out_far[cut:]]
        qkeep,qout=halve(qkeep,qout)
        qout=send(qout,steps[1])
        d_oth=other_p(1,d_oth)
        d_oth,qkeep,qout,keep,out,outs[0],outs[1]=join(d_oth,qkeep,qout,keep,out,*outs)
        outs[1]=send(outs[1],steps[3])
        near_small=send(out[:half,3456:],steps[2])
        qkeep,qout=halve(qkeep,qout)
        qout=send(qout,steps[2])
        d_oth=other_p(2,d_oth)
        d_oth,qkeep,qout,keep,out,near_small,*outs=join(d_oth,qkeep,qout,keep,out,near_small,*outs)
        qkeep,qout_sent=halve(qkeep,qout)
        qout=send(qout_sent,steps[3])
        got_far=jnp.concatenate(outs,0)
        early=(keep[:half,3456:]+near_small)+got_far[:,3456:]
        early_got=send(early,steps[3])
        peer=over(jnp.concatenate([qkeep[:,1152:1280],qout_sent[:,1152:1280]],0))
        near=send(out[:half,:3456],steps[2])
        pair=lambda bit,x,y: (lambda low: jnp.stack([jnp.where(low,x,y),jnp.where(low,y,x)]))((dp&bit)==0)
        d_in=inputs(d_oth)
        d_in,qkeep,qout,peer,early_got,near=join(d_in,qkeep,qout,peer,early_got,near)
        g=(keep[:half,:3456]+near)+got_far[:,:3456]
        qg=qkeep+qout
        small=qg[:,1152:]
        got=send(small,steps[3]); peer_got=send(peer,steps[3])
        early=pair(8,early,early_got)
        early=pair(2,early,send(early,flip(n,2)))
        r=qg.shape[0]
        small=jnp.concatenate([pair(8,small,got),pair(8,peer[:r]+peer_got[r:],peer_got[:r]+peer[r:])],2)
        early=pair(4,early,send(early,flip(n,4))).reshape(8,-1,256)
        small=pair(2,small,send(small,flip(n,2)))
        early=(early,send(early,core_flip))
        small=pair(4,small,send(small,flip(n,4))).reshape(8,-1,256)
        small=(small,send(small,core_flip))
        order=[(i>>2&1)*4+(i>>1&1)*2+(i>>3) for i in range(16)]
    else:
        d_own=mine_p(0,pages,())
        qkeep,qout=sums(d_own)
        rs=lambda v: lax.psum_scatter(v,"dp",scatter_dimension=0,tiled=True)
        g=rs(keep); qg=rs(qkeep)
        d_oth=d_own
        for p in range(pages): d_oth=other_p(p,d_oth)
        d_in=inputs(d_oth)
        whole=lambda v: (lambda w: (w[None],w[None,:8]))(lax.all_gather(v,"dp",tiled=True))
        small=whole(jnp.concatenate([qg[:,1152:],over(qg[:,1152:])],1)); early=whole(g[:,3456:])
        order=[]
    tg,lg=d_in
    r=g.shape[0]
    tvec,lvec,cs,shifts,gains,bst,qgl,csl,outl,shl,gal,upl,bstl,downl=finish(order,core[None],*small,*early)
    qg=jnp.moveaxis(qg[:,:1152].reshape(r,3,384),1,0)
    return (to,lo.T,tg,lg.T,tvec,lvec,qg,cs,g[:,3072:3456].T,shifts,gains,g[:,:1536],bst,g[:,1536:3072].T,
            qgl,csl,outl,shl,gal,upl,bstl,downl.T)


def solution(mesh):
    rows=P("dp",None); cols=P(None,"mp"); lead=P("mp",None); cube=P(None,None,"mp")
    weights=(cube,cols,lead,P(),P(),cols,P("mp"),lead)
    return jax.shard_map(shards,mesh=mesh,
        in_specs=(rows,rows,P("dp"),P("dp"),P("dp"),P(),P())+weights+weights+(rows,rows),
        out_specs=(rows,rows,rows,rows,P(),P(),P(None,"dp","mp"),cols,P("mp","dp"),P(),P(),P("dp","mp"),P("mp"),P("mp","dp"),
                   cube,cols,lead,P(),P(),cols,P("mp"),lead),
        check_vma=False)
```

```python
import functools
import jax, jax.numpy as jnp
from jax import lax
from jax.experimental import pallas as pl
from jax.experimental.pallas import tpu as pltpu
F32=jnp.float32; BF=jnp.bfloat16
NT=(((1,),(1,)),((),()))
TN=(((0,),(0,)),((),()))
def dot(a,b): return jnp.dot(a,b,preferred_element_type=F32)
def dotg(a,b,dn): return lax.dot_general(a,b,dn,preferred_element_type=F32)
VLIM=60*1024*1024
SMALL=36*1024*1024

def cost(us): return pl.CostEstimate(flops=int(us*1e7),bytes_accessed=1024,transcendentals=0)

def lane_iota(shape): return lax.broadcasted_iota(jnp.int32,shape,len(shape)-1)

def row_masks():
    i=lax.broadcasted_iota(jnp.int32,(1,128),1)
    return lambda f: jnp.where(f(i),1.0,0.0).astype(BF)


def attn_fwd_kernel(first, len_ref, half_ref, xt_ref, xl_ref, wt_ref, wl_ref, bt_ref, bl_ref, *rest):
    qt_ref, kt_ref, vt_ref, ql_ref, kl_ref, vl_ref, ot_ref, ol_ref, lse_ref, olT, lseT=rest[-11:]
    page=first+pl.program_id(0)
    seq=xt_ref.shape[0]
    xt=xt_ref[...]; xl=xl_ref[...]
    for c,(t,l) in enumerate(((qt_ref,ql_ref),(kt_ref,kl_ref),(vt_ref,vl_ref))):
        t[...]=(dot(xt,wt_ref[c])+bt_ref[c:c+1,:]).astype(BF)
        l[...]=(dot(xl,wl_ref[c])+bl_ref[c:c+1,:]).astype(BF)
    lane=lane_iota((seq,128))
    row=lax.broadcasted_iota(jnp.int32,(seq,128),0)
    length=len_ref[page]
    bias=jnp.where(row<length,0.0,-1e9).astype(BF)
    one=jnp.ones((seq,128),BF)
    ql=jnp.where(lane==96,one,ql_ref[...]*BF(0.25))
    kl=jnp.where(lane==96,bias,kl_ref[...])
    vlT=vl_ref[...].T; qlT=ql.T
    keep=row_masks()
    olT[...]=jnp.zeros_like(olT); lseT[...]=jnp.zeros_like(lseT)
    def scores(h):
        j,s=h//2,h%2
        cols=slice(128*j,128*j+128)
        qbig=jnp.concatenate([(qt_ref[:,cols]*BF(0.125)).T,qlT],0)
        kbig=jnp.concatenate([kt_ref[:,cols]*keep(lambda i: i//64==s),kl*keep(lambda i: (i//16==h)|(i==96))],1)
        return dot(kbig,qbig)
    halves=[]
    def finish(h,e,m,ssum):
        j,s=h//2,h%2
        vT=vt_ref[:,128*j:128*j+128].T
        v80=jnp.concatenate([vT[64*s:64*s+64],vlT[16*h:16*h+16]],0)
        o=dot(v80,e)*(1.0/ssum)
        halves.append(o[:64])
        olT[16*h:16*h+16,:]=o[64:]
        lseT[h:h+1,:]=m+jnp.log(ssum)
        if s==1: ot_ref[:,128*j:128*j+128]=jnp.concatenate(halves[-2:],0).T.astype(BF)
    ahead=scores(0); behind=None
    for h in range(6):
        S=ahead
        if h<5: ahead=scores(h+1)
        if behind is not None: finish(*behind)
        m=jnp.max(S,0,keepdims=True)
        e=jnp.exp(S-m)
        behind=(h,e.astype(BF),m,jnp.sum(e,0,keepdims=True))
    finish(*behind)
    ol_ref[...]=olT[...].T.astype(BF)
    lse_ref[...]=pltpu.roll(lseT[...].T,97,1)

def attn_fwd(first, count, lengths, half, xt, xl, wt, wl, bt, bl, prev):
    rows=xt.shape[0]; pages=lengths.shape[0]; seq=rows//pages
    rb=lambda n: pl.BlockSpec((seq,n),lambda p,*_:(first+p,0))
    full=lambda a: pl.BlockSpec((None,)*(a.ndim-3)+a.shape[-3:],lambda p,l,h:(h[0],0,0,0)[4-a.ndim:]) if a.ndim>2 else pl.BlockSpec(a.shape,lambda p,*_:(0,0))
    whole=pl.BlockSpec(memory_space=pl.ANY)
    o=lambda n,d=BF: jax.ShapeDtypeStruct((rows,n),d)
    return pl.pallas_call(functools.partial(attn_fwd_kernel,first),
        grid_spec=pltpu.PrefetchScalarGridSpec(num_scalar_prefetch=2,grid=(count,),
            in_specs=[rb(768),rb(192),full(wt),full(wl),full(bt),full(bl)]+[whole]*len(prev),
            out_specs=[rb(384)]*3+[rb(128)]*3+[rb(384),rb(128),rb(128)],
            scratch_shapes=[pltpu.VMEM((128,seq),F32),pltpu.VMEM((128,seq),F32)]),
        out_shape=[o(384)]*3+[o(128)]*3+[o(384),o(128),o(128,F32)],
        input_output_aliases={8+i:i for i in range(len(prev))},
        compiler_params=pltpu.CompilerParams(vmem_limit_bytes=VLIM),cost_estimate=cost(6.2*count),name="attn_fwd")(lengths,half,xt,xl,wt,wl,bt,bl,*prev)

def ind_matrix(j):
    r=lax.broadcasted_iota(jnp.int32,(256,128),0)%128
    l=lax.broadcasted_iota(jnp.int32,(256,128),1)
    h=(r//64+2*j) if j is not None else r//16
    return jnp.where((l==97+h)&(h<6),1.0,0.0).astype(BF)

def split2(v):
    hi=v.astype(BF)
    return hi,(v-hi.astype(F32)).astype(BF)

def bwd_page(length, qt_ref, kt_ref, vt_ref, ql_ref, kl_ref, vl_ref, ot_ref, ol_ref, lse_ref, dot_ref, dol_ref,
                    dpt_ref, dpl_ref, dqlT, lay):
    seq=qt_ref.shape[0]
    lane=lane_iota((seq,128))
    row=lax.broadcasted_iota(jnp.int32,(seq,128),0)
    bias=jnp.where(row<length,0.0,-1e9).astype(BF)
    zero=jnp.zeros((seq,128),BF); one=jnp.ones((seq,128),BF)
    nl=-lse_ref[...]
    hi=nl.astype(BF); r1=nl-hi.astype(F32); mid=r1.astype(BF); lo=r1-mid.astype(F32)
    ext=hi+pltpu.roll(mid.astype(F32),7,1).astype(BF)+pltpu.roll(lo,14,1).astype(BF)
    qle=jnp.where(lane<96,ql_ref[...]*BF(0.25),jnp.where(lane==96,one,ext))
    kl=kl_ref[...]; vl=vl_ref[...]; ql=ql_ref[...]
    klT=kl.T
    dqlT[...]=jnp.zeros_like(dqlT)
    def sums(a,b,m):
        p=a.astype(F32)*b.astype(F32)
        h_,l_=split2(p)
        return dot(jnp.concatenate([h_,l_],1),m)
    dol=dol_ref[...]
    d_l=sums(dol,ol_ref[...],ind_matrix(None))
    d_t=d_l
    for j in range(3):
        cols=slice(128*j,128*j+128)
        d_t=d_t+sums(dot_ref[:,cols],ot_ref[:,cols],ind_matrix(j))
    def ext_delta(d):
        h_=d.astype(BF); l_=d-h_.astype(F32)
        return h_+pltpu.roll(l_,7,1).astype(BF)
    dol1=jnp.where(lane<96,dol*BF(0.125),ext_delta(d_t*-0.125))
    dol2=jnp.where(lane<96,dol*BF(0.25),ext_delta(d_l*-0.25))
    keep=row_masks()
    kle=jnp.where(lane==96,bias,jnp.where(lane>96,one,kl))
    vle=jnp.where(lane>96,one,vl)
    qleT=qle.T; dol1T=dol1.T; dol2T=dol2.T
    rows2=lambda x,masks: jnp.concatenate([x*m for m in masks],0)
    for j in range(3):
        cols=slice(128*j,128*j+128)
        qt=qt_ref[:,cols]; kt=kt_ref[:,cols]; vt=vt_ref[:,cols]; dO=dot_ref[:,cols]
        qbig=jnp.concatenate([(qt*BF(0.125)).T,qleT],0)
        dbig=jnp.concatenate([(dO*BF(0.125)).T,dol1T],0)
        ktT=kt.T
        heads=(2*j,2*j+1)
        tms=[keep(lambda i: i//64==s) for s in range(2)]
        lms=[keep(lambda i: i//16==h) for h in heads]
        R1s=[]; R2s=[]; Ps=[]; dqs=[]
        for s,h in enumerate(heads):
            kbig=jnp.concatenate([kt*tms[s],kle*keep(lambda i: (i//16==h)|(i==96)|(i==97+h)|(i==104+h)|(i==111+h))],1)
            vleh=vle*keep(lambda i: (i//16==h)|(i==97+h)|(i==104+h))
            vbig=jnp.concatenate([vt*tms[s],vleh],1)
            S=dot(kbig,qbig)
            M1=dot(vbig,dbig)
            M2=dot(vleh,dol2T)
            Pm=jnp.exp(S)
            R1=(Pm*M1).astype(BF); R2=(Pm*M2).astype(BF)
            Ps.append(Pm.astype(BF)); R1s.append(R1); R2s.append(R2)
            dqs.append(dot(ktT[64*s:64*s+64],R1))
            dqlT[16*h:16*h+16,:]=dot(klT[16*h:16*h+16],R2)
        dpt_ref[0,:,cols]=jnp.concatenate(dqs,0).T.astype(BF)
        dpt_ref[1,:,cols]=dot(jnp.concatenate(R1s,1),rows2(qt,tms)).astype(BF)
        dv=dot(jnp.concatenate(Ps,1),jnp.concatenate([rows2(dO,tms),rows2(dol,lms)],1))
        dpt_ref[2,:,cols]=dv[:,:128].astype(BF)
        dkl=dot(jnp.concatenate(R2s,1),rows2(ql,lms))
        if j==0: lay[0]=dkl; lay[1]=dv[:,128:]
        else: lay[0]+=dkl; lay[1]+=dv[:,128:]
    dpl_ref[0]=dqlT[...].T.astype(BF)
    dpl_ref[1]=lay[0].astype(BF); dpl_ref[2]=lay[1].astype(BF)


def bwd_kernel(first, len_ref, half_ref, qt, kt, vt, ql, kl, vl, ot, ol, lse, dO, dOl, *rest):
    dpt,dpl,dqlT,lay=rest[-4:]
    bwd_page(len_ref[first+pl.program_id(0)],qt,kt,vt,ql,kl,vl,ot,ol,lse,dO.at[0],dOl.at[0],dpt,dpl,dqlT,lay)


def attn_bwd(first,count,lengths,half,saved,dO,dOl,prev):
    rows=saved[0].shape[0]; seq=rows//lengths.shape[0]
    rb=lambda n: pl.BlockSpec((seq,n),lambda i,*_:(first+i,0))
    hb=lambda n: pl.BlockSpec((1,seq,n),lambda i,l,h:(h[0],first+i,0))
    pb=lambda n: pl.BlockSpec((3,seq,n),lambda i,l,h:(h[0],first+i,0))
    whole=pl.BlockSpec(memory_space=pl.ANY)
    return pl.pallas_call(functools.partial(bwd_kernel,first),
        grid_spec=pltpu.PrefetchScalarGridSpec(num_scalar_prefetch=2,grid=(count,),
            in_specs=[rb(384)]*3+[rb(128)]*3+[rb(384),rb(128),rb(128),hb(384),hb(128)]+[whole]*len(prev),
            out_specs=[pb(384),pb(128)],scratch_shapes=[pltpu.VMEM((128,seq),F32),pltpu.VMEM((2,seq,128),F32)]),
        out_shape=[jax.ShapeDtypeStruct((6,rows,384),BF),jax.ShapeDtypeStruct((6,rows,128),BF)],
        input_output_aliases={13+i:i for i in range(len(prev))},
        compiler_params=pltpu.CompilerParams(vmem_limit_bytes=SMALL if prev else VLIM),cost_estimate=cost(9*count),name="attn_bwd")(lengths,half,*saved,dO,dOl,*prev)


def dx_kernel(dpt, dpl, wt, wl, dr1, dr1l, sel, dx, dxl, wts, wls):
    @pl.when(pl.program_id(0)==0)
    def _():
        for h in range(2):
            for c in range(3):
                i=3*h+c
                wts[:,384*i:384*i+384]=wt[h,c]
                wls[:,128*i:128*i+128]=wl[h,c]
    def back(d,w,base,flag):
        v=dotg(jnp.concatenate([d[i] for i in range(6)],1),w[...],NT)+base[...]
        return jnp.where(flag>0.5,0.0,v)
    flags=sel[...].astype(F32).T
    dx[...]=back(dpt,wts,dr1,flags[:,1:2])
    dxl[...]=back(dpl,wls,dr1l,flags[:,2:3]).T


def input_grad(tile,dp,wts,dr1,dr1l,sel):
    rows=dr1.shape[0]
    rb=lambda n: pl.BlockSpec((tile,n),lambda i:(i,0))
    pb=lambda n: pl.BlockSpec((6,tile,n),lambda i:(0,i,0))
    full=lambda a: pl.BlockSpec(a.shape,lambda i:(0,0,0,0))
    return pl.pallas_call(dx_kernel,grid=(rows//tile,),
        in_specs=[pb(384),pb(128)]+[full(w) for w in wts]+[rb(768),rb(192),pl.BlockSpec((8,tile),lambda i:(0,i))],
        out_specs=[rb(768),pl.BlockSpec((192,tile),lambda i:(0,i))],
        scratch_shapes=[pltpu.VMEM((768,2304),BF),pltpu.VMEM((192,768),BF)],
        out_shape=[jax.ShapeDtypeStruct((rows,768),F32),jax.ShapeDtypeStruct((192,rows),F32)],
        compiler_params=pltpu.CompilerParams(vmem_limit_bytes=44*1024*1024),cost_estimate=cost(5),name="input_grad")(*dp,*wts,dr1,dr1l,sel)


def move_blocks(acc, keep, send, sem, position, n, left, width, start):
    cols=pl.ds(left,width)
    if n!=16:
        cp=pltpu.make_async_copy(acc,keep.at[:,cols],sem)
        if start: cp.start()
        else: cp.wait()
        return
    c=position&1; x=(position>>1)&1; z0=(position>>2)&1; z1=(position>>3)&1
    rows=acc.shape[0]//16
    for out,core in ((keep,c),(send,1-c)):
        for q in range(8):
            r2,r3,r4=q>>2,(q>>1)&1,q&1
            fx=jnp.where(core==0,r2,r3); fz=jnp.where(core==0,r3,r2)
            block=(z1^r4)*8+(z0^fz)*4+(x^fx)*2+core
            cp=pltpu.make_async_copy(acc.at[pl.ds(pl.multiple_of(block*rows,8),rows)],out.at[pl.ds(q*rows,rows),cols],sem)
            if start: cp.start()
            else: cp.wait()


def place_blocks(acc, keep, send, sem, position, n):
    for start in (True,False): move_blocks(acc,keep,send,sem,position,n,0,acc.shape[1],start)


def block_shapes(rows,cols,n):
    S=jax.ShapeDtypeStruct
    if n!=16: return [S((rows,cols),F32),S((8,128),F32)]
    return [S((rows//2,cols),F32)]*2


def qkv_grad_kernel(n, pos_ref, xt, xl, dpt, dpl, sel, wt, wl, st, bst, keep, send, acc, sums, suml, sem):
    x=xt[...]; s=sel[...]; xv=xl[...]
    def add(first):
        def put(ref,v):
            if first: ref[...]=v
            else: ref[...]+=v
        cat=lambda d: jnp.concatenate([d[0],d[1],d[2]],1)
        t=cat(dpt); l=cat(dpl)
        put(acc.at[:,:1152],dotg(x,t,TN))
        g=dotg(xv,l,TN); a=dot(s,t); b=dot(s,l)
        for c in range(3):
            put(acc.at[192*c:192*c+192,1152:1280],g[:,128*c:128*c+128])
            put(sums.at[c],a[:,384*c:384*c+384]); put(suml.at[c],b[:,128*c:128*c+128])
    first=pl.program_id(0)==0
    pl.when(first)(lambda: add(True))
    pl.when(jnp.logical_not(first))(lambda: add(False))
    @pl.when(pl.program_id(0)==pl.num_programs(0)-1)
    def _():
        t=jnp.zeros((8,768),F32); l=jnp.zeros((8,192),F32)
        for c in range(3):
            for v,w,text in ((sums[c],wt,True),(suml[c],wl,False)):
                hi,lo=split2(v)
                lo2=(v-hi.astype(F32)-lo.astype(F32)).astype(BF)
                y=dotg(jnp.concatenate([hi,lo,lo2],0),w[0,c],NT)
                y=y[0:8]+y[8:16]+y[16:24]
                if text: t=t+y
                else: l=l+y
        acc[576:768,1152:1280]=jnp.zeros((192,128),F32)
        rows=[st[i:i+1,128*j:128*j+128] for i in range(7) for j in range(6)]+[bst[0:1,128*j:128*j+128] for j in range(12)]
        rows+=[sums[c][0:1,128*j:128*j+128] for c in (0,2) for j in range(3)]+[suml[c][0:1] for c in (0,2)]
        rows+=[t[1:2,128*j:128*j+128] for j in range(6)]+[l[2:3,0:128],jnp.concatenate([l[2:3,128:],jnp.zeros((1,64),F32)],1)]
        for i,v in enumerate(rows): acc[576+i:577+i,1152:1280]=v
        place_blocks(acc,keep,send,sem,pos_ref[1],n)


def qkv_grad(n,pos,pages,xt,xl,dpt,dpl,sel,wt,wl,st,bst):
    seq=xt.shape[0]//pages
    rb=lambda m: pl.BlockSpec((seq,m),lambda i,s:(i,0))
    pb=lambda m: pl.BlockSpec((3,seq,m),lambda i,s:(s[0],i,0))
    wb=lambda a: pl.BlockSpec((1,)+a.shape[1:],lambda i,s:(s[0],0,0,0))
    whole=pl.BlockSpec(memory_space=pl.ANY)
    return pl.pallas_call(functools.partial(qkv_grad_kernel,n),
        grid_spec=pltpu.PrefetchScalarGridSpec(num_scalar_prefetch=1,grid=(pages,),
            in_specs=[rb(768),rb(192),pb(384),pb(128),pl.BlockSpec((8,seq),lambda i,s:(0,i)),wb(wt),wb(wl)]+[pl.BlockSpec(a.shape,lambda i,s:(0,0)) for a in (st,bst)],
            out_specs=[whole,whole],
            scratch_shapes=[pltpu.VMEM((768,1280),F32),pltpu.VMEM((3,8,384),F32),pltpu.VMEM((3,8,128),F32),pltpu.SemaphoreType.DMA]),
        out_shape=block_shapes(768,1280,n),
        compiler_params=pltpu.CompilerParams(vmem_limit_bytes=SMALL),cost_estimate=cost(8),name="qkv_grad")(pos,xt,xl,dpt,dpl,sel,wt,wl,st,bst)


EPS=1e-5
def gelu_parts(x):
    cdf=0.5+0.5*lax.erf(x*0.7071067811865476)
    phi=jnp.exp2(x*x*-0.7213475204444817-1.3257480647361593)
    return cdf, cdf+x*phi

def norm(v):
    mu=jnp.mean(v,-1,keepdims=True)
    c=v-mu
    inv=lax.rsqrt(jnp.mean(c*c,-1,keepdims=True)+EPS)
    return c*inv,inv

def norm_back(g,u,inv,gain):
    s=g*gain
    return inv*(s-jnp.mean(s,-1,keepdims=True)-u*jnp.mean(s*u,-1,keepdims=True))

def stream(own_off, x, o, o_own, cot, outw, up, down, shift, gain, upb, act, gp, out_ref, dr1_ref, dos, gup, gdn, gout, stat, bstat, chunk, flag, kept=None):
    d=x.shape[1]; F=up.shape[1]; half=F//2
    h1u,i1=norm(x.astype(F32)+dot(o,outw[...])+shift[2:3])
    h1=h1u*gain[0:1]+shift[0:1]
    h1b=h1.astype(BF)
    yield
    def units(i,carry):
        cs=pl.ds(pl.multiple_of(i*chunk,chunk),chunk)
        pre=dot(h1b,up[:,cs])+upb[:,cs]
        cdf,der=gelu_parts(pre)
        act[:,cs]=(pre*cdf).astype(BF)
        gp[:,cs]=der.astype(BF)
        return carry
    lax.fori_loop(0,F//chunk,units,0)
    yield
    r2=h1+dot(act[...],down[...])+shift[3:4]
    u2,i2=norm(r2)
    y=u2*gain[1:2]+shift[1:2]
    out_ref[...]=y if out_ref.shape==y.shape else y.T
    g=cot.astype(F32)
    dr2=norm_back(g,u2,i2,gain[1:2])
    dr2b=dr2.astype(BF)
    def units_back(i,carry):
        cs=pl.ds(pl.multiple_of(i*chunk,chunk),chunk)
        da=dotg(dr2b,down[cs,:],NT)
        gp[:,cs]=(da*gp[:,cs].astype(F32)).astype(BF)
        return carry
    lax.fori_loop(0,F//chunk,units_back,0)
    dh1=dotg(gp[...],up[...],NT)+dr2
    dr1=norm_back(dh1,h1u,i1,gain[0:1])
    dr1_ref[...]=dr1
    dr1b=dr1.astype(BF)
    dO=dotg(dr1b,outw[...],NT).astype(BF)
    w=dO.shape[1]//2
    dos[0]=dO[:,:w]; dos[1]=dO[:,w:]
    osl=pl.ds(pl.multiple_of(own_off,128),half)
    dpo=gp[:,osl]
    rs=lambda v: jnp.sum(v,0,keepdims=True)
    stat[...]+=jnp.concatenate([rs(dh1),rs(g),rs(dr1),rs(dr2),rs(dh1*h1u),rs(g*u2),rs(jnp.where(flag>0.5,dr1,0.0)),jnp.zeros((1,d),F32)],0)
    bstat[...]+=dot(jnp.ones((8,x.shape[0]),BF),dpo)
    if kept is not None:
        for ref,v in zip(kept,(h1b,dr2b,dr1b,o_own)): ref[...]=v
    else:
        gup[...]+=dotg(h1b,dpo,TN)
        gdn[...]+=dotg(dr2b,act[:,osl],TN)
        gout[...]+=dotg(dr1b,o_own,TN)
    yield


def halves_of(mp, a, b):
    a=a[...]; b=b[...]
    z=mp==0
    return jnp.concatenate([jnp.where(z,a,b),jnp.where(z,b,a)],1)


def half(k, m): return pl.ds(pl.multiple_of(k*m,m),m)


def side_kernel(s_ref, xl, ola, olb, cl, lm, little, shl, gal, outl_own, upl_own, downl_own, upbl_own, pa, pb, pc, pd,
                lo, dr1l, dosl, extra, actl, gpl, outwl, upl, downl, upbl, gupl, gdnl, goutl, stl, bstl, outs):
    mp=s_ref[0]; other=1-mp
    @pl.when(pl.program_id(0)==0)
    def _():
        upbl[:,half(mp,384)]=upbl_own[...]
        upl[:,half(mp,384)]=upl_own[...]
        downl[half(mp,384),:]=downl_own[...]
        outwl[half(mp,128),:]=jnp.concatenate([outl_own[...],jnp.zeros((32,192),BF)],0)
        outs[...]=jnp.zeros_like(outs)
        for i,v in enumerate((pa,pb,pc,pd)):
            p=s_ref[2+i]
            rows=pl.ds(pl.multiple_of(p*24,8),24)
            outs[rows,0:128]=v[0:24]; outs[rows,128:192]=v[24:48,0:64]
            for j in range(3):
                upl[half(p,48),pl.ds(pl.multiple_of(other*384+128*j,128),128)]=v[48+48*j:96+48*j].astype(BF)
            rows=pl.ds(pl.multiple_of(other*384+p*96,16),96)
            downl[rows,0:128]=v[192:288].astype(BF)
            downl[rows,128:192]=v[288:384,0:64].astype(BF)
        outwl[half(other,128),:]=outs[...].astype(BF)
        for j in range(3):
            upbl[:,pl.ds(pl.multiple_of(other*384+128*j,128),128)]=little[12+j:13+j]
        for ref in (gupl,gdnl,goutl,stl,bstl): ref[...]=jnp.zeros_like(ref)
    phases=stream(mp*384,xl[...],halves_of(mp,ola,olb),ola[...],cl[...].T,outwl,upl,downl,shl,gal,upbl,actl,gpl,lo,dr1l,dosl,gupl,gdnl,goutl,stl,bstl,768,lm[...].astype(F32).T[:,2:3])
    next(phases); next(phases); next(phases)
    @pl.when(pl.program_id(0)==pl.num_programs(0)-1)
    def _():
        blocks=[gupl[:,128*j:128*j+128] for j in range(3)]+[gdnl[:,128*j:128*j+128] for j in range(3)]+[goutl[...]]
        rest=[stl[:,0:128],jnp.concatenate([stl[:,128:192],jnp.zeros((8,64),F32)],1)]
        rest+=[bstl[:,128*j:128*j+128] for j in range(3)]+[jnp.zeros((152,128),F32)]
        blocks.append(jnp.concatenate(rest,0))
        for i,v in enumerate(blocks):
            extra[192*(i%4):192*(i%4)+192,128*(i//4):128*(i//4)+128]=v


def side(scal,xl,ola,olb,cl,lm,little,params,own,pieces,tile=768):
    rows=xl.shape[0]
    rb=lambda n: pl.BlockSpec((tile,n),lambda p,*_:(p,0))
    cb=pl.BlockSpec((192,tile),lambda p,*_:(0,p))
    full=lambda a: pl.BlockSpec(a.shape,lambda p,*_:(0,)*len(a.shape))
    S=jax.ShapeDtypeStruct; V=pltpu.VMEM
    last=pl.BlockSpec((400,128),lambda p,*_:(0,0))
    return pl.pallas_call(side_kernel,
        grid_spec=pltpu.PrefetchScalarGridSpec(num_scalar_prefetch=1,grid=(rows//tile,),
            in_specs=[rb(192),rb(128),rb(128),cb,pl.BlockSpec((8,tile),lambda p,*_:(0,p)),pl.BlockSpec((16,128),lambda p,*_:(36,0))]+[full(a) for a in params+own]+[last]*4,
            out_specs=[cb,rb(192),pl.BlockSpec((2,tile,128),lambda p,*_:(0,p,0)),pl.BlockSpec((768,256),lambda p,*_:(0,0))],
            scratch_shapes=[V((tile,768),BF),V((tile,768),BF),V((256,192),BF),V((192,768),BF),V((768,192),BF),V((1,768),F32),
                V((192,384),F32),V((192,384),F32),V((192,128),F32),V((8,192),F32),V((8,384),F32),V((128,192),F32)]),
        out_shape=[S((192,rows),F32),S((rows,192),F32),S((2,rows,128),BF),S((768,256),F32)],
        compiler_params=pltpu.CompilerParams(vmem_limit_bytes=VLIM),cost_estimate=cost(10),name="side")(scal,xl,ola,olb,cl,lm,little,*params,*own,*pieces)


def ffn_kernel(n, s_ref, *refs):
    (xt, oa, ob, ct, tm, sh, ga, upb_own)=refs[:8]
    (up_own, outw_own, down_own)=refs[8:11]
    second=refs[11:19]; third=[refs[19+2*i:21+2*i] for i in range(4)]; extra=refs[27]
    (to, dr1, dos, keep, send, st, bst)=refs[28:35]
    (act2, gp2, hb2, rb2, sb2, ob2, acc, up, outw, down, upb, gbias, sem, sem_own, sem2, sem3, sem4)=refs[35:]
    step=pl.program_id(0); odd=step%2; tile=xt.shape[0]
    part=pl.ds(pl.multiple_of(odd*tile,tile),tile)
    act=act2.at[part]; gp=gp2.at[part]
    mp=s_ref[0]; other=1-mp
    first=pl.program_id(0)==0
    column=lambda k: acc.at[:,128*k:128*k+128]
    own=[pltpu.make_async_copy(src,dst,sem_own.at[i]) for i,(src,dst) in enumerate((
        (outw_own,outw.at[half(mp,384),:]),(up_own,up.at[:,half(mp,1536)]),(down_own,down.at[half(mp,1536),:])))]
    two=[]; three=[]
    for i,src in enumerate(second):
        two.append([pltpu.make_async_copy(src.at[a:b],column(2*i+k).at[0:b-a],sem2.at[i,k]) for k,(a,b) in enumerate(((0,768),(768,1152)))])
    outs=[]
    for i,src in enumerate(third):
        base=16+4*i if i<3 else 0
        three.append([pltpu.make_async_copy(src[s].at[r:r+768],column(base+k),sem3.at[i,k]) for k,(s,r) in enumerate(((0,0),(1,592),(1,1360)))])
        outs.append(pltpu.make_async_copy(src[1].at[0:576],column(19+4*i if i<3 else 28).at[0:576],sem3.at[i,3]))
    bias=[pltpu.make_async_copy(third[0][1].at[576:592],gbias,sem4)]
    @pl.when(first)
    def _():
        for cp in outs+own[:1]+bias: cp.start()
        for cps in two:
            for cp in cps: cp.start()
        own[1].start()
        for cps in three[:3]:
            for cp in cps: cp.start()
        own[2].start()
        for cp in outs: cp.wait()
        for i in range(4):
            for j in range(6):
                v=column(19+4*i if i<3 else 28)[96*j:96*j+96]
                outw[pl.ds(pl.multiple_of(other*384+s_ref[2+i]*96,16),96),128*j:128*j+128]=v.astype(BF)
        own[0].wait()
    phases=stream(mp*1536,xt[...],halves_of(mp,oa,ob),oa[...],ct[...],outw,up,down,sh,ga,upb,act,gp,to,dr1,dos,
        None,None,None,st,bst,1536,tm[...].astype(F32).T[:,1:2],[r.at[part] for r in (hb2,rb2,sb2,ob2)])
    next(phases)
    @pl.when(first)
    def _():
        for cps in two:
            for cp in cps: cp.wait()
        def unpack_second(i,carry):
            p=s_ref[6+i]
            left=pl.ds(pl.multiple_of(256*i,128),128); right=pl.ds(pl.multiple_of(256*i+128,128),128)
            for j in range(12):
                v=acc[96*j:96*j+96,left] if j<8 else acc[96*(j-8):96*(j-8)+96,right]
                up[half(p,96),pl.ds(pl.multiple_of(other*1536+128*j,128),128)]=v.astype(BF)
            return carry
        lax.fori_loop(0,8,unpack_second,0)
        for cp in three[3]: cp.start()
        bias[0].wait()
        for j in range(12):
            upb[:,pl.ds(pl.multiple_of(other*1536+128*j,128),128)]=gbias[j:j+1]
        upb[:,half(mp,1536)]=upb_own[...]
        own[1].wait()
    next(phases)
    @pl.when(first)
    def _():
        own[2].wait()
        for cps in three:
            for cp in cps: cp.wait()
        def unpack_third(i,carry):
            p=s_ref[2+i]
            base=jnp.where(i<3,2048+512*i,0)
            for j in range(6):
                v=acc[384*(j%2):384*(j%2)+384,pl.ds(pl.multiple_of(base+128*(j//2),128),128)]
                down[pl.ds(pl.multiple_of(other*1536+p*384,16),384),128*j:128*j+128]=v.astype(BF)
            return carry
        lax.fori_loop(0,4,unpack_third,0)
        def clear(i,carry):
            acc[pl.ds(pl.multiple_of(16*i,16),16),:]=jnp.zeros((16,acc.shape[1]),F32)
            return carry
        lax.fori_loop(0,48,clear,0)
        st[...]=jnp.zeros_like(st); bst[...]=jnp.zeros_like(bst)
    next(phases)
    last=step==pl.num_programs(0)-1
    osl=half(mp,1536)
    copies=[]
    def into(left,width,lhs,rhs):
        acc[:,left:left+width]+=dotg(lhs,rhs,TN)
        @pl.when(last)
        def _(): move_blocks(acc.at[:,left:left+width],keep,send,sem,s_ref[1],n,left,width,True)
    @pl.when(odd==1)
    def _():
        @pl.when(last)
        def _():
            cp=pltpu.make_async_copy(extra,acc.at[:,3456:3712],sem4)
            cp.start(); cp.wait()
            move_blocks(acc.at[:,3456:3712],keep,send,sem,s_ref[1],n,3456,256,True)
        into(0,1536,hb2[...],gp2[:,osl])
        into(1536,1536,rb2[...],act2[:,osl])
        into(3072,384,sb2[...],ob2[...])
        @pl.when(last)
        def _(): move_blocks(acc,keep,send,sem,s_ref[1],n,0,3712,False)


def ffn(n,scal,rowed,params,own,second,third,extra,tile=384):
    rows=rowed[0].shape[0]
    rb=lambda a: pl.BlockSpec((tile,a.shape[1]),lambda p,*_:(p,0))
    full=lambda a: pl.BlockSpec(a.shape,lambda p,*_:(0,)*len(a.shape),pipeline_mode=pl.Buffered(1))
    whole=pl.BlockSpec(memory_space=pl.ANY)
    S=jax.ShapeDtypeStruct; V=pltpu.VMEM; D=pltpu.SemaphoreType.DMA
    rowout=[S((rows,768),F32),S((rows,768),F32)]
    dos=[S((2,rows,384),BF)]
    return pl.pallas_call(functools.partial(ffn_kernel,n),
        grid_spec=pltpu.PrefetchScalarGridSpec(num_scalar_prefetch=1,grid=(rows//tile,),
            in_specs=[rb(a) for a in rowed[:-1]]+[pl.BlockSpec((8,tile),lambda p,*_:(0,p))]+[full(w) for w in params]+[whole]*(len(own)+17),
            out_specs=[rb(a) for a in rowout]+[pl.BlockSpec((2,tile,384),lambda p,*_:(0,p,0)),whole,whole]+[pl.BlockSpec((8,m),lambda p,*_:(0,0)) for m in (768,1536)],
            scratch_shapes=[V((2*tile,3072),BF),V((2*tile,3072),BF),V((2*tile,768),BF),V((2*tile,768),BF),V((2*tile,768),BF),V((2*tile,384),BF),V((768,3712),F32),V((768,3072),BF),V((768,768),BF),V((3072,768),BF),
                V((1,3072),F32),V((16,128),F32),D,D((3,)),D((8,2)),D((4,4)),D]),
        out_shape=rowout+dos+block_shapes(768,3712,n)+[S((8,768),F32),S((8,1536),F32)],
        compiler_params=pltpu.CompilerParams(vmem_limit_bytes=VLIM),cost_estimate=cost(80),name="middle")(scal,*rowed,*params,*own,*second,*[v for pair in third for v in pair],extra)


from jax.sharding import PartitionSpec as P


def pack_kernel(starts, idx_ref, *refs):
    out=refs[-1]
    out[...]=jnp.zeros_like(out)
    r=0
    for k,src in enumerate(refs[:-1]):
        r=starts.get(k,r)
        lead=src.shape[0] if len(src.shape)==3 else None
        for c in range(lead or 1):
            w=src[c] if lead else src[...]
            n,m=w.shape
            for j in range(0,m,128):
                e=min(128,m-j)
                out[r:r+n,:e]=w[:,j:j+e].astype(F32)
                r+=n


def pack(idx, groups, parts):
    specs=[]; n=0; arrays=[]; starts=[]
    for split,whole in groups:
        starts.append((len(arrays),n))
        split=[a if isinstance(a,tuple) else (a,(0,1)) for a in split]
        for a,part in split:
            rows=a.shape[-2]//parts
            width=a.shape[-1]//part[1]
            blocks=-(-width//128)
            if a.ndim==3:
                specs.append(pl.BlockSpec((a.shape[0],rows,a.shape[2]),lambda i,s:(0,s[0],0)))
                n+=a.shape[0]*rows*blocks
            else:
                specs.append(pl.BlockSpec((rows,width),functools.partial(lambda k,i,s:(s[0],k),part[0])))
                n+=rows*blocks
        for a in whole:
            specs.append(pl.BlockSpec(a.shape,lambda i,s:(0,0)))
            n+=a.shape[0]*(-(-a.shape[1]//128))
        n=-(-n//8)*8
        arrays+=[a for a,_ in split]+whole
    return pl.pallas_call(functools.partial(pack_kernel,dict(starts)),
        grid_spec=pltpu.PrefetchScalarGridSpec(num_scalar_prefetch=1,grid=(1,),in_specs=specs,
            out_specs=pl.BlockSpec((n,128),lambda i,s:(0,0))),
        out_shape=jax.ShapeDtypeStruct((n,128),F32),
        compiler_params=pltpu.CompilerParams(vmem_limit_bytes=VLIM),cost_estimate=cost(2),name="pack")(idx,*arrays)


def unpack_first_kernel(s_ref, pa, pb, pc, pd, wt_own, wl_own, wt, wl, bt, bl):
    mine=s_ref[0]; other=1-mine
    wl[...]=jnp.zeros_like(wl)
    wt[mine]=wt_own[...]
    wl[mine]=wl_own[...]
    bt[...]=jnp.zeros_like(bt); bl[...]=jnp.zeros_like(bl)
    for p,ref in enumerate((pa,pb,pc,pd)):
        i=s_ref[2+p]
        at=lambda n: pl.ds(pl.multiple_of(i*n,n),n)
        r=400
        for c in range(3):
            for j in range(3):
                wt[other,c,at(192),128*j:128*j+128]=ref[r:r+192].astype(BF); r+=192
        for c in range(3):
            wl[other,c,at(48),:]=ref[r:r+48].astype(BF); r+=48
        if p==0:
            for c in range(2):
                for j in range(3):
                    bt[2*c:2*c+1,128*j:128*j+128]=ref[r+2*j+c:r+2*j+c+1]
            r+=6
            for c in range(2):
                bl[2*c:2*c+1,:]=ref[r+c:r+c+1]


def unpack_first(scal, pieces, wt, wl):
    S=jax.ShapeDtypeStruct
    full=lambda a: pl.BlockSpec(a.shape,lambda i,*_:(0,)*len(a.shape))
    outs=[S((2,3,768,384),BF),S((2,3,192,128),BF),S((3,384),F32),S((3,128),F32)]
    ins=[*pieces,wt,wl]
    return pl.pallas_call(unpack_first_kernel,
        grid_spec=pltpu.PrefetchScalarGridSpec(num_scalar_prefetch=1,grid=(1,),in_specs=[full(a) for a in ins],
            out_specs=[full(a) for a in outs]),
        out_shape=outs,compiler_params=pltpu.CompilerParams(vmem_limit_bytes=VLIM),cost_estimate=cost(4),name="unpack")(scal,*ins)


def flip(n, bit):
    return [(i,i^bit) for i in range(n)]


def cross(n, even, odd):
    return [(i,i^(even if i%2==0 else odd)) for i in range(n)]


def gather4(piece, n):
    a=lax.ppermute(piece,"mp",[(0,1),(1,0)])
    b=lax.ppermute(a,"dp",cross(n,2,4))
    c=lax.ppermute(a,"dp",flip(n,1))
    d=lax.ppermute(b,"dp",flip(n,1))
    return a,b,c,d


def gather8(piece, n):
    a=lax.ppermute(piece,"mp",[(0,1),(1,0)])
    b=lax.ppermute(a,"dp",cross(n,2,4))
    e=lax.ppermute(a,"dp",cross(n,4,2))
    f=lax.ppermute(b,"dp",cross(n,4,2))
    return (a,b,e,f)+tuple(lax.ppermute(v,"dp",flip(n,1)) for v in (a,b,e,f))


def ids8(dp):
    base=dp&7; odd=dp&1
    near=jnp.where(odd==0,2,4); far=6-near
    return [base,base^near,base^far,base^6,base^1,base^1^far,base^1^near,base^7]


def join(*values):
    return lax.optimization_barrier(values)


def stages(n):
    return (flip(n,1),cross(n,2,4),cross(n,4,2),flip(n,8))


def halve(keep, recv):
    half=keep.shape[0]//2
    return keep[:half]+recv[:half],keep[half:]+recv[half:]


def finish_kernel(order, c_ref, small, other, early, early_other, tv, lv, cs, sh, ga, bst, gl, csl, ol, shl, gal, ul, bl, dl, buf):
    rows=small.shape[1]
    for ref,ref2,(a,b) in ((small,other,((0,128),(384,512))),(early,early_other,((128,256),(256,384)))):
        if not order:
            v=ref[0]
            buf[:,a[0]:a[1]]=v[:,:128]; buf[:,b[0]:b[1]]=v[:,128:]
        low=c_ref[0]==0
        for i,k in enumerate(order):
            mine,got=ref[k],ref2[k]
            v=jnp.where(low,mine,got) if i%2==0 else jnp.where(low,got,mine)
            buf[rows*i:rows*i+rows,a[0]:a[1]]=v[:,:128]; buf[rows*i:rows*i+rows,b[0]:b[1]]=v[:,128:]
    block=lambda i: buf[192*(i%4):192*(i%4)+192,128+128*(i//4):256+128*(i//4)]
    for j in range(3):
        ul[:,128*j:128*j+128]=block(j)
        dl[:,128*j:128*j+128]=block(3+j)
        gl[j]=buf[192*j:192*j+192,0:96]
    ol[...]=block(6).T[0:96]
    last=block(7)
    for ref,r0 in ((shl,0),(gal,4)):
        n=ref.shape[0]
        ref[:,0:128]=last[r0:r0+n]; ref[:,128:192]=last[8+r0:8+r0+n,0:64]
    for j in range(3): bl[128*j:128*j+128]=last[16+8*j]
    row=lambda i,c=0: buf[576+i:577+i,128*c:128*c+128]
    for j in range(6):
        s=slice(128*j,128*j+128)
        for i in range(4): sh[i:i+1,s]=row(6*i+j)
        for i in range(2): ga[i:i+1,s]=row(24+6*i+j)
        tv[s]=((row(62+j)+row(62+j,3))+row(36+j))[0]
    for j in range(12): bst[128*j:128*j+128]=row(42+j)[0]
    for i in range(2):
        for j in range(3): cs[i:i+1,128*j:128*j+128]=row(54+3*i+j)
        csl[i:i+1,:]=row(60+i)[:,0:96]
    lv[0:128]=((row(68)+row(68,3))+last[6:7])[0]
    lv[128:192]=((row(69)+row(69,3))[:,0:64]+last[14:15,0:64])[0]


def finish(order, core, *parts):
    S=lambda *shape: jax.ShapeDtypeStruct(shape,F32)
    outs=[S(768),S(192),S(2,384),S(4,768),S(2,768),S(1536),S(3,192,96),S(2,96),S(96,192),S(4,192),S(2,192),S(192,384),S(384),S(192,384)]
    full=lambda a: pl.BlockSpec(a.shape,lambda i,*_:(0,)*len(a.shape))
    return pl.pallas_call(functools.partial(finish_kernel,order),
        grid_spec=pltpu.PrefetchScalarGridSpec(num_scalar_prefetch=1,grid=(1,),in_specs=[full(a) for a in parts],
            out_specs=[full(a) for a in outs],scratch_shapes=[pltpu.VMEM((768,512),F32)]),
        out_shape=outs,
        compiler_params=pltpu.CompilerParams(vmem_limit_bytes=VLIM),cost_estimate=cost(2),name="finish")(core,*parts)


def bias_rows(pair):
    b=pair.astype(F32)
    return jnp.stack([b[0],jnp.zeros_like(b[0]),b[1]])


def shards(text_in, layout_in, token_mask, box_mask, lengths, text_mask_vec, layout_mask_vec,
           text_qkv, text_qv_bias, text_out_w, text_shifts, text_gains, text_up, text_up_bias, text_down,
           layout_qkv, layout_qv_bias, layout_out_w, layout_shifts, layout_gains, layout_up, layout_up_bias, layout_down,
           text_cot, layout_cot):
    n=lax.axis_size("dp")
    mp=lax.axis_index("mp").astype(jnp.int32); dp=lax.axis_index("dp").astype(jnp.int32)
    core=dp&1; color=((dp>>1)^(dp>>2))&1
    ids=[2*color+core,2*(1-color)+core,2*color+1-core,2*(1-color)+1-core]
    scal=jnp.stack([mp,dp]+ids+ids8(dp))
    idx=ids[0][None]; idx8=(dp&7)[None]
    even_odd=cross(n,2,4); odd_even=cross(n,4,2); core_flip=flip(n,1)
    over=lambda v: lax.ppermute(v,"mp",[(0,1),(1,0)])
    send=lambda v,pairs: lax.ppermute(v,"dp",pairs)
    upb=text_up_bias.astype(F32)[None]; upbl=layout_up_bias.astype(F32)[None]
    p1=pack(idx,[([layout_out_w,layout_up,layout_down],[jnp.zeros((16,128),BF)]),([text_qkv,layout_qkv],[text_qv_bias,layout_qv_bias])],4)
    p2=pack(idx8,[([text_up],[])],8)
    p3=pack(idx,[([(text_down,(0,3))],[])],4)
    p4=pack(idx,[([text_out_w],[upb,upbl]),([(text_down,(1,3)),(text_down,(2,3))],[])],4)
    xt=jnp.where(token_mask[:,None]==1,text_mask_vec[None],text_in)
    xl=jnp.where(box_mask[:,None]==1,layout_mask_vec[None],layout_in)
    sel=jnp.concatenate([jnp.ones_like(token_mask)[None],(token_mask==1).astype(jnp.int32)[None],(box_mask==1).astype(jnp.int32)[None],
        jnp.zeros((5,token_mask.shape[0]),jnp.int32)],0).astype(BF)
    pad=lambda v: jnp.pad(v,((0,0),)*(v.ndim-1)+((0,32),))
    wl=pad(layout_qkv)
    a1=over(p1)
    bt=bias_rows(text_qv_bias); bl=pad(bias_rows(layout_qv_bias))
    pages=lengths.shape[0]
    forward=lambda first,count,x,w,prev: attn_fwd(first,count,lengths,1-mp[None],x,xl,*w,prev)
    xa,p2,sel=join(xt,p2,sel)
    w_own=(text_qkv,wl,bt,bl)
    own=forward(0,pages-1,xa,w_own,())
    own,a1,p2=join(own,a1,p2)
    b1=send(a1,even_odd); c1=send(a1,core_flip); a2=over(p2)
    own=forward(pages-1,1,xt,w_own,own)
    own,b1,c1,a2,p3,p4=join(own,b1,c1,a2,p3,p4)
    d1=send(b1,core_flip); b2=send(a2,even_odd); a3=over(p3)
    cores=[send(a2,core_flip)]
    wt_both,wl_both,bt_o,bl_o=unpack_first(scal,(a1,b1,c1,d1),text_qkv,wl)
    wt_both,wl_both,bt_o,bl_o,a2,b2,a3,p4,cores=join(wt_both,wl_both,bt_o,bl_o,a2,b2,a3,p4,cores)
    e2=send(a2,odd_even); f2=send(b2,odd_even); a4=over(p4); b3=send(a3,even_odd)
    cores+=[send(b2,core_flip)]
    w_oth=(wt_both,wl_both,bt_o,bl_o)
    oth=forward(0,pages-1,xt,w_oth,())
    oth=forward(pages-1,1,xt,w_oth,oth)
    oth,e2,f2,a4,b3,cores=join(oth,e2,f2,a4,b3,cores)
    b4=send(a4,even_odd); c4=send(a4,core_flip); c3=send(a3,core_flip)
    cores+=[send(v,core_flip) for v in (e2,f2)]
    beside=side(scal,xl,own[7],oth[7],layout_cot.T,sel,a4,[layout_shifts.astype(F32),layout_gains.astype(F32)],
        [layout_out_w,layout_up,layout_down,upbl],[a1,b1,c1,d1])
    beside,b4,c4,c3,cores=join(beside,b4,c4,c3,cores)
    lo,dr1l,dOl,extra=beside
    second=(a2,b2,e2,f2,*cores)
    d3=send(b3,core_flip); d4=send(b4,core_flip)
    to,dr1,dO,keep,out,st,bst=ffn(n,scal,[xt,own[6],oth[6],text_cot,sel],[text_shifts.astype(F32),text_gains.astype(F32),upb],
        [text_up,text_out_w,text_down],second,((a3,a4),(b3,b4),(c3,c4),(d3,d4)),extra)
    steps=stages(n)
    wts=[wt_both,wl_both]
    tile=text_in.shape[0]//3
    mine_p=lambda p,c,d: attn_bwd(p,c,lengths,mp[None],own,dO,dOl,d)
    other_p=lambda p,d: attn_bwd(p,1,lengths,1-mp[None],oth,dO,dOl,d)
    sums=lambda d: qkv_grad(n,jnp.stack([mp,dp]),pages,xt,xl,*d,sel,*wts,st,bst)
    inputs=lambda d: input_grad(tile,d,wts,dr1,dr1l,sel)
    if n==16:
        out=send(out,steps[0])
        d_own=mine_p(0,1,())
        d_own,out,keep=join(d_own,out,keep)
        keep,out=halve(keep,out)
        out=send(out,steps[1])
        d_own=mine_p(1,pages-1,d_own)
        qkeep,qout=sums(d_own)
        qkeep,qout,keep,out=join(qkeep,qout,keep,out)
        qout=send(qout,steps[0])
        keep,out=halve(keep,out)
        half=keep.shape[0]//2
        far=send(out[half:],steps[2])
        d_oth=other_p(0,d_own)
        d_oth,qkeep,qout,keep,out,far=join(d_oth,qkeep,qout,keep,out,far)
        out_far=keep[half:]+far
        cut=out_far.shape[0]*2//3
        outs=[send(out_far[:cut],steps[3]),out_far[cut:]]
        qkeep,qout=halve(qkeep,qout)
        qout=send(qout,steps[1])
        d_oth=other_p(1,d_oth)
        d_oth,qkeep,qout,keep,out,outs[0],outs[1]=join(d_oth,qkeep,qout,keep,out,*outs)
        outs[1]=send(outs[1],steps[3])
        near_small=send(out[:half,3456:],steps[2])
        qkeep,qout=halve(qkeep,qout)
        qout=send(qout,steps[2])
        d_oth=other_p(2,d_oth)
        d_oth,qkeep,qout,keep,out,near_small,*outs=join(d_oth,qkeep,qout,keep,out,near_small,*outs)
        qkeep,qout_sent=halve(qkeep,qout)
        qout=send(qout_sent,steps[3])
        got_far=jnp.concatenate(outs,0)
        early=(keep[:half,3456:]+near_small)+got_far[:,3456:]
        early_got=send(early,steps[3])
        peer=over(jnp.concatenate([qkeep[:,1152:1280],qout_sent[:,1152:1280]],0))
        near=send(out[:half,:3456],steps[2])
        pair=lambda bit,x,y: (lambda low: jnp.stack([jnp.where(low,x,y),jnp.where(low,y,x)]))((dp&bit)==0)
        d_in=inputs(d_oth)
        d_in,qkeep,qout,peer,early_got,near=join(d_in,qkeep,qout,peer,early_got,near)
        g=(keep[:half,:3456]+near)+got_far[:,:3456]
        qg=qkeep+qout
        small=qg[:,1152:]
        got=send(small,steps[3]); peer_got=send(peer,steps[3])
        early=pair(8,early,early_got)
        early=pair(2,early,send(early,flip(n,2)))
        r=qg.shape[0]
        small=jnp.concatenate([pair(8,small,got),pair(8,peer[:r]+peer_got[r:],peer_got[:r]+peer[r:])],2)
        early=pair(4,early,send(early,flip(n,4))).reshape(8,-1,256)
        small=pair(2,small,send(small,flip(n,2)))
        early=(early,send(early,core_flip))
        small=pair(4,small,send(small,flip(n,4))).reshape(8,-1,256)
        small=(small,send(small,core_flip))
        order=[(i>>2&1)*4+(i>>1&1)*2+(i>>3) for i in range(16)]
    else:
        d_own=mine_p(0,pages,())
        qkeep,qout=sums(d_own)
        rs=lambda v: lax.psum_scatter(v,"dp",scatter_dimension=0,tiled=True)
        g=rs(keep); qg=rs(qkeep)
        d_oth=d_own
        for p in range(pages): d_oth=other_p(p,d_oth)
        d_in=inputs(d_oth)
        whole=lambda v: (lambda w: (w[None],w[None,:8]))(lax.all_gather(v,"dp",tiled=True))
        small=whole(jnp.concatenate([qg[:,1152:],over(qg[:,1152:])],1)); early=whole(g[:,3456:])
        order=[]
    tg,lg=d_in
    r=g.shape[0]
    tvec,lvec,cs,shifts,gains,bst,qgl,csl,outl,shl,gal,upl,bstl,downl=finish(order,core[None],*small,*early)
    qg=jnp.moveaxis(qg[:,:1152].reshape(r,3,384),1,0)
    return (to,lo.T,tg,lg.T,tvec,lvec,qg,cs,g[:,3072:3456].T,shifts,gains,g[:,:1536],bst,g[:,1536:3072].T,
            qgl,csl,outl,shl,gal,upl,bstl,downl.T)


def solution(mesh):
    rows=P("dp",None); cols=P(None,"mp"); lead=P("mp",None); cube=P(None,None,"mp")
    weights=(cube,cols,lead,P(),P(),cols,P("mp"),lead)
    return jax.shard_map(shards,mesh=mesh,
        in_specs=(rows,rows,P("dp"),P("dp"),P("dp"),P(),P())+weights+weights+(rows,rows),
        out_specs=(rows,rows,rows,rows,P(),P(),P(None,"dp","mp"),cols,P("mp","dp"),P(),P(),P("dp","mp"),P("mp"),P("mp","dp"),
                   cube,cols,lead,P(),P(),cols,P("mp"),lead),
        check_vma=False)
```
